32 devices in a mesh: rep: 4 (over y, x), exp: 8 (over z, core).
Axes of the slice: x: 2, y: 2, z: 4, core: 2. Of those that a mesh axis runs over, the one named last changes fastest.
Arguments:
- tokens: bfloat16 [1024, 2048], P('exp', 'rep'), may hold values from -6 to 6
- expert_ids: int32 [1024, 8], P('exp'), may hold values from 0 to 127, all different within a row; in each aligned block of 128 rows (0 to 127, 128 to 255, ...) at most 12 rows name the same one
- route_weights: float32 [1024, 8], P('exp'), may hold values from 0.05 to 1
- w_gate: bfloat16 [128, 768, 2048], P('exp', None, 'rep'), may hold values from -0.125 to 0.125
- w_up: bfloat16 [128, 768, 2048], P('exp', None, 'rep'), may hold values from -0.125 to 0.125
- w_down: bfloat16 [128, 768, 2048], P('exp', None, 'rep'), may hold values from -0.21875 to 0.21875
Outputs:
- mixed: bfloat16 [1024, 2048], P('exp', 'rep')
The draws below stay inside these ranges and needn't reach their ends.
Inputs may be any that keep to these rules, and one draw needn't show every extreme that they name: `expert_ids`: each token names 8 different experts. Within the rows of one index of exp (aligned blocks of 128 tokens) no expert is named more than 12 times, a bound that some block reaches.
All inputs are finite; a program needn't handle non-finite values.
Results may differ from the reference program's by a relative error of at most 0.0058.
Values may be sent and summed in bfloat16 or wider, within the bound.
No kernel may reach another device: no remote copies, remote signals or barrier semaphores. Data moves between devices by JAX's collectives and lax.ppermute only.
A program may use at most 256 MiB of HBM per device.

```python
import math
import jax
import jax.numpy as jnp
import numpy as np
from jax import lax

D = 2048
FF = 768
EXPERTS = 128
TOP = 8
TOK_DEV = 128
CAP = 12
TOKENS = 1024


def block_scale(own_key, extent, shards, least, largest):
    factor_of, own = 1.0, jax.random.fold_in(own_key, 6)
    for axis_at, blocks in shards:
        draws = jnp.exp(jax.random.uniform(jax.random.fold_in(own, axis_at), (blocks,), jnp.float32, least / len(shards), largest / len(shards)))
        factor_of = factor_of * jnp.repeat(draws, extent[axis_at] // blocks).reshape([-1 if axis == axis_at else 1 for axis in range(len(extent))])
    return factor_of


def routed_block(rng, own, number, rows, count, top, most, slope):
    sequence = jax.random.permutation(rng, count)
    packed, common = shares(count, rows * top, most, slope, True), shares(count, rows * top, most, slope, False)
    places = jnp.arange(count)

    def named(lengths, offset_by):
        used = int((lengths > 0).sum())
        fixed = max(1, used // 4)
        shifted = fixed + (places - fixed + offset_by * (used - fixed)) % max(1, count - fixed)
        return jnp.zeros((count,), jnp.int32).at[sequence[jnp.where(places < fixed, places, shifted)]].set(jnp.asarray(lengths, jnp.int32))

    lengths = jnp.where(number % 4 == 0, named(packed, number // 4), named(common, number - number // 4 - 1))
    mixed = jax.random.permutation(jax.random.fold_in(own, 3), count)
    donor, taker = mixed[0:count // 2 * 2:2], mixed[1:count // 2 * 2:2]
    slack = jnp.minimum(lengths[donor] - 1, most - lengths[taker]) // 2
    slack = jnp.where((donor == sequence[0]) | (taker == sequence[0]) | (lengths[taker] == 0), 0, jnp.maximum(slack, 0))
    shifted = jax.random.randint(jax.random.fold_in(own, 4), (count // 2,), 0, 1 << 20) % (slack + 1)
    lengths = lengths.at[donor].add(-shifted).at[taker].add(shifted)
    members = jnp.searchsorted(jnp.cumsum(lengths), jnp.arange(rows * top), side="right").astype(jnp.int32)
    table = members.reshape(top, rows).T
    table = table[jax.random.permutation(jax.random.fold_in(own, 1), rows)]
    offset_by = jax.random.randint(jax.random.fold_in(own, 2), (rows, 1), 0, top)
    return jnp.take_along_axis(table, (jnp.arange(top)[None, :] + offset_by) % top, axis=1)


def shares(number_of, total, bound, lean, full):
    weights = [(1 << 20) // math.isqrt(grade ** lean) + 1 for grade in range(1, number_of + 1)]
    largest = bound if full else min(bound, max(-(-total // number_of), total * weights[0] // sum(weights)))
    least = 1 if total - largest >= number_of - 1 else 0
    given, rest = [largest] + [least] * (number_of - 1), total - largest - least * (number_of - 1)
    while rest > 0:
        movable = [i for i in range(1, number_of) if given[i] < largest] or [i for i in range(1, number_of) if given[i] < bound]
        mass, budget = sum([weights[i] for i in movable]), rest
        for i in movable:
            addition = min(bound - given[i], max(1, budget * weights[i] // mass), rest)
            given[i] = given[i] + addition
            rest = rest - addition
    return np.array(given)


def gaussian(key, extent, scale, most, shards=(), kind=jnp.bfloat16):
    entries = scale * jax.random.normal(key, extent, jnp.float32)
    if shards:
        entries = entries * block_scale(key, extent, shards, -0.22, 0.18)
    return jnp.clip(entries, -most, most).astype(kind)


def setup_inputs(seed: int = 0) -> dict:
    seeds = jax.random.split(jax.random.key(seed), 7)
    tokens = gaussian(seeds[0], (TOKENS, D), 1.0, 6.0, ((0, 8), (1, 4)))
    expert_ids_keys = jax.random.split(jax.random.fold_in(seeds[1], 1), TOKENS // TOK_DEV)
    expert_ids_turns = jax.random.permutation(jax.random.fold_in(seeds[1], 3), TOKENS // TOK_DEV)
    expert_ids = jax.vmap(lambda own, number: routed_block(jax.random.fold_in(seeds[1], 2), own, number, TOK_DEV, EXPERTS, TOP, CAP, 2))(expert_ids_keys, expert_ids_turns).reshape((TOKENS, TOP))
    route_weights = jnp.clip(jnp.exp(math.log(1.0) - 2.9957323 * jax.random.uniform(seeds[2], (TOKENS, TOP), jnp.float32) ** block_scale(seeds[2], (TOKENS, TOP), ((0, 8),), -0.2, 0.2)), 0.05, 1.0)
    w_gate = gaussian(seeds[3], (EXPERTS, FF, D), D ** -0.5, 0.125, ((0, 8), (2, 4)))
    w_up = gaussian(seeds[4], (EXPERTS, FF, D), D ** -0.5, 0.125, ((0, 8), (2, 4)))
    w_down = gaussian(seeds[5], (EXPERTS, FF, D), FF ** -0.5, 0.21875, ((0, 8), (2, 4)))
    return {"tokens": tokens, "expert_ids": expert_ids, "route_weights": route_weights, "w_gate": w_gate, "w_up": w_up, "w_down": w_down}


def block_slots(block_ids):
    onehot = (block_ids[:, None] == jnp.arange(EXPERTS, dtype=jnp.int32)[None, :]).astype(jnp.int32)
    before = jnp.cumsum(onehot, axis=0) - onehot
    return jnp.sum(before * onehot, axis=1).astype(jnp.int32)


def reference(tokens, expert_ids, route_weights, w_gate, w_up, w_down):
    tok_total = expert_ids.shape[0]
    top_count = expert_ids.shape[1]
    blocks = tok_total // TOK_DEV
    per_block = expert_ids.reshape(blocks, TOK_DEV * top_count)
    slot_ids = lax.map(block_slots, per_block).reshape(-1)
    assigned = expert_ids.reshape(-1)
    block_index = (jnp.arange(tok_total * top_count) // (TOK_DEV * top_count)).astype(jnp.int32)
    position = (block_index * CAP + slot_ids).astype(jnp.int32)
    token_source = (jnp.arange(tok_total * top_count) // top_count).astype(jnp.int32)
    probs = route_weights / jnp.sum(route_weights, axis=1, keepdims=True)
    norm_weight = probs.reshape(-1)
    rows_expert = blocks * CAP
    token_table = jnp.zeros((EXPERTS, rows_expert), jnp.int32).at[assigned, position].set(token_source)
    weight_table = jnp.zeros((EXPERTS, rows_expert), jnp.float32).at[assigned, position].set(norm_weight)

    def add_expert(accumulated, expert_index):
        row_tokens = token_table[expert_index]
        row_scale = weight_table[expert_index]
        chosen = tokens[row_tokens]
        gate_part = jnp.dot(chosen, w_gate[expert_index].T, preferred_element_type=jnp.float32)
        up_part = jnp.dot(chosen, w_up[expert_index].T, preferred_element_type=jnp.float32)
        hidden = (jax.nn.silu(gate_part) * up_part).astype(jnp.bfloat16)
        expert_out = jnp.dot(hidden, w_down[expert_index], preferred_element_type=jnp.float32).astype(jnp.bfloat16)
        expert_out = lax.optimization_barrier(expert_out).astype(jnp.float32)
        return accumulated.at[row_tokens].add(expert_out * row_scale[:, None]), None

    start_sum = jnp.zeros((tok_total, tokens.shape[1]), jnp.float32)
    accumulated, _ = lax.scan(add_expert, start_sum, jnp.arange(EXPERTS, dtype=jnp.int32))
    return accumulated.astype(jnp.bfloat16)
```

```python
import functools

import jax
import jax.numpy as jnp
from jax import lax
from jax.experimental import pallas as pl
from jax.experimental.pallas import tpu as pltpu
from jax.sharding import PartitionSpec as P

EXPERTS = 128
F32 = jnp.float32
BF16 = jnp.bfloat16
VMEM_LIMIT = 56 * 2**20
ALIGN = 16
META = 16


def ceil_to(value, unit):
    return -(-value // unit) * unit


def vmem():
    return pl.BlockSpec(memory_space=pltpu.VMEM)


def smem():
    return pl.BlockSpec(memory_space=pltpu.SMEM)


def hbm():
    return pl.BlockSpec(memory_space=pl.ANY)


def params():
    return pltpu.CompilerParams(vmem_limit_bytes=VMEM_LIMIT)


def cost(flops, moved):
    return pl.CostEstimate(flops=int(flops), bytes_accessed=int(moved), transcendentals=0)


def route(dims, base, gathered, rowid, probs, rowk, offs):
    blocks, rows, top, experts = dims["blocks"], dims["rows"], dims["top"], dims["experts"]
    expert_at = lax.broadcasted_iota(jnp.int32, (experts, rows), 0) + base
    upper = (
        lax.broadcasted_iota(jnp.int32, (rows, rows), 0)
        <= lax.broadcasted_iota(jnp.int32, (rows, rows), 1)
    ).astype(BF16)

    def count(block, seen):
        meta = gathered[block, rows : rows + META, :].astype(F32)
        ids = meta[:top, :rows].astype(jnp.int32)
        chance = meta[:top, rows : 2 * rows] + meta[:top, 2 * rows : 3 * rows]
        chance = chance + meta[:top, 3 * rows : 4 * rows]
        member = jnp.zeros((experts, rows), F32)
        share = jnp.zeros((experts, rows), F32)
        for k in range(top):
            hit = ids[k : k + 1, :] == expert_at
            member = member + hit.astype(F32)
            share = share + jnp.where(hit, chance[k : k + 1, :], 0.0)
        upto = jnp.dot(member.astype(BF16), upper, preferred_element_type=F32)
        rowid[block] = jnp.where(member > 0, seen + upto - 1.0, -1e6)
        probs[block] = share
        return seen + upto[:, rows - 1 : rows]

    total = lax.fori_loop(0, blocks, count, jnp.zeros((experts, rows), F32))
    starts, before = [], jnp.zeros((1, rows), F32)
    for e in range(experts):
        starts.append(before)
        before = before + total[e : e + 1, :]
    start = jnp.concatenate(starts, axis=0) if experts > 1 else starts[0]

    def place(block, carry):
        ids = gathered[block, rows : rows + META, :][:top, :rows].astype(F32).astype(jnp.int32)
        at = rowid[block] + start
        rowid[block] = at
        chosen = []
        for k in range(top):
            hit = ids[k : k + 1, :] == expert_at
            chosen.append(jnp.max(jnp.where(hit, at, -1e6), axis=0, keepdims=True))
        rowk[block] = jnp.concatenate(chosen, axis=0)
        return carry

    lax.fori_loop(0, blocks, place, 0)
    offs[0] = start.astype(jnp.int32)
    offs[1] = total.astype(jnp.int32)
    return start


def window_hits(dims, rowid, block, e, start):
    at = lax.broadcasted_iota(jnp.int32, (dims["window"], dims["rows"]), 0) + start
    return rowid[block, e : e + 1, :].astype(jnp.int32) == at


def dispatch_kernel(dims, base_ref, gathered, x, rowid, probs, rowk, offs, select, total):
    blocks, rows, experts, window = dims["blocks"], dims["rows"], dims["experts"], dims["window"]
    group = dims["group"]
    start = route(dims, base_ref[0], gathered, rowid, probs, rowk, offs).astype(jnp.int32)
    starts = [start[e, 0] for e in range(experts)]

    def body(step, carry):
        select[...] = jnp.zeros_like(select)
        for e in range(experts):
            first = pl.multiple_of(starts[e] // ALIGN * ALIGN, ALIGN)
            at = pl.ds(first, window)
            for inner in range(group):
                cols = slice(inner * rows, (inner + 1) * rows)
                hit = window_hits(dims, rowid, step * group + inner, e, first)
                select[at, cols] = select[at, cols] + hit.astype(F32).astype(BF16)
        width = x.shape[1]
        part = gathered[pl.ds(step * group, group), :rows, :].reshape(group * rows, width)
        tile = dims["tile"]
        for r in range(0, x.shape[0], tile):
            size = min(tile, x.shape[0] - r)
            got = jnp.dot(select[r : r + size, :], part, preferred_element_type=F32)
            if blocks > group:
                got = got + jnp.where(step == 0, 0.0, total[r : r + size, :])
                total[r : r + size, :] = got
            x[r : r + size, :] = got.astype(BF16)
        return carry

    if blocks > group:
        total[...] = jnp.zeros_like(total)
        lax.fori_loop(0, blocks // group, body, 0)
    else:
        body(0, 0)


def dispatch(dims, base, gathered):
    blocks, rows, top, experts = dims["blocks"], dims["rows"], dims["top"], dims["experts"]
    width, padded = gathered.shape[2], dims["padded"]
    acc_rows = padded if blocks > dims["group"] else 8
    return pl.pallas_call(
        functools.partial(dispatch_kernel, dims),
        out_shape=(
            jax.ShapeDtypeStruct((padded, width), BF16),
            jax.ShapeDtypeStruct((blocks, experts, rows), F32),
            jax.ShapeDtypeStruct((blocks, experts, rows), F32),
            jax.ShapeDtypeStruct((blocks, top, rows), F32),
            jax.ShapeDtypeStruct((2, experts, rows), jnp.int32),
        ),
        in_specs=[smem(), vmem()],
        out_specs=(vmem(),) * 5,
        scratch_shapes=[
            pltpu.VMEM((padded, dims["group"] * rows), BF16),
            pltpu.VMEM((acc_rows, width), F32),
        ],
        compiler_params=params(),
        cost_estimate=cost(2 * padded * blocks * rows * width, 2 * blocks * rows * width * 2),
        name="dispatch",
    )(base, gathered)


def row_mask(dims, first, offs, e):
    at = lax.broadcasted_iota(jnp.int32, (dims["window"], 1), 0) + first
    begin = offs[0, e]
    return (at >= begin) & (at < begin + offs[1, e])


def gate_up_kernel(dims, c, me_ref, offs, x, w_gate, w_up, gx, uy, g2, u1, g0, u0, gate_w, up_w, gate, up, sems):
    experts, window, part, quarter = dims["experts"], dims["window"], dims["part"], dims["quarter"]
    units = pl.ds(c * part, part)

    def copies(e):
        return (
            pltpu.make_async_copy(w_gate.at[e, units, :], gate_w.at[e], sems.at[0, e]),
            pltpu.make_async_copy(w_up.at[e, units, :], up_w.at[e], sems.at[1, e]),
        )

    for e in range(experts):
        for copy in copies(e):
            copy.start()
    gate[...] = jnp.zeros_like(gate)
    up[...] = jnp.zeros_like(up)
    contract = (((1,), (1,)), ((), ()))
    for e in range(experts):
        first = pl.multiple_of(offs[0, e] // ALIGN * ALIGN, ALIGN)
        at = pl.ds(first, window)
        rows = x[at, :]
        mask = row_mask(dims, first, offs, e)
        for copy, held, into in zip(copies(e), (gate_w, up_w), (gate, up)):
            copy.wait()
            got = lax.dot_general(rows, held[e], contract, preferred_element_type=F32)
            into[at, :] = jnp.where(mask, got, into[at, :])
    me = me_ref[0]

    def piece(total, j):
        return total[pl.ds(pl.multiple_of((me ^ j) * quarter, ALIGN), quarter), :]

    gx[0] = piece(gate, 1).astype(BF16)
    gx[1] = piece(gate, 3).astype(BF16)
    uy[0] = piece(up, 2).astype(BF16)
    uy[1] = piece(up, 3).astype(BF16)
    g2[...] = piece(gate, 2)
    u1[...] = piece(up, 1)
    g0[...] = piece(gate, 0)
    u0[...] = piece(up, 0)


def gate_up(dims, c, me, offs, x, w_gate, w_up):
    experts, part, quarter, padded = dims["experts"], dims["part"], dims["quarter"], dims["padded"]
    width = x.shape[1]
    half = jax.ShapeDtypeStruct((2, quarter, part), BF16)
    own = jax.ShapeDtypeStruct((quarter, part), F32)
    return pl.pallas_call(
        functools.partial(gate_up_kernel, dims, c),
        out_shape=(half, half, own, own, own, own),
        in_specs=[smem(), smem(), vmem(), hbm(), hbm()],
        out_specs=(vmem(),) * 6,
        scratch_shapes=[
            pltpu.VMEM((experts, part, width), BF16),
            pltpu.VMEM((experts, part, width), BF16),
            pltpu.VMEM((padded, part), F32),
            pltpu.VMEM((padded, part), F32),
            pltpu.SemaphoreType.DMA((2, experts)),
        ],
        compiler_params=params(),
        cost_estimate=cost(4 * padded * width * part, 4 * experts * part * width + 2 * padded * width),
        name="gate_up",
    )(me, offs, x, w_gate, w_up)


def gather_hidden(dims, me, pieces, hidden):
    quarter, half = dims["quarter"], dims["part"] // 2
    for c, chunk in enumerate(pieces):
        for j, halves in enumerate(chunk):
            at = pl.ds(pl.multiple_of((me ^ j) * quarter, ALIGN), quarter)
            for side, held in enumerate(halves):
                col = c * dims["part"] + side * half
                hidden[at, col : col + half] = held[...]


def unpack(refs, chunks):
    pieces = [[refs[c * 8 + j * 2 : c * 8 + j * 2 + 2] for j in range(4)] for c in range(chunks)]
    return pieces, refs[chunks * 8 :]


def choose(dims, rowk, block):
    at = lax.broadcasted_iota(jnp.int32, (dims["rows"], dims["total"]), 1)
    rows_of = rowk[block].T.astype(jnp.int32)
    hit = rows_of[:, 0:1] == at
    for k in range(1, dims["top"]):
        hit = hit | (rows_of[:, k : k + 1] == at)
    return hit.astype(F32).astype(BF16)


def down_first_kernel(dims, chunks, me_ref, offs, rowid, probs, rowk, w_down, *refs):
    experts, window = dims["experts"], dims["window"]
    pieces, (y, scale, chosen, held, hidden, sems) = unpack(refs, chunks)
    units = pl.ds(0, chunks * dims["part"])

    def copy(e):
        return pltpu.make_async_copy(w_down.at[e, units, :], held.at[e], sems.at[e])

    for e in range(experts):
        copy(e).start()
    hidden[...] = jnp.zeros_like(hidden)
    gather_hidden(dims, me_ref[0], pieces, hidden)
    y[...] = jnp.zeros_like(y)
    scale[...] = jnp.zeros_like(scale)
    if dims["early"]:
        def early(block, carry):
            chosen[block] = choose(dims, rowk, block)
            return carry

        lax.fori_loop(0, dims["blocks"], early, 0)
    else:
        chosen[...] = jnp.zeros_like(chosen)
    for e in range(experts):
        first = pl.multiple_of(offs[0, e] // ALIGN * ALIGN, ALIGN)
        at = pl.ds(first, window)
        mask = row_mask(dims, first, offs, e)

        def share(block, carry):
            hit = window_hits(dims, rowid, block, e, first)
            return carry + jnp.where(hit, probs[block, e : e + 1, :], 0.0)

        shares = lax.fori_loop(
            0, dims["blocks"], share, jnp.zeros((window, dims["rows"]), F32)
        )
        wide = jnp.broadcast_to(jnp.sum(shares, axis=1, keepdims=True), (window, scale.shape[1]))
        scale[at, :] = jnp.where(mask, wide, scale[at, :])
        copy(e).wait()
        got = jnp.dot(hidden[at, :], held[e], preferred_element_type=F32)
        y[at, :] = jnp.where(mask, got, y[at, :])


def down_last_kernel(dims, c, me_ref, offs, y, scale, chosen, rowk, w_down, *refs):
    experts, window, part = dims["experts"], dims["window"], dims["part"]
    pieces, (out, held, hidden, scaled, sems) = unpack(refs, 1)
    units = pl.ds(c * part, part)

    def copy(e):
        return pltpu.make_async_copy(w_down.at[e, units, :], held.at[e], sems.at[e])

    for e in range(experts):
        copy(e).start()
    hidden[...] = jnp.zeros_like(hidden)
    scaled[...] = jnp.zeros_like(scaled)
    gather_hidden(dims, me_ref[0], pieces, hidden)
    width = y.shape[1]
    for e in range(experts):
        first = pl.multiple_of(offs[0, e] // ALIGN * ALIGN, ALIGN)
        at = pl.ds(first, window)
        mask = row_mask(dims, first, offs, e)
        copy(e).wait()
        got = jnp.dot(hidden[at, :], held[e], preferred_element_type=F32) + y[at, :]
        got = got * scale[at, 0:1]
        scaled[at, :] = jnp.where(mask, got, scaled[at, :].astype(F32)).astype(BF16)
    rows, group, total = dims["rows"], dims["group"], dims["total"]

    def combine(step, carry):
        many = min(4, group)
        for inner in range(0, group, many):
            if dims["early"]:
                picked = chosen[pl.ds(step * group + inner, many)].reshape(many * rows, total)
            else:
                picked = jnp.concatenate(
                    [choose(dims, rowk, step * group + inner + i) for i in range(many)], axis=0
                )
            summed = jnp.dot(picked, scaled[:total, :], preferred_element_type=F32)
            out[pl.ds(step * group + inner, many)] = summed.astype(BF16).reshape(many, rows, width)
        return carry

    if dims["blocks"] > group:
        lax.fori_loop(0, dims["blocks"] // group, combine, 0)
    else:
        combine(0, 0)


def flat(pieces):
    return [held for chunk in pieces for halves in chunk for held in halves]


def down_first(dims, me, offs, rowid, probs, rowk, w_down, pieces):
    experts, padded, part = dims["experts"], dims["padded"], dims["part"]
    chunks, width = len(pieces), w_down.shape[2]
    picked = (dims["blocks"], dims["rows"], dims["total"]) if dims["early"] else (1, ALIGN, 128)
    return pl.pallas_call(
        functools.partial(down_first_kernel, dims, chunks),
        out_shape=(
            jax.ShapeDtypeStruct((padded, width), F32),
            jax.ShapeDtypeStruct((padded, 128), F32),
            jax.ShapeDtypeStruct(picked, BF16),
        ),
        in_specs=[smem(), smem(), vmem(), vmem(), vmem(), hbm()] + [vmem()] * (8 * chunks),
        out_specs=(vmem(),) * 3,
        scratch_shapes=[
            pltpu.VMEM((experts, chunks * part, width), BF16),
            pltpu.VMEM((padded, chunks * part), BF16),
            pltpu.SemaphoreType.DMA((experts,)),
        ],
        compiler_params=params(),
        cost_estimate=cost(
            2 * padded * width * part * chunks, 2 * experts * part * chunks * width + 8 * padded * width
        ),
        name="down_first",
    )(me, offs, rowid, probs, rowk, w_down, *flat(pieces))


def down_last(dims, c, me, offs, y, scale, chosen, rowk, w_down, pieces):
    experts, padded, part = dims["experts"], dims["padded"], dims["part"]
    width = w_down.shape[2]
    return pl.pallas_call(
        functools.partial(down_last_kernel, dims, c),
        out_shape=jax.ShapeDtypeStruct((dims["blocks"], dims["rows"], width), BF16),
        in_specs=[smem(), smem()] + [vmem()] * 4 + [hbm()] + [vmem()] * 8,
        out_specs=vmem(),
        scratch_shapes=[
            pltpu.VMEM((experts, part, width), BF16),
            pltpu.VMEM((padded, part), BF16),
            pltpu.VMEM((padded, width), BF16),
            pltpu.SemaphoreType.DMA((experts,)),
        ],
        compiler_params=params(),
        cost_estimate=cost(4 * padded * width * part, 2 * experts * part * width + 8 * padded * width),
        name="down_last",
    )(me, offs, y, scale, chosen, rowk, w_down, *flat([pieces]))


def swap(value, bit):
    count = lax.axis_size("rep")
    return lax.ppermute(value, "rep", [(i, i ^ bit) for i in range(count)])


def reduce_chunk(parts):
    gx, uy, g2, u1, g0, u0 = parts
    from_x = swap(gx, 1)
    from_y = swap(uy, 2)
    gate_rest = swap((g2 + from_x[1].astype(F32)).astype(BF16), 2)
    up_rest = swap((u1 + from_y[1].astype(F32)).astype(BF16), 1)
    gate = g0 + from_x[0].astype(F32) + gate_rest.astype(F32)
    up = u0 + from_y[0].astype(F32) + up_rest.astype(F32)
    hidden = (jax.nn.silu(gate) * up).astype(BF16)
    half = hidden.shape[1] // 2
    return hidden[:, :half], hidden[:, half:]


def spread_chunk(left, right):
    x = (swap(left, 1), swap(right, 1))
    y = (swap(left, 2), swap(right, 2))
    corner = (swap(x[0], 2), swap(y[1], 1))
    return [(left, right), x, y, corner]


def local(tokens, expert_ids, route_weights, w_gate, w_up, w_down):
    rows, top = expert_ids.shape
    width = tokens.shape[1]
    experts, units, _ = w_gate.shape
    blocks = lax.axis_size("exp")
    replicas = lax.axis_size("rep")
    cap = replicas * max(1, rows * top * 3 // (8 * EXPERTS))
    total = ceil_to(experts * blocks * cap, replicas * 128)
    window = ceil_to(blocks * cap, ALIGN) + ALIGN
    part = 256
    dims = dict(
        blocks=blocks,
        rows=rows,
        top=top,
        experts=experts,
        window=window,
        total=total,
        quarter=total // replicas,
        padded=total + window,
        part=part,
        group=min(blocks, 8),
        tile=512,
        early=blocks * rows * total <= 4 * 2**20,
    )
    me = lax.axis_index("rep").astype(jnp.int32).reshape(1)
    base = (lax.axis_index("exp") * experts).astype(jnp.int32).reshape(1)

    chance = (route_weights / jnp.sum(route_weights, axis=1, keepdims=True)).T
    high = lax.reduce_precision(chance, 8, 7)
    middle = lax.reduce_precision(chance - high, 8, 7)
    low = chance - high - middle
    chance = jnp.concatenate([high, middle, low], axis=1).astype(BF16)
    meta = jnp.concatenate([expert_ids.T.astype(BF16), chance], axis=1)
    meta = jnp.pad(meta, ((0, META - top), (0, width - meta.shape[1])))
    packed = jnp.concatenate([tokens, meta], axis=0)
    gathered = lax.all_gather(packed, "exp", axis=0)

    x, rowid, probs, rowk, offs_wide = dispatch(dims, base, gathered)
    offs = offs_wide[:, :, 0]

    pieces = []
    for c in range(units // part):
        left, right = reduce_chunk(gate_up(dims, c, me, offs, x, w_gate, w_up))
        pieces.append(spread_chunk(left, right))
    y, scale, chosen = down_first(dims, me, offs, rowid, probs, rowk, w_down, pieces[:-1])
    last = len(pieces) - 1
    mixed = down_last(dims, last, me, offs, y, scale, chosen, rowk, w_down, pieces[-1])
    return lax.psum_scatter(mixed, "exp", scatter_dimension=0, tiled=False)


def solution(mesh):
    return jax.shard_map(
        local,
        mesh=mesh,
        in_specs=(
            P("exp", "rep"),
            P("exp", None),
            P("exp", None),
            P("exp", None, "rep"),
            P("exp", None, "rep"),
            P("exp", None, "rep"),
        ),
        out_specs=P("exp", "rep"),
        check_vma=False,
    )
```

```python
import functools

import jax
import jax.numpy as jnp
from jax import lax
from jax.experimental import pallas as pl
from jax.experimental.pallas import tpu as pltpu
from jax.sharding import PartitionSpec as P

EXPERTS = 128
F32 = jnp.float32
BF16 = jnp.bfloat16
VMEM_LIMIT = 56 * 2**20
ALIGN = 16
META = 16


def ceil_to(value, unit):
    return -(-value // unit) * unit


def vmem():
    return pl.BlockSpec(memory_space=pltpu.VMEM)


def smem():
    return pl.BlockSpec(memory_space=pltpu.SMEM)


def hbm():
    return pl.BlockSpec(memory_space=pl.ANY)


def params():
    return pltpu.CompilerParams(vmem_limit_bytes=VMEM_LIMIT)


def cost(flops, moved):
    return pl.CostEstimate(flops=int(flops), bytes_accessed=int(moved), transcendentals=0)


def prepare_kernel(dims, ids, weights, meta):
    rows, top = dims["rows"], dims["top"]
    chance = weights[...]
    chance = (chance / jnp.sum(chance, axis=1, keepdims=True)).T
    high = chance.astype(BF16)
    rest = chance - high.astype(F32)
    middle = rest.astype(BF16)
    low = (rest - middle.astype(F32)).astype(BF16)
    meta[...] = jnp.zeros_like(meta)
    parts = (ids[...].astype(F32).T, high.astype(F32), middle.astype(F32), low.astype(F32))
    for i, part in enumerate(parts):
        block = jnp.concatenate([part, jnp.zeros((META - top, rows), F32)], axis=0)
        meta[:, i * rows : (i + 1) * rows] = block.astype(BF16)


def prepare(dims, ids, weights):
    return pl.pallas_call(
        functools.partial(prepare_kernel, dims),
        out_shape=jax.ShapeDtypeStruct((META, 4 * dims["rows"]), BF16),
        in_specs=[vmem(), vmem()],
        out_specs=vmem(),
        compiler_params=params(),
        name="prepare",
    )(ids, weights)


def loop(count, body, carry):
    if count > 8:
        return lax.fori_loop(0, count, body, carry)
    for i in range(count):
        carry = body(i, carry)
    return carry


def route(dims, base, meta, rowid, probs, rowk):
    blocks, rows, top, experts = dims["blocks"], dims["rows"], dims["top"], dims["experts"]
    expert_at = lax.broadcasted_iota(jnp.int32, (experts, rows), 0) + base
    upper = (
        lax.broadcasted_iota(jnp.int32, (rows, rows), 0)
        <= lax.broadcasted_iota(jnp.int32, (rows, rows), 1)
    ).astype(BF16)

    def chosen_ids(block):
        return meta[block, :, :rows].astype(F32)[:top].astype(jnp.int32)

    def count(block, seen):
        held = meta[block].astype(F32)[:top]
        ids = held[:, :rows].astype(jnp.int32)
        chance = held[:, rows : 2 * rows] + held[:, 2 * rows : 3 * rows]
        chance = chance + held[:, 3 * rows : 4 * rows]
        member = jnp.zeros((experts, rows), F32)
        share = jnp.zeros((experts, rows), F32)
        for k in range(top):
            hit = ids[k : k + 1, :] == expert_at
            member = member + hit.astype(F32)
            share = share + jnp.where(hit, chance[k : k + 1, :], 0.0)
        upto = jnp.dot(member.astype(BF16), upper, preferred_element_type=F32)
        rowid[block] = jnp.where(member > 0, seen + upto - 1.0, -1e6).astype(jnp.int32)
        probs[block] = share
        return seen + upto[:, rows - 1 : rows]

    total = loop(blocks, count, jnp.zeros((experts, rows), F32))
    starts, before = [], jnp.zeros((1, rows), F32)
    for e in range(experts):
        starts.append(before)
        before = before + total[e : e + 1, :]
    start = jnp.concatenate(starts, axis=0) if experts > 1 else starts[0]
    start, total = start.astype(jnp.int32), total.astype(jnp.int32)

    def place(block, carry):
        ids = chosen_ids(block)
        at = rowid[block] + start
        rowid[block] = at
        found = []
        for k in range(top):
            hit = ids[k : k + 1, :] == expert_at
            found.append(jnp.max(jnp.where(hit, at, -1), axis=0, keepdims=True))
        rowk[block] = jnp.concatenate(found, axis=0)
        return carry

    loop(blocks, place, 0)
    return start, total


def window_hits(dims, rowid, block, e, start):
    at = lax.broadcasted_iota(jnp.int32, (dims["window"], dims["rows"]), 0) + start
    return rowid[block, e : e + 1, :] == at


def aligned(value):
    return pl.multiple_of(value // ALIGN * ALIGN, ALIGN)


def fill_select(dims, rowid, starts, select, step):
    rows = dims["rows"]
    select[...] = jnp.zeros_like(select)
    for e in range(dims["experts"]):
        first = aligned(starts[e])
        at = pl.ds(first, dims["window"])
        for inner in range(dims["group"]):
            cols = slice(inner * rows, (inner + 1) * rows)
            hit = window_hits(dims, rowid, step * dims["group"] + inner, e, first)
            select[at, cols] = select[at, cols] + hit.astype(F32).astype(BF16)


def publish(dims, offs, start, total):
    starts = [start[e, 0] for e in range(dims["experts"])]
    for e in range(dims["experts"]):
        offs[0, e] = starts[e]
        offs[1, e] = total[e, 0]
    return starts


def route_kernel(dims, me_ref, meta, rowid, probs, rowk, select, offs):
    start, total = route(dims, me_ref[1] * dims["experts"], meta, rowid, probs, rowk)
    fill_select(dims, rowid, publish(dims, offs, start, total), select, 0)


def dispatch_kernel(dims, me_ref, meta, gathered, rowid, probs, rowk, x, offs, select, total):
    blocks, rows, group, tile = dims["blocks"], dims["rows"], dims["group"], dims["tile"]
    start, count = route(dims, me_ref[1] * dims["experts"], meta, rowid, probs, rowk)
    starts = publish(dims, offs, start, count)
    total[...] = jnp.zeros_like(total)

    def body(step, carry):
        fill_select(dims, rowid, starts, select, step)
        part = gathered[pl.ds(step * group, group)].reshape(group * rows, x.shape[1])
        for r in range(0, x.shape[0], tile):
            size = min(tile, x.shape[0] - r)
            got = jnp.dot(select[r : r + size, :], part, preferred_element_type=F32)
            got = got + total[r : r + size, :]
            total[r : r + size, :] = got
            x[r : r + size, :] = got.astype(BF16)
        return carry

    lax.fori_loop(0, blocks // group, body, 0)


def route_shapes(dims):
    blocks, rows, top, experts = dims["blocks"], dims["rows"], dims["top"], dims["experts"]
    return (
        jax.ShapeDtypeStruct((blocks, experts, rows), jnp.int32),
        jax.ShapeDtypeStruct((blocks, experts, rows), F32),
        jax.ShapeDtypeStruct((blocks, top, rows), jnp.int32),
    ), jax.ShapeDtypeStruct((2, experts), jnp.int32)


def route_rows(dims, me, meta):
    shapes, offs = route_shapes(dims)
    select = jax.ShapeDtypeStruct((dims["padded"], dims["blocks"] * dims["rows"]), BF16)
    return pl.pallas_call(
        functools.partial(route_kernel, dims),
        out_shape=shapes + (select, offs),
        in_specs=[smem(), vmem()],
        out_specs=(vmem(),) * 4 + (smem(),),
        compiler_params=params(),
        cost_estimate=cost(4e9, 4e6),
        name="route",
    )(me, meta)


def dispatch(dims, me, meta, gathered):
    shapes, offs = route_shapes(dims)
    width, padded = gathered.shape[2], dims["padded"]
    return pl.pallas_call(
        functools.partial(dispatch_kernel, dims),
        out_shape=shapes + (jax.ShapeDtypeStruct((padded, width), BF16), offs),
        in_specs=[smem(), vmem(), vmem()],
        out_specs=(vmem(),) * 4 + (smem(),),
        scratch_shapes=[
            pltpu.VMEM((padded, dims["group"] * dims["rows"]), BF16),
            pltpu.VMEM((padded, width), F32),
        ],
        compiler_params=params(),
        name="dispatch",
    )(me, meta, gathered)


def choose(dims, rowk, block):
    at = lax.broadcasted_iota(jnp.int32, (dims["rows"], dims["total"]), 1)
    rows_of = rowk[block].astype(F32).T.astype(jnp.int32)
    hit = rows_of[:, 0:1] == at
    for k in range(1, dims["top"]):
        hit = hit | (rows_of[:, k : k + 1] == at)
    return hit.astype(F32).astype(BF16)


def weigh_kernel(dims, offs, rowid, probs, rowk, scale, chosen):
    if dims["small"]:
        def pick(block, carry):
            chosen[block] = choose(dims, rowk, block)
            return carry

        lax.fori_loop(0, dims["blocks"], pick, 0)
    else:
        chosen[...] = jnp.zeros_like(chosen)
    for e in range(dims["experts"]):
        first = aligned(offs[0, e])
        at = pl.ds(first, dims["window"])

        def share(block, carry):
            hit = window_hits(dims, rowid, block, e, first)
            return carry + jnp.where(hit, probs[block, e : e + 1, :], 0.0)

        shares = loop(dims["blocks"], share, jnp.zeros((dims["window"], dims["rows"]), F32))
        wide = jnp.sum(shares, axis=1, keepdims=True)
        wide = jnp.broadcast_to(wide, (dims["window"], scale.shape[1]))
        scale[at, :] = jnp.where(row_mask(dims, first, offs, e), wide, scale[at, :])


def weigh(dims, offs, rowid, probs, rowk):
    picked = (dims["blocks"], dims["rows"], dims["total"]) if dims["small"] else (1, ALIGN, 128)
    return pl.pallas_call(
        functools.partial(weigh_kernel, dims),
        out_shape=(
            jax.ShapeDtypeStruct((dims["padded"], 128), F32),
            jax.ShapeDtypeStruct(picked, BF16),
        ),
        in_specs=[smem(), vmem(), vmem(), vmem()],
        out_specs=(vmem(), vmem()),
        compiler_params=params(),
        cost_estimate=cost(6e9, 8e6),
        name="weigh",
    )(offs, rowid, probs, rowk)


def row_mask(dims, first, offs, e):
    at = lax.broadcasted_iota(jnp.int32, (dims["window"], 1), 0) + first
    begin = offs[0, e]
    return (at >= begin) & (at < begin + offs[1, e])


def batches(experts):
    return [range(b, min(b + 4, experts)) for b in range(0, experts, 4)]


def gate_up_kernel(dims, c, first_part, me_ref, offs, *refs):
    experts, window, part, quarter = dims["experts"], dims["window"], dims["part"], dims["quarter"]
    if first_part:
        blocks, rows = dims["blocks"], dims["rows"]
        select, tokens, refs = refs[0], refs[1 : 1 + blocks], refs[1 + blocks :]
        w_gate, w_up, x, gx, uy, g2, u1, g0, u0, gate_w, up_w, gate, up, sems, table = refs
    else:
        x, w_gate, w_up, gx, uy, g2, u1, g0, u0, gate_w, up_w, gate, up, sems = refs
    units = pl.ds(c * part, part)

    def copies(e):
        return (
            pltpu.make_async_copy(w_gate.at[e, units, :], gate_w.at[e], sems.at[0, e]),
            pltpu.make_async_copy(w_up.at[e, units, :], up_w.at[e], sems.at[1, e]),
        )

    for e in range(experts):
        for copy in copies(e):
            copy.start()
    if first_part:
        for j, held in enumerate(tokens):
            table[pl.ds(pl.multiple_of((me_ref[1] ^ j) * rows, rows), rows), :] = held[...]
        for r in range(0, x.shape[0], dims["tile"]):
            size = min(dims["tile"], x.shape[0] - r)
            got = jnp.dot(select[r : r + size, :], table[...], preferred_element_type=F32)
            x[r : r + size, :] = got.astype(BF16)
    contract = (((1,), (1,)), ((), ()))
    for batch in batches(experts):
        for e in batch:
            for copy in copies(e):
                copy.wait()
        for e in batch:
            first = aligned(offs[0, e])
            rows_in = x[pl.ds(first, window), :]
            keep = (lax.broadcasted_iota(jnp.int32, (ALIGN, 1), 0) + first) >= offs[0, e]
            edge, rest = pl.ds(first, ALIGN), pl.ds(first + ALIGN, window - ALIGN)
            for held, into in ((gate_w, gate), (up_w, up)):
                got = lax.dot_general(rows_in, held[e], contract, preferred_element_type=F32)
                into[edge, :] = jnp.where(keep, got[:ALIGN], into[edge, :])
                into[rest, :] = got[ALIGN:]
    me = me_ref[0]

    def piece(total, j):
        return total[pl.ds(pl.multiple_of((me ^ j) * quarter, ALIGN), quarter), :]

    gx[0] = piece(gate, 1).astype(BF16)
    gx[1] = piece(gate, 3).astype(BF16)
    uy[0] = piece(up, 2).astype(BF16)
    uy[1] = piece(up, 3).astype(BF16)
    g2[...] = piece(gate, 2)
    u1[...] = piece(up, 1)
    g0[...] = piece(gate, 0)
    u0[...] = piece(up, 0)


def gate_up(dims, c, me, offs, rows_of, w_gate, w_up):
    experts, part, quarter, padded = dims["experts"], dims["part"], dims["quarter"], dims["padded"]
    width = w_gate.shape[2]
    half = jax.ShapeDtypeStruct((2, quarter, part), BF16)
    own = jax.ShapeDtypeStruct((quarter, part), F32)
    first_part = len(rows_of) > 1
    outs = (half, half, own, own, own, own)
    scratch = [
        pltpu.VMEM((experts, part, width), BF16),
        pltpu.VMEM((experts, part, width), BF16),
        pltpu.VMEM((padded, part), F32),
        pltpu.VMEM((padded, part), F32),
        pltpu.SemaphoreType.DMA((2, experts)),
    ]
    if first_part:
        outs = (jax.ShapeDtypeStruct((padded, width), BF16),) + outs
        scratch.append(pltpu.VMEM((dims["blocks"] * dims["rows"], width), BF16))
    return pl.pallas_call(
        functools.partial(gate_up_kernel, dims, c, first_part),
        out_shape=outs,
        in_specs=[smem(), smem()] + [vmem()] * len(rows_of) + [hbm(), hbm()],
        out_specs=(vmem(),) * len(outs),
        scratch_shapes=scratch,
        compiler_params=params(),
        cost_estimate=cost(4 * padded * width * part, 4 * experts * part * width + 2 * padded * width),
        name="gate_up",
    )(me, offs, *rows_of, w_gate, w_up)


def gather_hidden(dims, me, pieces, hidden):
    quarter, half = dims["quarter"], dims["part"] // 2
    for j in range(4):
        at = pl.ds(pl.multiple_of((me ^ j) * quarter, ALIGN), quarter)
        for side in range(2):
            hidden[at, side * half : (side + 1) * half] = pieces[2 * j + side][...]


def down_kernel(dims, c, last, me_ref, offs, w_down, *refs):
    experts, window, part = dims["experts"], dims["window"], dims["part"]
    pieces, refs = refs[:8], refs[8:]
    y_in = None
    if c > 0:
        y_in, refs = refs[0], refs[1:]
    if last:
        scale, chosen, rowk, refs = refs[0], refs[1], refs[2], refs[3:]
        if dims["small"]:
            stay, away, held, hidden, sems, y_out = refs
        else:
            out, held, hidden, sems, y_out = refs
        y_out[...] = jnp.zeros_like(y_out)
    else:
        y_out, held, hidden, sems = refs
    units = pl.ds(c * part, part)

    def copy(e):
        return pltpu.make_async_copy(w_down.at[e, units, :], held.at[e], sems.at[e])

    for e in range(experts):
        copy(e).start()
    gather_hidden(dims, me_ref[0], pieces, hidden)
    for batch in batches(experts):
        for e in batch:
            copy(e).wait()
        for e in batch:
            first = aligned(offs[0, e])
            at = pl.ds(first, window)
            got = jnp.dot(hidden[at, :], held[e], preferred_element_type=F32)
            if y_in is not None:
                got = got + y_in[at, :]
            mask = row_mask(dims, first, offs, e)
            if last:
                got = got * scale[at, 0:1]
                y_out[at, :] = jnp.where(mask, got, y_out[at, :].astype(F32)).astype(BF16)
            else:
                y_out[at, :] = jnp.where(mask, got, y_out[at, :])
    if not last:
        return
    rows, total, width = dims["rows"], dims["total"], w_down.shape[2]
    blocks, many = dims["blocks"], min(4, dims["blocks"])
    if dims["small"]:
        order = halving_order(blocks)
        for side, into in enumerate((stay, away)):
            for p in range(0, blocks // 2, many):
                at = [me_ref[1] ^ order[side * (blocks // 2) + p + i] for i in range(many)]
                picked = jnp.concatenate([chosen[i] for i in at], axis=0)
                summed = jnp.dot(picked, y_out[:total, :], preferred_element_type=F32)
                into[p : p + many] = summed.astype(BF16).reshape(many, rows, width)
        return

    def combine(step, carry):
        picked = [choose(dims, rowk, step * many + i) for i in range(many)]
        summed = jnp.dot(
            jnp.concatenate(picked, axis=0), y_out[:total, :], preferred_element_type=F32
        )
        out[pl.ds(step * many, many)] = summed.astype(BF16).reshape(many, rows, width)
        return carry

    lax.fori_loop(0, blocks // many, combine, 0)


def halving_order(blocks):
    bits = blocks.bit_length() - 1
    return [sum(((i >> b) & 1) << (bits - 1 - b) for b in range(bits)) for i in range(blocks)]


def down(dims, c, last, me, offs, w_down, pieces, y, extra):
    experts, padded, part = dims["experts"], dims["padded"], dims["part"]
    width = w_down.shape[2]
    operands = list(pieces) + ([y] if c > 0 else []) + list(extra)
    blocks, rows = dims["blocks"], dims["rows"]
    scratch = [
        pltpu.VMEM((experts, part, width), BF16),
        pltpu.VMEM((padded, part), BF16),
        pltpu.SemaphoreType.DMA((experts,)),
    ]
    if not last:
        outs = (jax.ShapeDtypeStruct((padded, width), F32),)
    else:
        scratch.append(pltpu.VMEM((padded, width), BF16))
        if dims["small"]:
            outs = (jax.ShapeDtypeStruct((blocks // 2, rows, width), BF16),) * 2
        else:
            outs = (jax.ShapeDtypeStruct((blocks, rows, width), BF16),)
    return pl.pallas_call(
        functools.partial(down_kernel, dims, c, last),
        out_shape=outs,
        in_specs=[smem(), smem(), hbm()] + [vmem()] * len(operands),
        out_specs=(vmem(),) * len(outs),
        scratch_shapes=scratch,
        compiler_params=params(),
        cost_estimate=cost(4 * padded * width * part, 2 * experts * part * width + 8 * padded * width),
        name="down",
    )(me, offs, w_down, *operands)


def swap(value, axis, bit):
    count = lax.axis_size(axis)
    return lax.ppermute(value, axis, [(i, i ^ bit) for i in range(count)])


def reduce_chunk(parts):
    gx, uy, g2, u1, g0, u0 = parts
    from_x = swap(gx, "rep", 1)
    from_y = swap(uy, "rep", 2)
    gate_rest = swap((g2 + from_x[1].astype(F32)).astype(BF16), "rep", 2)
    up_rest = swap((u1 + from_y[1].astype(F32)).astype(BF16), "rep", 1)
    gate = g0 + from_x[0].astype(F32) + gate_rest.astype(F32)
    up = u0 + from_y[0].astype(F32) + up_rest.astype(F32)
    hidden = (jax.nn.silu(gate) * up).astype(BF16)
    half = hidden.shape[1] // 2
    return hidden[:, :half], hidden[:, half:]


def spread_chunk(left, right):
    x = (swap(left, "rep", 1), swap(right, "rep", 1))
    y = (swap(left, "rep", 2), swap(right, "rep", 2))
    corner = (swap(x[0], "rep", 2), swap(y[1], "rep", 1))
    return [left, right, *x, *y, *corner]


def gather_tokens(tokens):
    held = {0: tokens}
    bit = lax.axis_size("exp") // 2
    while bit:
        for known in list(held):
            held[known | bit] = swap(held[known], "exp", bit)
        bit //= 2
    return [held[j] for j in range(len(held))]


def sum_over_exp(stay, away):
    bit = 1
    while True:
        came = swap(away, "exp", bit)
        total = stay.astype(F32) + came.astype(F32)
        count = total.shape[0] // 2
        if count == 0:
            return total[0].astype(BF16)
        stay, away = total[:count], total[count:].astype(BF16)
        bit *= 2


def local(tokens, expert_ids, route_weights, w_gate, w_up, w_down):
    rows, top = expert_ids.shape
    width = tokens.shape[1]
    experts, units, _ = w_gate.shape
    blocks = lax.axis_size("exp")
    replicas = lax.axis_size("rep")
    cap = replicas * max(1, rows * top * 3 // (8 * EXPERTS))
    total = ceil_to(experts * blocks * cap, replicas * 128)
    window = ceil_to(blocks * cap, ALIGN) + ALIGN
    part = 256
    small = blocks * rows * total <= 4 * 2**20
    dims = dict(
        blocks=blocks,
        rows=rows,
        top=top,
        experts=experts,
        window=window,
        total=total,
        quarter=total // replicas,
        padded=total + window,
        part=part,
        group=min(blocks, 8),
        tile=512,
        small=small,
    )
    me = jnp.stack([lax.axis_index("rep"), lax.axis_index("exp")]).astype(jnp.int32)
    meta = lax.all_gather(prepare(dims, expert_ids, route_weights), "exp", axis=0)
    if small:
        held = gather_tokens(tokens)
        rowid, probs, rowk, select, offs = route_rows(dims, me, meta)
        sources = [select, *held]
    else:
        gathered = lax.all_gather(tokens, "exp", axis=0)
        rowid, probs, rowk, x, offs = dispatch(dims, me, meta, gathered)
        sources = [x]
    scale, chosen = weigh(dims, offs, rowid, probs, rowk)

    pieces = []
    for c in range(units // part):
        parts = gate_up(dims, c, me, offs, sources, w_gate, w_up)
        if len(sources) > 1:
            sources, parts = [parts[0]], parts[1:]
        pieces.append(spread_chunk(*reduce_chunk(parts)))
    y = None
    last = len(pieces) - 1
    for c in range(last):
        y = down(dims, c, False, me, offs, w_down, pieces[c], y, ())[0]
    mixed = down(dims, last, True, me, offs, w_down, pieces[last], y, (scale, chosen, rowk))
    if small:
        return sum_over_exp(*mixed)
    return lax.psum_scatter(mixed[0], "exp", scatter_dimension=0, tiled=False)


def solution(mesh):
    return jax.shard_map(
        local,
        mesh=mesh,
        in_specs=(
            P("exp", "rep"),
            P("exp", None),
            P("exp", None),
            P("exp", None, "rep"),
            P("exp", None, "rep"),
            P("exp", None, "rep"),
        ),
        out_specs=P("exp", "rep"),
        check_vma=False,
    )
```

```python
import functools
import math

import jax
import jax.numpy as jnp
from jax import lax
from jax.experimental import pallas as pl
from jax.experimental.pallas import tpu as pltpu
from jax.sharding import PartitionSpec as P

EXPERTS = 128
F32 = jnp.float32
BF16 = jnp.bfloat16
VMEM_LIMIT = 56 * 2**20
VMEM_SPARE = 10 * 2**20
ALIGN = 16
META = 16


def ceil_to(value, unit):
    return -(-value // unit) * unit


def vmem():
    return pl.BlockSpec(memory_space=pltpu.VMEM)


def smem():
    return pl.BlockSpec(memory_space=pltpu.SMEM)


def hbm():
    return pl.BlockSpec(memory_space=pl.ANY)


def params(*shapes):
    need = sum(math.prod(s.shape) * jnp.dtype(s.dtype).itemsize for s in shapes if hasattr(s, "dtype"))
    return pltpu.CompilerParams(vmem_limit_bytes=min(VMEM_LIMIT, need + need // 4 + VMEM_SPARE))


def held(*arrays):
    return [jax.ShapeDtypeStruct(a.shape, a.dtype) for a in arrays]


def cost(flops, moved):
    return pl.CostEstimate(flops=int(flops), bytes_accessed=int(moved), transcendentals=0)


def pack_kernel(dims, tokens, ids, weights, packed):
    rows, top = dims["rows"], dims["top"]
    chance = weights[...]
    chance = chance / jnp.sum(chance, axis=0, keepdims=True)
    high = chance.astype(BF16)
    rest = chance - high.astype(F32)
    middle = rest.astype(BF16)
    low = (rest - middle.astype(F32)).astype(BF16)
    packed[:rows, :] = tokens[...]
    packed[rows:, :] = jnp.zeros((META, packed.shape[1]), BF16)
    parts = (ids[...].astype(F32), high.astype(F32), middle.astype(F32), low.astype(F32))
    for i, part in enumerate(parts):
        block = jnp.concatenate([part, jnp.zeros((META - top, rows), F32)], axis=0)
        packed[rows:, i * rows : (i + 1) * rows] = block.astype(BF16)


def pack(dims, tokens, ids, weights):
    return pl.pallas_call(
        functools.partial(pack_kernel, dims),
        out_shape=jax.ShapeDtypeStruct((dims["rows"] + META, tokens.shape[1]), BF16),
        in_specs=[vmem()] * 3,
        out_specs=vmem(),
        compiler_params=params(),
        name="pack",
    )(tokens, ids.T, weights.T)


def loop(count, body, carry):
    if count > 8:
        return lax.fori_loop(0, count, body, carry)
    for i in range(count):
        carry = body(i, carry)
    return carry


def route(dims, base, meta_of, rowid, probs, rowk):
    blocks, rows, top, experts = dims["blocks"], dims["rows"], dims["top"], dims["experts"]
    expert_at = lax.broadcasted_iota(jnp.int32, (experts, rows), 0) + base
    upper = (
        lax.broadcasted_iota(jnp.int32, (rows, rows), 0)
        <= lax.broadcasted_iota(jnp.int32, (rows, rows), 1)
    ).astype(BF16)

    def chosen_ids(block):
        return meta_of(block)[:, :rows].astype(F32)[:top].astype(jnp.int32)

    def count(block, seen):
        held = meta_of(block).astype(F32)[:top]
        ids = held[:, :rows].astype(jnp.int32)
        chance = held[:, rows : 2 * rows] + held[:, 2 * rows : 3 * rows]
        chance = chance + held[:, 3 * rows : 4 * rows]
        member = jnp.zeros((experts, rows), F32)
        share = jnp.zeros((experts, rows), F32)
        for k in range(top):
            hit = ids[k : k + 1, :] == expert_at
            member = member + hit.astype(F32)
            share = share + jnp.where(hit, chance[k : k + 1, :], 0.0)
        upto = jnp.dot(member.astype(BF16), upper, preferred_element_type=F32)
        rowid[block] = jnp.where(member > 0, seen + upto - 1.0, -1e6).astype(jnp.int32)
        probs[block] = share
        return seen + upto[:, rows - 1 : rows]

    total = loop(blocks, count, jnp.zeros((experts, rows), F32))
    starts, before = [], jnp.zeros((1, rows), F32)
    for e in range(experts):
        starts.append(before)
        before = before + total[e : e + 1, :]
    start = jnp.concatenate(starts, axis=0) if experts > 1 else starts[0]
    start, total = start.astype(jnp.int32), total.astype(jnp.int32)

    def place(block, carry):
        ids = chosen_ids(block)
        at = rowid[block] + start
        rowid[block] = at
        found = []
        for k in range(top):
            hit = ids[k : k + 1, :] == expert_at
            found.append(jnp.max(jnp.where(hit, at, -1), axis=0, keepdims=True))
        rowk[block] = jnp.concatenate(found, axis=0)
        return carry

    loop(blocks, place, 0)
    return start, total


def window_hits(dims, rowid, block, e, start):
    at = lax.broadcasted_iota(jnp.int32, (dims["window"], dims["rows"]), 0) + start
    return rowid[block, e : e + 1, :] == at


def aligned(value):
    return pl.multiple_of(value // ALIGN * ALIGN, ALIGN)


def fill_select(dims, rowid, starts, select, step):
    rows = dims["rows"]
    select[...] = jnp.zeros_like(select)
    for e in range(dims["experts"]):
        first = aligned(starts[e])
        at = pl.ds(first, dims["window"])
        for inner in range(dims["group"]):
            cols = slice(inner * rows, (inner + 1) * rows)
            hit = window_hits(dims, rowid, step * dims["group"] + inner, e, first)
            select[at, cols] = select[at, cols] + hit.astype(F32).astype(BF16)


def publish(dims, offs, start, total):
    starts = [start[e, 0] for e in range(dims["experts"])]
    for e in range(dims["experts"]):
        offs[0, e] = starts[e]
        offs[1, e] = total[e, 0]
    return starts


def dispatch_kernel(dims, me_ref, gathered, rowid, probs, rowk, x, offs, select, total):
    blocks, rows, group, tile = dims["blocks"], dims["rows"], dims["group"], dims["tile"]
    start, count = route(
        dims, me_ref[1] * dims["experts"], lambda block: gathered[block, rows:, :], rowid, probs, rowk
    )
    starts = publish(dims, offs, start, count)
    total[...] = jnp.zeros_like(total)

    def body(step, carry):
        fill_select(dims, rowid, starts, select, step)
        part = gathered[pl.ds(step * group, group), :rows, :].reshape(group * rows, x.shape[1])
        for r in range(0, x.shape[0], tile):
            size = min(tile, x.shape[0] - r)
            got = jnp.dot(select[r : r + size, :], part, preferred_element_type=F32)
            got = got + total[r : r + size, :]
            total[r : r + size, :] = got
            x[r : r + size, :] = got.astype(BF16)
        return carry

    lax.fori_loop(0, blocks // group, body, 0)


def route_shapes(dims):
    blocks, rows, top, experts = dims["blocks"], dims["rows"], dims["top"], dims["experts"]
    return (
        jax.ShapeDtypeStruct((blocks, experts, rows), jnp.int32),
        jax.ShapeDtypeStruct((blocks, experts, rows), F32),
        jax.ShapeDtypeStruct((blocks, top, rows), jnp.int32),
    ), jax.ShapeDtypeStruct((2, experts), jnp.int32)


def dispatch(dims, me, gathered):
    shapes, offs = route_shapes(dims)
    width, padded = gathered.shape[2], dims["padded"]
    return pl.pallas_call(
        functools.partial(dispatch_kernel, dims),
        out_shape=shapes + (jax.ShapeDtypeStruct((padded, width), BF16), offs),
        in_specs=[smem(), vmem()],
        out_specs=(vmem(),) * 4 + (smem(),),
        scratch_shapes=[
            pltpu.VMEM((padded, dims["group"] * dims["rows"]), BF16),
            pltpu.VMEM((padded, width), F32),
        ],
        compiler_params=pltpu.CompilerParams(vmem_limit_bytes=VMEM_LIMIT),
        name="dispatch",
    )(me, gathered)


def choose(dims, rowk, block):
    at = lax.broadcasted_iota(jnp.int32, (dims["rows"], dims["total"]), 1)
    rows_of = rowk[block].astype(F32).T.astype(jnp.int32)
    hit = rows_of[:, 0:1] == at
    for k in range(1, dims["top"]):
        hit = hit | (rows_of[:, k : k + 1] == at)
    return hit.astype(F32).astype(BF16)


def weigh_small_kernel(dims, offs, select, probs, scale, chosen, table):
    rows, experts, total, blocks = dims["rows"], dims["experts"], dims["total"], dims["blocks"]
    same = lax.broadcasted_iota(jnp.int32, (rows, rows), 0) == lax.broadcasted_iota(
        jnp.int32, (rows, rows), 1
    )
    eye = same.astype(F32).astype(BF16)
    contract = (((1,), (1,)), ((), ()))
    for b in range(blocks):
        cols = slice(b * rows, (b + 1) * rows)
        picked = lax.dot_general(eye, select[:total, cols], contract, preferred_element_type=F32)
        chosen[b] = picked.astype(BF16)
        exact = probs[b]
        high = exact.astype(BF16)
        rest = exact - high.astype(F32)
        middle = rest.astype(BF16)
        low = (rest - middle.astype(F32)).astype(BF16)
        table[:, cols] = jnp.concatenate([high, middle, low], axis=0)
    wide = lax.dot_general(select[...], table[...], contract, preferred_element_type=F32)
    scale[:, : 3 * experts] = wide
    lane = lax.broadcasted_iota(jnp.int32, (dims["window"], scale.shape[1]), 1)
    for e in range(experts):
        first = aligned(offs[0, e])
        at = pl.ds(first, dims["window"])
        old = scale[at, :]
        mine = (lane == e) | (lane == e + experts) | (lane == e + 2 * experts)
        found = jnp.sum(jnp.where(mine, old, 0.0), axis=1, keepdims=True)
        mask = row_mask(dims, first, offs, e)
        scale[at, :] = jnp.where(mask, jnp.broadcast_to(found, old.shape), old)


def weigh_large_kernel(dims, offs, rowid, probs, scale, chosen):
    chosen[...] = jnp.zeros_like(chosen)
    for e in range(dims["experts"]):
        first = aligned(offs[0, e])
        at = pl.ds(first, dims["window"])

        def share(block, carry):
            hit = window_hits(dims, rowid, block, e, first)
            return carry + jnp.where(hit, probs[block, e : e + 1, :], 0.0)

        shares = loop(dims["blocks"], share, jnp.zeros((dims["window"], dims["rows"]), F32))
        wide = jnp.sum(shares, axis=1, keepdims=True)
        wide = jnp.broadcast_to(wide, (dims["window"], scale.shape[1]))
        scale[at, :] = jnp.where(row_mask(dims, first, offs, e), wide, scale[at, :])


def weigh(dims, offs, rows_of, probs):
    small = dims["small"]
    picked = (dims["blocks"], dims["rows"], dims["total"]) if small else (1, ALIGN, 128)
    outs = (
        jax.ShapeDtypeStruct((dims["padded"], 128), F32),
        jax.ShapeDtypeStruct(picked, BF16),
    )
    table = pltpu.VMEM((3 * dims["experts"], dims["blocks"] * dims["rows"]), BF16)
    return pl.pallas_call(
        functools.partial(weigh_small_kernel if small else weigh_large_kernel, dims),
        out_shape=outs,
        in_specs=[smem(), vmem(), vmem()],
        out_specs=(vmem(), vmem()),
        scratch_shapes=[table] if small else [],
        compiler_params=params(*outs, *held(rows_of, probs)),
        cost_estimate=cost(6e9, 8e6),
        name="weigh",
    )(offs, rows_of, probs)


def row_mask(dims, first, offs, e):
    at = lax.broadcasted_iota(jnp.int32, (dims["window"], 1), 0) + first
    begin = offs[0, e]
    return (at >= begin) & (at < begin + offs[1, e])


def batches(experts):
    return [range(b, min(b + 4, experts)) for b in range(0, experts, 4)]


def gate_up_kernel(dims, c, first_part, me_ref, *refs):
    experts, window, part, quarter = dims["experts"], dims["window"], dims["part"], dims["quarter"]
    if first_part:
        blocks, rows = dims["blocks"], dims["rows"]
        packed, refs = refs[:blocks], refs[blocks:]
        w_gate, w_up, rowid, probs, rowk, x, select, offs_out, refs = *refs[:8], refs[8:]
        gx, uy, g2, u1, g0, u0, gate_w, up_w, gate, up, sems, table, meta = refs
    else:
        offs, x, w_gate, w_up, gx, uy, g2, u1, g0, u0, gate_w, up_w, gate, up, sems = refs
    units = pl.ds(c * part, part)

    def copies(e):
        return (
            pltpu.make_async_copy(w_gate.at[e, units, :], gate_w.at[e], sems.at[0, e]),
            pltpu.make_async_copy(w_up.at[e, units, :], up_w.at[e], sems.at[1, e]),
        )

    for e in range(experts):
        for copy in copies(e):
            copy.start()
    if first_part:
        for j, block in enumerate(packed):
            at = me_ref[1] ^ j
            table[pl.ds(pl.multiple_of(at * rows, rows), rows), :] = block[:rows, :]
            meta[at] = block[rows:, :]
        start, count = route(
            dims, me_ref[1] * experts, lambda block: meta[block], rowid, probs, rowk
        )
        offs = offs_out
        fill_select(dims, rowid, publish(dims, offs, start, count), select, 0)
        for r in range(0, x.shape[0], dims["tile"]):
            size = min(dims["tile"], x.shape[0] - r)
            got = jnp.dot(select[r : r + size, :], table[...], preferred_element_type=F32)
            x[r : r + size, :] = got.astype(BF16)
    contract = (((1,), (1,)), ((), ()))
    for batch in batches(experts):
        for e in batch:
            for copy in copies(e):
                copy.wait()
        for e in batch:
            first = aligned(offs[0, e])
            rows_in = x[pl.ds(first, window), :]
            keep = (lax.broadcasted_iota(jnp.int32, (ALIGN, 1), 0) + first) >= offs[0, e]
            edge, rest = pl.ds(first, ALIGN), pl.ds(first + ALIGN, window - ALIGN)
            for held, into in ((gate_w, gate), (up_w, up)):
                got = lax.dot_general(rows_in, held[e], contract, preferred_element_type=F32)
                into[edge, :] = jnp.where(keep, got[:ALIGN], into[edge, :])
                into[rest, :] = got[ALIGN:]
    me = me_ref[0]

    def piece(total, j):
        return total[pl.ds(pl.multiple_of((me ^ j) * quarter, ALIGN), quarter), :]

    gx[0] = piece(gate, 1).astype(BF16)
    gx[1] = piece(gate, 3).astype(BF16)
    uy[0] = piece(up, 2).astype(BF16)
    uy[1] = piece(up, 3).astype(BF16)
    g2[...] = piece(gate, 2)
    u1[...] = piece(up, 1)
    g0[...] = piece(gate, 0)
    u0[...] = piece(up, 0)


def gate_up(dims, c, me, sources, w_gate, w_up):
    experts, part, quarter, padded = dims["experts"], dims["part"], dims["quarter"], dims["padded"]
    width = w_gate.shape[2]
    half = jax.ShapeDtypeStruct((2, quarter, part), BF16)
    own = jax.ShapeDtypeStruct((quarter, part), F32)
    first_part = len(sources) > 2
    outs = (half, half, own, own, own, own)
    scratch = [
        pltpu.VMEM((experts, part, width), BF16),
        pltpu.VMEM((experts, part, width), BF16),
        pltpu.VMEM((padded, part), F32),
        pltpu.VMEM((padded, part), F32),
        pltpu.SemaphoreType.DMA((2, experts)),
    ]
    into = (vmem(),) * len(outs)
    if first_part:
        blocks, rows = dims["blocks"], dims["rows"]
        shapes, offs = route_shapes(dims)
        x = jax.ShapeDtypeStruct((padded, width), BF16)
        select = jax.ShapeDtypeStruct((padded, blocks * rows), BF16)
        outs = shapes + (x, select, offs) + outs
        into = (vmem(),) * 5 + (smem(),) + into
        scratch.append(pltpu.VMEM((blocks * rows, width), BF16))
        scratch.append(pltpu.VMEM((blocks, META, width), BF16))
        specs = [vmem()] * blocks
    else:
        specs = [smem(), vmem()]
    return pl.pallas_call(
        functools.partial(gate_up_kernel, dims, c, first_part),
        out_shape=outs,
        in_specs=[smem()] + specs + [hbm(), hbm()],
        out_specs=into,
        scratch_shapes=scratch,
        compiler_params=params(*outs, *held(*sources), *[b for b in scratch if "dma" not in str(b)]),
        cost_estimate=cost(4 * padded * width * part, 4 * experts * part * width + 2 * padded * width),
        name="gate_up",
    )(me, *sources, w_gate, w_up)


def gather_hidden(dims, me, pieces, hidden):
    quarter = dims["quarter"]
    for j, piece in zip((0, 3, 1, 2), pieces):
        hidden[pl.ds(pl.multiple_of((me ^ j) * quarter, ALIGN), quarter), :] = piece[...]


def down_kernel(dims, c, last, me_ref, offs, w_down, *refs):
    experts, window, part = dims["experts"], dims["window"], dims["part"]
    pieces, refs = refs[:4], refs[4:]
    y_in = None
    if c > 0:
        y_in, refs = refs[0], refs[1:]
    if last:
        scale, chosen, rowk, refs = refs[0], refs[1], refs[2], refs[3:]
        if dims["small"]:
            stay, away, held, hidden, sems, y_out = refs
        else:
            out, held, hidden, sems, y_out = refs
        y_out[...] = jnp.zeros_like(y_out)
    else:
        y_out, held, hidden, sems = refs
    units = pl.ds(c * part, part)

    def copy(e):
        return pltpu.make_async_copy(w_down.at[e, units, :], held.at[e], sems.at[e])

    for e in range(experts):
        copy(e).start()
    gather_hidden(dims, me_ref[0], pieces, hidden)
    for batch in batches(experts):
        for e in batch:
            copy(e).wait()
        for e in batch:
            first = aligned(offs[0, e])
            at = pl.ds(first, window)
            got = jnp.dot(hidden[at, :], held[e], preferred_element_type=F32)
            if y_in is not None:
                got = got + y_in[at, :]
            mask = row_mask(dims, first, offs, e)
            if last:
                got = got * scale[at, 0:1]
                y_out[at, :] = jnp.where(mask, got, y_out[at, :].astype(F32)).astype(BF16)
            else:
                y_out[at, :] = jnp.where(mask, got, y_out[at, :])
    if not last:
        return
    rows, total, width = dims["rows"], dims["total"], w_down.shape[2]
    blocks, many = dims["blocks"], min(4, dims["blocks"])
    if dims["small"]:
        for side, into in enumerate((stay, away)):
            for p in range(0, blocks // 2, many):
                at = [me_ref[1] ^ (2 * (p + i) + side) for i in range(many)]
                picked = jnp.concatenate([chosen[i] for i in at], axis=0)
                summed = jnp.dot(picked, y_out[:total, :], preferred_element_type=F32)
                into[p : p + many] = summed.astype(BF16).reshape(many, rows, width)
        return

    def combine(step, carry):
        picked = [choose(dims, rowk, step * many + i) for i in range(many)]
        summed = jnp.dot(
            jnp.concatenate(picked, axis=0), y_out[:total, :], preferred_element_type=F32
        )
        out[pl.ds(step * many, many)] = summed.astype(BF16).reshape(many, rows, width)
        return carry

    lax.fori_loop(0, blocks // many, combine, 0)


def down(dims, c, last, me, offs, w_down, pieces, y, extra):
    experts, padded, part = dims["experts"], dims["padded"], dims["part"]
    width = w_down.shape[2]
    operands = list(pieces) + ([y] if c > 0 else []) + list(extra)
    blocks, rows = dims["blocks"], dims["rows"]
    scratch = [
        pltpu.VMEM((experts, part, width), BF16),
        pltpu.VMEM((padded, part), BF16),
        pltpu.SemaphoreType.DMA((experts,)),
    ]
    if not last:
        outs = (jax.ShapeDtypeStruct((padded, width), F32),)
    else:
        scratch.append(pltpu.VMEM((padded, width), BF16))
        if dims["small"]:
            outs = (jax.ShapeDtypeStruct((blocks // 2, rows, width), BF16),) * 2
        else:
            outs = (jax.ShapeDtypeStruct((blocks, rows, width), BF16),)
    return pl.pallas_call(
        functools.partial(down_kernel, dims, c, last),
        out_shape=outs,
        in_specs=[smem(), smem(), hbm()] + [vmem()] * len(operands),
        out_specs=(vmem(),) * len(outs),
        scratch_shapes=scratch,
        compiler_params=params(*outs, *held(*operands), *[b for b in scratch if "dma" not in str(b)]),
        cost_estimate=cost(4 * padded * width * part, 2 * experts * part * width + 8 * padded * width),
        name="down",
    )(me, offs, w_down, *operands)


def swap(value, axis, bit):
    count = lax.axis_size(axis)
    return lax.ppermute(value, axis, [(i, i ^ bit) for i in range(count)])


def reduce_chunk(parts):
    gx, uy, g2, u1, g0, u0 = parts
    from_x = swap(gx, "rep", 1)
    from_y = swap(uy, "rep", 2)
    gate_rest = swap((g2 + from_x[1].astype(F32)).astype(BF16), "rep", 2)
    up_rest = swap((u1 + from_y[1].astype(F32)).astype(BF16), "rep", 1)
    gate = g0 + from_x[0].astype(F32) + gate_rest.astype(F32)
    up = u0 + from_y[0].astype(F32) + up_rest.astype(F32)
    return (jax.nn.silu(gate) * up).astype(BF16)


def spread_chunk(hidden):
    return [hidden] + [swap(hidden, "rep", bit) for bit in (3, 1, 2)]


def gather_tokens(tokens):
    held = {0: tokens}
    bit = lax.axis_size("exp") // 2
    while bit:
        for known in list(held):
            held[known | bit] = swap(held[known], "exp", bit)
        bit //= 2
    return [held[j] for j in range(len(held))]


def sum_over_exp(stay, away):
    total = stay.astype(F32) + swap(away, "exp", 1).astype(F32)
    came = [
        swap(total[i].astype(BF16), "exp", 2 * i) for i in range(total.shape[0] - 1, 0, -1)
    ]
    return (total[0] + sum(part.astype(F32) for part in came)).astype(BF16)


def local(tokens, expert_ids, route_weights, w_gate, w_up, w_down):
    rows, top = expert_ids.shape
    width = tokens.shape[1]
    experts, units, _ = w_gate.shape
    blocks = lax.axis_size("exp")
    replicas = lax.axis_size("rep")
    cap = replicas * max(1, rows * top * 3 // (8 * EXPERTS))
    total = ceil_to(experts * blocks * cap, replicas * 128)
    window = ceil_to(blocks * cap, ALIGN) + ALIGN
    part = units // 2
    small = blocks * rows * total <= 4 * 2**20
    dims = dict(
        blocks=blocks,
        rows=rows,
        top=top,
        experts=experts,
        window=window,
        total=total,
        quarter=total // replicas,
        padded=total + window,
        part=part,
        group=min(blocks, 8),
        tile=512,
        small=small,
    )
    me = jnp.stack([lax.axis_index("rep"), lax.axis_index("exp")]).astype(jnp.int32)
    packed = pack(dims, tokens, expert_ids, route_weights)
    if small:
        sources = gather_tokens(packed)
    else:
        gathered = lax.all_gather(packed, "exp", axis=0)
        rowid, probs, rowk, x, offs = dispatch(dims, me, gathered)
        rows_of, sources = rowid, [offs, x]

    pieces = []
    for c in range(units // part):
        parts = gate_up(dims, c, me, sources, w_gate, w_up)
        if len(sources) > 2:
            rowid, probs, rowk, x, rows_of, offs = parts[:6]
            sources, parts = [offs, x], parts[6:]
        pieces.append(spread_chunk(reduce_chunk(parts)))
    scale, chosen = weigh(dims, offs, rows_of, probs)
    y = None
    last = len(pieces) - 1
    for c in range(last):
        y = down(dims, c, False, me, offs, w_down, pieces[c], y, ())[0]
    mixed = down(dims, last, True, me, offs, w_down, pieces[last], y, (scale, chosen, rowk))
    if small:
        return sum_over_exp(*mixed)
    return lax.psum_scatter(mixed[0], "exp", scatter_dimension=0, tiled=False)


def solution(mesh):
    return jax.shard_map(
        local,
        mesh=mesh,
        in_specs=(
            P("exp", "rep"),
            P("exp", None),
            P("exp", None),
            P("exp", None, "rep"),
            P("exp", None, "rep"),
            P("exp", None, "rep"),
        ),
        out_specs=P("exp", "rep"),
        check_vma=False,
    )
```

```python
import functools
import math

import jax
import jax.numpy as jnp
from jax import lax
from jax.experimental import pallas as pl
from jax.experimental.pallas import tpu as pltpu
from jax.sharding import PartitionSpec as P

EXPERTS = 128
F32 = jnp.float32
BF16 = jnp.bfloat16
VMEM_LIMIT = 56 * 2**20
VMEM_SPARE = 10 * 2**20
ALIGN = 16
META = 16


def ceil_to(value, unit):
    return -(-value // unit) * unit


def vmem():
    return pl.BlockSpec(memory_space=pltpu.VMEM)


def smem():
    return pl.BlockSpec(memory_space=pltpu.SMEM)


def hbm():
    return pl.BlockSpec(memory_space=pltpu.HBM)


def params(*shapes):
    need = sum(math.prod(s.shape) * jnp.dtype(s.dtype).itemsize for s in shapes if hasattr(s, "dtype"))
    return pltpu.CompilerParams(vmem_limit_bytes=min(VMEM_LIMIT, need + need // 4 + VMEM_SPARE))


def held(*arrays):
    return [jax.ShapeDtypeStruct(a.shape, a.dtype) for a in arrays]


def cost(flops, moved):
    return pl.CostEstimate(flops=int(flops), bytes_accessed=int(moved), transcendentals=0)


def pack_kernel(dims, ids, weights, meta):
    rows, top = dims["rows"], dims["top"]
    chance = weights[...]
    chance = chance / jnp.sum(chance, axis=0, keepdims=True)
    high = chance.astype(BF16)
    rest = chance - high.astype(F32)
    middle = rest.astype(BF16)
    low = (rest - middle.astype(F32)).astype(BF16)
    meta[...] = jnp.zeros_like(meta)
    parts = (ids[...].astype(F32), high.astype(F32), middle.astype(F32), low.astype(F32))
    for i, part in enumerate(parts):
        block = jnp.concatenate([part, jnp.zeros((META - top, rows), F32)], axis=0)
        meta[:, i * rows : (i + 1) * rows] = block.astype(BF16)


def pack(dims, ids, weights, width):
    return pl.pallas_call(
        functools.partial(pack_kernel, dims),
        out_shape=jax.ShapeDtypeStruct((META, width), BF16),
        in_specs=[vmem()] * 2,
        out_specs=vmem(),
        compiler_params=params(),
        name="pack",
    )(ids.T, weights.T)


def loop(count, body, carry):
    if count > 8:
        return lax.fori_loop(0, count, body, carry)
    for i in range(count):
        carry = body(i, carry)
    return carry


def route(dims, base, meta_of, rowid, probs, rowk):
    blocks, rows, top, experts = dims["blocks"], dims["rows"], dims["top"], dims["experts"]
    expert_at = lax.broadcasted_iota(jnp.int32, (experts, rows), 0) + base
    upper = (
        lax.broadcasted_iota(jnp.int32, (rows, rows), 0)
        <= lax.broadcasted_iota(jnp.int32, (rows, rows), 1)
    ).astype(BF16)

    def chosen_ids(block):
        return meta_of(block)[:, :rows].astype(F32)[:top].astype(jnp.int32)

    def count(block, seen):
        held = meta_of(block).astype(F32)[:top]
        ids = held[:, :rows].astype(jnp.int32)
        chance = held[:, rows : 2 * rows] + held[:, 2 * rows : 3 * rows]
        chance = chance + held[:, 3 * rows : 4 * rows]
        member = jnp.zeros((experts, rows), F32)
        share = jnp.zeros((experts, rows), F32)
        for k in range(top):
            hit = ids[k : k + 1, :] == expert_at
            member = member + hit.astype(F32)
            share = share + jnp.where(hit, chance[k : k + 1, :], 0.0)
        upto = jnp.dot(member.astype(BF16), upper, preferred_element_type=F32)
        rowid[block] = jnp.where(member > 0, seen + upto - 1.0, -1e6).astype(jnp.int32)
        probs[block] = share
        return seen + upto[:, rows - 1 : rows]

    total = loop(blocks, count, jnp.zeros((experts, rows), F32))
    starts, before = [], jnp.zeros((1, rows), F32)
    for e in range(experts):
        starts.append(before)
        before = before + total[e : e + 1, :]
    start = jnp.concatenate(starts, axis=0) if experts > 1 else starts[0]
    start, total = start.astype(jnp.int32), total.astype(jnp.int32)

    def place(block, carry):
        ids = chosen_ids(block)
        at = rowid[block] + start
        rowid[block] = at
        found = []
        for k in range(top):
            hit = ids[k : k + 1, :] == expert_at
            found.append(jnp.max(jnp.where(hit, at, -1), axis=0, keepdims=True))
        rowk[block] = jnp.concatenate(found, axis=0)
        return carry

    loop(blocks, place, 0)
    return start, total


def window_hits(dims, rowid, block, e, start):
    at = lax.broadcasted_iota(jnp.int32, (dims["window"], dims["rows"]), 0) + start
    return rowid[block, e : e + 1, :] == at


def aligned(dims, value):
    return pl.multiple_of(jnp.minimum(value // ALIGN * ALIGN, dims["total"]), ALIGN)


def fill_select(dims, rowid, starts, select, step):
    rows = dims["rows"]
    select[...] = jnp.zeros_like(select)
    for e in range(dims["experts"]):
        first = aligned(dims, starts[e])
        at = pl.ds(first, dims["window"])
        for inner in range(dims["group"]):
            cols = slice(inner * rows, (inner + 1) * rows)
            hit = window_hits(dims, rowid, step * dims["group"] + inner, e, first)
            select[at, cols] = select[at, cols] + hit.astype(F32).astype(BF16)


def publish(dims, offs, start, total):
    starts = [start[e, 0] for e in range(dims["experts"])]
    for e in range(dims["experts"]):
        offs[0, e] = starts[e]
        offs[1, e] = total[e, 0]
    return starts


def fullest(dims, meta):
    blocks, rows, top, experts = dims["blocks"], dims["rows"], dims["top"], dims["experts"]
    ids = [meta[b][:, :rows].astype(F32)[:top].astype(jnp.int32) for b in range(blocks)]
    counts = []
    for group in range(blocks):
        mine = jnp.zeros((top, rows), F32)
        for held_ids in ids:
            inside = (held_ids >= group * experts) & (held_ids < (group + 1) * experts)
            mine = mine + inside.astype(F32)
        counts.append(jnp.sum(mine, axis=0, keepdims=True))
    return jnp.max(jnp.sum(jnp.concatenate(counts, axis=0), axis=1, keepdims=True)).astype(jnp.int32)


def route_kernel(dims, order, me_ref, packed, rowid, probs, rowk, select, offs, peak, meta):
    for p, j in enumerate(order):
        meta[me_ref[1] ^ j] = packed[p]
    start, count = route(dims, me_ref[1] * dims["experts"], lambda b: meta[b], rowid, probs, rowk)
    starts = publish(dims, offs, start, count)
    peak[0] = fullest(dims, meta)
    fill_select(dims, rowid, starts, select, 0)


def route_rows(dims, order, me, packed):
    shapes, offs = route_shapes(dims)
    select = jax.ShapeDtypeStruct((dims["padded"], dims["blocks"] * dims["rows"]), BF16)
    outs = shapes + (select, offs, jax.ShapeDtypeStruct((1,), jnp.int32))
    scratch = pltpu.VMEM(packed.shape, BF16)
    return pl.pallas_call(
        functools.partial(route_kernel, dims, order),
        out_shape=outs,
        in_specs=[smem(), vmem()],
        out_specs=(vmem(),) * 4 + (smem(),) * 2,
        scratch_shapes=[scratch],
        compiler_params=params(*outs, *held(packed), scratch),
        cost_estimate=cost(4e9, 4e6),
        name="route",
    )(me, packed)


def dispatch_kernel(dims, me_ref, packed, gathered, rowid, probs, rowk, x, offs, select, total):
    blocks, rows, group, tile = dims["blocks"], dims["rows"], dims["group"], dims["tile"]
    start, count = route(
        dims, me_ref[1] * dims["experts"], lambda block: packed[block], rowid, probs, rowk
    )
    starts = publish(dims, offs, start, count)
    total[...] = jnp.zeros_like(total)

    def body(step, carry):
        fill_select(dims, rowid, starts, select, step)
        part = gathered[pl.ds(step * group, group)].reshape(group * rows, x.shape[1])
        for r in range(0, x.shape[0], tile):
            size = min(tile, x.shape[0] - r)
            got = jnp.dot(select[r : r + size, :], part, preferred_element_type=F32)
            got = got + total[r : r + size, :]
            total[r : r + size, :] = got
            x[r : r + size, :] = got.astype(BF16)
        return carry

    lax.fori_loop(0, blocks // group, body, 0)


def route_shapes(dims):
    blocks, rows, top, experts = dims["blocks"], dims["rows"], dims["top"], dims["experts"]
    return (
        jax.ShapeDtypeStruct((blocks, experts, rows), jnp.int32),
        jax.ShapeDtypeStruct((blocks, experts, rows), F32),
        jax.ShapeDtypeStruct((blocks, top, rows), jnp.int32),
    ), jax.ShapeDtypeStruct((2, experts), jnp.int32)


def dispatch(dims, me, packed, gathered):
    shapes, offs = route_shapes(dims)
    width, padded = gathered.shape[2], dims["padded"]
    return pl.pallas_call(
        functools.partial(dispatch_kernel, dims),
        out_shape=shapes + (jax.ShapeDtypeStruct((padded, width), BF16), offs),
        in_specs=[smem(), vmem(), vmem()],
        out_specs=(vmem(),) * 4 + (smem(),),
        scratch_shapes=[
            pltpu.VMEM((padded, dims["group"] * dims["rows"]), BF16),
            pltpu.VMEM((padded, width), F32),
        ],
        compiler_params=pltpu.CompilerParams(vmem_limit_bytes=VMEM_LIMIT),
        name="dispatch",
    )(me, packed, gathered)


def choose(dims, rowk, block):
    at = lax.broadcasted_iota(jnp.int32, (dims["rows"], dims["total"]), 1)
    rows_of = rowk[block].astype(F32).T.astype(jnp.int32)
    hit = rows_of[:, 0:1] == at
    for k in range(1, dims["top"]):
        hit = hit | (rows_of[:, k : k + 1] == at)
    return hit.astype(F32).astype(BF16)


def weigh_small_kernel(dims, offs, select, probs, scale, chosen, table):
    rows, experts, total, blocks = dims["rows"], dims["experts"], dims["total"], dims["blocks"]
    same = lax.broadcasted_iota(jnp.int32, (rows, rows), 0) == lax.broadcasted_iota(
        jnp.int32, (rows, rows), 1
    )
    eye = same.astype(F32).astype(BF16)
    contract = (((1,), (1,)), ((), ()))
    for b in range(blocks):
        cols = slice(b * rows, (b + 1) * rows)
        picked = lax.dot_general(eye, select[:total, cols], contract, preferred_element_type=F32)
        chosen[b] = picked.astype(BF16)
        exact = probs[b]
        high = exact.astype(BF16)
        rest = exact - high.astype(F32)
        middle = rest.astype(BF16)
        low = (rest - middle.astype(F32)).astype(BF16)
        table[:, cols] = jnp.concatenate([high, middle, low], axis=0)
    wide = lax.dot_general(
        select[: scale.shape[0], :], table[...], contract, preferred_element_type=F32
    )
    scale[:, : 3 * experts] = wide
    lane = lax.broadcasted_iota(jnp.int32, (dims["window"], scale.shape[1]), 1)
    for e in range(experts):
        first = aligned(dims, offs[0, e])
        at = pl.ds(first, dims["window"])
        old = scale[at, :]
        mine = (lane == e) | (lane == e + experts) | (lane == e + 2 * experts)
        found = jnp.sum(jnp.where(mine, old, 0.0), axis=1, keepdims=True)
        mask = row_mask(dims, first, offs, e)
        scale[at, :] = jnp.where(mask, jnp.broadcast_to(found, old.shape), old)


def weigh_large_kernel(dims, offs, rowid, probs, scale, chosen):
    chosen[...] = jnp.zeros_like(chosen)
    for e in range(dims["experts"]):
        first = aligned(dims, offs[0, e])
        at = pl.ds(first, dims["window"])

        def share(block, carry):
            hit = window_hits(dims, rowid, block, e, first)
            return carry + jnp.where(hit, probs[block, e : e + 1, :], 0.0)

        shares = loop(dims["blocks"], share, jnp.zeros((dims["window"], dims["rows"]), F32))
        wide = jnp.sum(shares, axis=1, keepdims=True)
        wide = jnp.broadcast_to(wide, (dims["window"], scale.shape[1]))
        scale[at, :] = jnp.where(row_mask(dims, first, offs, e), wide, scale[at, :])


def weigh(dims, offs, rows_of, probs):
    small = dims["small"]
    picked = (dims["blocks"], dims["rows"], dims["total"]) if small else (1, ALIGN, 128)
    outs = (
        jax.ShapeDtypeStruct((dims["padded"], 128), F32),
        jax.ShapeDtypeStruct(picked, BF16),
    )
    table = pltpu.VMEM((3 * dims["experts"], dims["blocks"] * dims["rows"]), BF16)
    return pl.pallas_call(
        functools.partial(weigh_small_kernel if small else weigh_large_kernel, dims),
        out_shape=outs,
        in_specs=[smem(), vmem(), vmem()],
        out_specs=(vmem(), vmem()),
        scratch_shapes=[table] if small else [],
        compiler_params=params(*outs, *held(rows_of, probs)),
        cost_estimate=cost(6e9, 8e6),
        name="weigh",
    )(offs, rows_of, probs)


def row_mask(dims, first, offs, e):
    at = lax.broadcasted_iota(jnp.int32, (dims["window"], 1), 0) + first
    begin = offs[0, e]
    return (at >= begin) & (at < begin + offs[1, e])


def batches(experts):
    return [range(b, min(b + 4, experts)) for b in range(0, experts, 4)]


def gate_up_kernel(dims, c, first_part, me_ref, *refs):
    experts, window, part, quarter = dims["experts"], dims["window"], dims["part"], dims["quarter"]
    if first_part:
        blocks, rows = dims["blocks"], dims["rows"]
        offs, select, tokens, refs = refs[0], refs[1], refs[2 : 2 + blocks], refs[2 + blocks :]
        w_gate, w_up, x, gx, uy, g2, u1, g0, u0, gate_w, up_w, gate, up, sems, table = refs
    else:
        offs, x, w_gate, w_up, gx, uy, g2, u1, g0, u0, gate_w, up_w, gate, up, sems = refs
    units = pl.ds(c * part, part)

    def copies(e):
        return (
            pltpu.make_async_copy(w_gate.at[e, units, :], gate_w.at[e], sems.at[0, e]),
            pltpu.make_async_copy(w_up.at[e, units, :], up_w.at[e], sems.at[1, e]),
        )

    for e in range(experts):
        for copy in copies(e):
            copy.start()
    if first_part:
        for j, block in enumerate(tokens):
            at = pl.multiple_of((me_ref[1] ^ j) * rows, rows)
            table[pl.ds(at, rows), :] = block[...]
        for r in range(0, x.shape[0], dims["tile"]):
            size = min(dims["tile"], x.shape[0] - r)
            got = jnp.dot(select[r : r + size, :], table[...], preferred_element_type=F32)
            x[r : r + size, :] = got.astype(BF16)
    contract = (((1,), (1,)), ((), ()))
    for batch in batches(experts):
        for e in batch:
            for copy in copies(e):
                copy.wait()
        for e in batch:
            first = aligned(dims, offs[0, e])
            rows_in = x[pl.ds(first, window), :]
            keep = (lax.broadcasted_iota(jnp.int32, (ALIGN, 1), 0) + first) >= offs[0, e]
            edge, rest = pl.ds(first, ALIGN), pl.ds(first + ALIGN, window - ALIGN)
            for held, into in ((gate_w, gate), (up_w, up)):
                got = lax.dot_general(rows_in, held[e], contract, preferred_element_type=F32)
                into[edge, :] = jnp.where(keep, got[:ALIGN], into[edge, :])
                into[rest, :] = got[ALIGN:]
    me = me_ref[0]

    def piece(total, j):
        return total[pl.ds(pl.multiple_of((me ^ j) * quarter, ALIGN), quarter), :]

    gx[0] = piece(gate, 1).astype(BF16)
    gx[1] = piece(gate, 3).astype(BF16)
    uy[0] = piece(up, 2).astype(BF16)
    uy[1] = piece(up, 3).astype(BF16)
    g2[...] = piece(gate, 2)
    u1[...] = piece(up, 1)
    g0[...] = piece(gate, 0)
    u0[...] = piece(up, 0)


def gate_up(dims, c, me, sources, w_gate, w_up):
    experts, part, quarter, padded = dims["experts"], dims["part"], dims["quarter"], dims["padded"]
    width = w_gate.shape[2]
    half = jax.ShapeDtypeStruct((2, quarter, part), BF16)
    own = jax.ShapeDtypeStruct((quarter, part), F32)
    first_part = len(sources) > 2
    outs = (half, half, own, own, own, own)
    scratch = [
        pltpu.VMEM((experts, part, width), BF16),
        pltpu.VMEM((experts, part, width), BF16),
        pltpu.VMEM((padded, part), F32),
        pltpu.VMEM((padded, part), F32),
        pltpu.SemaphoreType.DMA((2, experts)),
    ]
    if first_part:
        outs = (jax.ShapeDtypeStruct((padded, width), BF16),) + outs
        scratch.append(pltpu.VMEM((dims["blocks"] * dims["rows"], width), BF16))
    return pl.pallas_call(
        functools.partial(gate_up_kernel, dims, c, first_part),
        out_shape=outs,
        in_specs=[smem(), smem()] + [vmem()] * (len(sources) - 1) + [hbm(), hbm()],
        out_specs=(vmem(),) * len(outs),
        scratch_shapes=scratch,
        compiler_params=params(*outs, *held(*sources), *[b for b in scratch if "dma" not in str(b)]),
        cost_estimate=cost(4 * padded * width * part, 4 * experts * part * width + 2 * padded * width),
        name="gate_up",
    )(me, *sources, w_gate, w_up)


def gather_hidden(dims, me, pieces, hidden):
    quarter = dims["quarter"]
    for j, piece in zip((0, 3, 1, 2), pieces):
        hidden[pl.ds(pl.multiple_of((me ^ j) * quarter, ALIGN), quarter), :] = piece[...]


def down_kernel(dims, c, last, me_ref, offs, w_down, *refs):
    experts, window, part = dims["experts"], dims["window"], dims["part"]
    pieces, refs = refs[:4], refs[4:]
    y_in = None
    if c > 0:
        y_in, refs = refs[0], refs[1:]
    if last:
        scale, chosen, rowk, refs = refs[0], refs[1], refs[2], refs[3:]
        if dims["small"]:
            stay, away, held, hidden, sems, y_out = refs
        else:
            out, held, hidden, sems, y_out = refs
        y_out[...] = jnp.zeros_like(y_out)
    else:
        y_out, held, hidden, sems = refs
    units = pl.ds(c * part, part)

    def copy(e):
        return pltpu.make_async_copy(w_down.at[e, units, :], held.at[e], sems.at[e])

    for e in range(experts):
        copy(e).start()
    gather_hidden(dims, me_ref[0], pieces, hidden)
    for batch in batches(experts):
        for e in batch:
            copy(e).wait()
        for e in batch:
            first = aligned(dims, offs[0, e])
            at = pl.ds(first, window)
            got = jnp.dot(hidden[at, :], held[e], preferred_element_type=F32)
            if y_in is not None:
                got = got + y_in[at, :]
            mask = row_mask(dims, first, offs, e)
            if last:
                got = got * scale[at, 0:1]
                y_out[at, :] = jnp.where(mask, got, y_out[at, :].astype(F32)).astype(BF16)
            else:
                y_out[at, :] = jnp.where(mask, got, y_out[at, :])
    if not last:
        return
    rows, total, width = dims["rows"], dims["total"], w_down.shape[2]
    blocks, many = dims["blocks"], min(4, dims["blocks"])
    if dims["small"]:
        for side, into in enumerate((stay, away)):
            for p in range(0, blocks // 2, many):
                at = [me_ref[1] ^ (2 * (p + i) + side) for i in range(many)]
                picked = jnp.concatenate([chosen[i] for i in at], axis=0)
                summed = jnp.dot(picked, y_out[:total, :], preferred_element_type=F32)
                into[p : p + many] = summed.astype(BF16).reshape(many, rows, width)
        return

    def combine(step, carry):
        picked = [choose(dims, rowk, step * many + i) for i in range(many)]
        summed = jnp.dot(
            jnp.concatenate(picked, axis=0), y_out[:total, :], preferred_element_type=F32
        )
        out[pl.ds(step * many, many)] = summed.astype(BF16).reshape(many, rows, width)
        return carry

    lax.fori_loop(0, blocks // many, combine, 0)


def down(dims, c, last, me, offs, w_down, pieces, y, extra):
    experts, padded, part = dims["experts"], dims["padded"], dims["part"]
    width = w_down.shape[2]
    operands = list(pieces) + ([y] if c > 0 else []) + list(extra)
    blocks, rows = dims["blocks"], dims["rows"]
    scratch = [
        pltpu.VMEM((experts, part, width), BF16),
        pltpu.VMEM((padded, part), BF16),
        pltpu.SemaphoreType.DMA((experts,)),
    ]
    if not last:
        outs = (jax.ShapeDtypeStruct((padded, width), F32),)
    else:
        scratch.append(pltpu.VMEM((padded, width), BF16))
        if dims["small"]:
            outs = (jax.ShapeDtypeStruct((blocks // 2, rows, width), BF16),) * 2
        else:
            outs = (jax.ShapeDtypeStruct((blocks, rows, width), BF16),)
    return pl.pallas_call(
        functools.partial(down_kernel, dims, c, last),
        out_shape=outs,
        in_specs=[smem(), smem(), hbm()] + [vmem()] * len(operands),
        out_specs=(vmem(),) * len(outs),
        scratch_shapes=scratch,
        compiler_params=params(*outs, *held(*operands), *[b for b in scratch if "dma" not in str(b)]),
        cost_estimate=cost(4 * padded * width * part, 2 * experts * part * width + 8 * padded * width),
        name="down",
    )(me, offs, w_down, *operands)


def swap(value, axis, bit):
    count = lax.axis_size(axis)
    return lax.ppermute(value, axis, [(i, i ^ bit) for i in range(count)])


def reduce_chunk(parts):
    gx, uy, g2, u1, g0, u0 = parts
    from_x = swap(gx, "rep", 1)
    from_y = swap(uy, "rep", 2)
    gate_rest = swap((g2 + from_x[1].astype(F32)).astype(BF16), "rep", 2)
    up_rest = swap((u1 + from_y[1].astype(F32)).astype(BF16), "rep", 1)
    gate = g0 + from_x[0].astype(F32) + gate_rest.astype(F32)
    up = u0 + from_y[0].astype(F32) + up_rest.astype(F32)
    return (jax.nn.silu(gate) * up).astype(BF16)


def spread_chunk(hidden):
    return [hidden] + [swap(hidden, "rep", bit) for bit in (3, 1, 2)]


def gather_tokens(tokens):
    blocks = {0: tokens}
    bit = lax.axis_size("exp") // 2
    while bit:
        for known in list(blocks):
            blocks[known | bit] = swap(blocks[known], "exp", bit)
        bit //= 2
    return [blocks[j] for j in range(len(blocks))]


def gather_meta(meta):
    order, packed, bit = [0], meta[None], 1
    while bit < lax.axis_size("exp"):
        packed = jnp.concatenate([packed, swap(packed, "exp", bit)], axis=0)
        order = order + [j | bit for j in order]
        bit *= 2
    return order, packed


def sum_over_exp(stay, away):
    total = stay.astype(F32) + swap(away, "exp", 1).astype(F32)
    came = [
        swap(total[i].astype(BF16), "exp", 2 * i) for i in range(total.shape[0] - 1, 0, -1)
    ]
    return (total[0] + sum(part.astype(F32) for part in came)).astype(BF16)


def local(tokens, expert_ids, route_weights, w_gate, w_up, w_down):
    rows, top = expert_ids.shape
    width = tokens.shape[1]
    experts, units, _ = w_gate.shape
    blocks = lax.axis_size("exp")
    replicas = lax.axis_size("rep")
    cap = replicas * max(1, rows * top * 3 // (8 * EXPERTS))
    total = ceil_to(experts * blocks * cap, replicas * 128)
    window = ceil_to(blocks * cap, ALIGN) + ALIGN
    part = units // 2
    small = blocks * rows * total <= 4 * 2**20

    def sizes(total):
        return dict(
            blocks=blocks,
            rows=rows,
            top=top,
            experts=experts,
            window=window,
            total=total,
            quarter=total // replicas,
            padded=total + window,
            part=part,
            group=min(blocks, 8),
            tile=512,
            small=small,
        )

    full = sizes(total)
    me = jnp.stack([lax.axis_index("rep"), lax.axis_index("exp")]).astype(jnp.int32)
    meta = pack(full, expert_ids, route_weights, width)
    if not small:
        packed = lax.all_gather(meta, "exp", axis=0)
        gathered = lax.all_gather(tokens, "exp", axis=0)
        rowid, probs, rowk, x, offs = dispatch(full, me, packed, gathered)
        return one_pass(full, me, [offs, x], rowid, probs, rowk, w_gate, w_up, w_down)
    blocks_of = gather_tokens(tokens)
    order, packed = gather_meta(meta)
    rowid, probs, rowk, select, offs, peak = route_rows(full, order, me, packed)
    sources = [offs, select, *blocks_of]
    usual = min(total, ceil_to(rows * top * 5 // 4, replicas * 64))
    mixed = one_pass(sizes(usual), me, sources, select, probs, rowk, w_gate, w_up, w_down)
    if usual == total:
        return mixed
    return lax.cond(
        peak[0] > usual,
        lambda: one_pass(full, me, sources, select, probs, rowk, w_gate, w_up, w_down),
        lambda: mixed,
    )


def one_pass(dims, me, sources, rows_of, probs, rowk, w_gate, w_up, w_down):
    pieces, offs = [], sources[0]
    scale, chosen = weigh(dims, offs, rows_of, probs)
    for c in range(w_gate.shape[1] // dims["part"]):
        parts = gate_up(dims, c, me, sources, w_gate, w_up)
        if len(sources) > 2:
            sources, parts = [offs, parts[0]], parts[1:]
        pieces.append(spread_chunk(reduce_chunk(parts)))
    y = None
    last = len(pieces) - 1
    for c in range(last):
        y = down(dims, c, False, me, offs, w_down, pieces[c], y, ())[0]
    mixed = down(dims, last, True, me, offs, w_down, pieces[last], y, (scale, chosen, rowk))
    if dims["small"]:
        return sum_over_exp(*mixed)
    return lax.psum_scatter(mixed[0], "exp", scatter_dimension=0, tiled=False)


def solution(mesh):
    return jax.shard_map(
        local,
        mesh=mesh,
        in_specs=(
            P("exp", "rep"),
            P("exp", None),
            P("exp", None),
            P("exp", None, "rep"),
            P("exp", None, "rep"),
            P("exp", None, "rep"),
        ),
        out_specs=P("exp", "rep"),
        check_vma=False,
    )
```

```python
import functools
import math

import jax
import jax.numpy as jnp
from jax import lax
from jax.experimental import pallas as pl
from jax.experimental.pallas import tpu as pltpu
from jax.sharding import PartitionSpec as P

EXPERTS = 128
F32 = jnp.float32
BF16 = jnp.bfloat16
VMEM_LIMIT = 56 * 2**20
VMEM_SPARE = 10 * 2**20
ALIGN = 16
META = 16


def ceil_to(value, unit):
    return -(-value // unit) * unit


def vmem():
    return pl.BlockSpec(memory_space=pltpu.VMEM)


def smem():
    return pl.BlockSpec(memory_space=pltpu.SMEM)


def hbm():
    return pl.BlockSpec(memory_space=pltpu.HBM)


def params(*shapes):
    need = sum(math.prod(s.shape) * jnp.dtype(s.dtype).itemsize for s in shapes if hasattr(s, "dtype"))
    return pltpu.CompilerParams(vmem_limit_bytes=min(VMEM_LIMIT, need + need // 4 + VMEM_SPARE))


def held(*arrays):
    return [jax.ShapeDtypeStruct(a.shape, a.dtype) for a in arrays]


def cost(flops, moved):
    return pl.CostEstimate(flops=int(flops), bytes_accessed=int(moved), transcendentals=0)


def pack_kernel(dims, tokens, ids, weights, packed):
    rows, top = dims["rows"], dims["top"]
    chance = weights[...]
    chance = chance / jnp.sum(chance, axis=0, keepdims=True)
    high = chance.astype(BF16)
    rest = chance - high.astype(F32)
    middle = rest.astype(BF16)
    low = (rest - middle.astype(F32)).astype(BF16)
    packed[:rows, :] = tokens[...]
    packed[rows:, :] = jnp.zeros((META, packed.shape[1]), BF16)
    parts = (ids[...].astype(F32), high.astype(F32), middle.astype(F32), low.astype(F32))
    for i, part in enumerate(parts):
        block = jnp.concatenate([part, jnp.zeros((META - top, rows), F32)], axis=0)
        packed[rows:, i * rows : (i + 1) * rows] = block.astype(BF16)


def pack(dims, tokens, ids, weights):
    return pl.pallas_call(
        functools.partial(pack_kernel, dims),
        out_shape=jax.ShapeDtypeStruct((dims["rows"] + META, tokens.shape[1]), BF16),
        in_specs=[vmem()] * 3,
        out_specs=vmem(),
        compiler_params=params(),
        name="pack",
    )(tokens, ids.T, weights.T)


def loop(count, body, carry):
    if count > 8:
        return lax.fori_loop(0, count, body, carry)
    for i in range(count):
        carry = body(i, carry)
    return carry


def route(dims, base, meta_of, rowid, probs, rowk):
    blocks, rows, top, experts = dims["blocks"], dims["rows"], dims["top"], dims["experts"]
    expert_at = lax.broadcasted_iota(jnp.int32, (experts, rows), 0) + base
    upper = (
        lax.broadcasted_iota(jnp.int32, (rows, rows), 0)
        <= lax.broadcasted_iota(jnp.int32, (rows, rows), 1)
    ).astype(BF16)

    def chosen_ids(block):
        return meta_of(block)[:, :rows].astype(F32)[:top].astype(jnp.int32)

    def count(block, seen):
        held = meta_of(block).astype(F32)[:top]
        ids = held[:, :rows].astype(jnp.int32)
        chance = held[:, rows : 2 * rows] + held[:, 2 * rows : 3 * rows]
        chance = chance + held[:, 3 * rows : 4 * rows]
        member = jnp.zeros((experts, rows), F32)
        share = jnp.zeros((experts, rows), F32)
        for k in range(top):
            hit = ids[k : k + 1, :] == expert_at
            member = member + hit.astype(F32)
            share = share + jnp.where(hit, chance[k : k + 1, :], 0.0)
        upto = jnp.dot(member.astype(BF16), upper, preferred_element_type=F32)
        rowid[block] = jnp.where(member > 0, seen + upto - 1.0, -1e6).astype(jnp.int32)
        probs[block] = share
        return seen + upto[:, rows - 1 : rows]

    total = loop(blocks, count, jnp.zeros((experts, rows), F32))
    starts, before = [], jnp.zeros((1, rows), F32)
    for e in range(experts):
        starts.append(before)
        before = before + total[e : e + 1, :]
    start = jnp.concatenate(starts, axis=0) if experts > 1 else starts[0]
    start, total = start.astype(jnp.int32), total.astype(jnp.int32)

    def place(block, carry):
        ids = chosen_ids(block)
        at = rowid[block] + start
        rowid[block] = at
        found = []
        for k in range(top):
            hit = ids[k : k + 1, :] == expert_at
            found.append(jnp.max(jnp.where(hit, at, -1), axis=0, keepdims=True))
        rowk[block] = jnp.concatenate(found, axis=0)
        return carry

    loop(blocks, place, 0)
    return start, total


def window_hits(dims, rowid, block, e, start):
    at = lax.broadcasted_iota(jnp.int32, (dims["window"], dims["rows"]), 0) + start
    return rowid[block, e : e + 1, :] == at


def aligned(dims, value):
    return pl.multiple_of(jnp.minimum(value // ALIGN * ALIGN, dims["total"]), ALIGN)


def fill_select(dims, rowid, starts, select, step):
    rows = dims["rows"]
    select[...] = jnp.zeros_like(select)
    for e in range(dims["experts"]):
        first = aligned(dims, starts[e])
        at = pl.ds(first, dims["window"])
        for inner in range(dims["group"]):
            cols = slice(inner * rows, (inner + 1) * rows)
            hit = window_hits(dims, rowid, step * dims["group"] + inner, e, first)
            select[at, cols] = select[at, cols] + hit.astype(F32).astype(BF16)


def publish(dims, offs, start, total):
    starts = [start[e, 0] for e in range(dims["experts"])]
    for e in range(dims["experts"]):
        offs[0, e] = starts[e]
        offs[1, e] = total[e, 0]
    return starts


def fullest(dims, meta):
    blocks, rows, top, experts = dims["blocks"], dims["rows"], dims["top"], dims["experts"]
    ids = [meta[b][:, :rows].astype(F32)[:top].astype(jnp.int32) for b in range(blocks)]
    counts = []
    for group in range(blocks):
        mine = jnp.zeros((top, rows), F32)
        for block_ids in ids:
            inside = (block_ids >= group * experts) & (block_ids < (group + 1) * experts)
            mine = mine + inside.astype(F32)
        counts.append(jnp.sum(mine, axis=0, keepdims=True))
    return jnp.max(jnp.sum(jnp.concatenate(counts, axis=0), axis=1, keepdims=True)).astype(jnp.int32)


def dispatch_kernel(dims, me_ref, gathered, rowid, probs, rowk, x, offs, select, total):
    blocks, rows, group, tile = dims["blocks"], dims["rows"], dims["group"], dims["tile"]
    start, count = route(
        dims, me_ref[1] * dims["experts"], lambda block: gathered[block, rows:, :], rowid, probs, rowk
    )
    starts = publish(dims, offs, start, count)
    total[...] = jnp.zeros_like(total)

    def body(step, carry):
        fill_select(dims, rowid, starts, select, step)
        part = gathered[pl.ds(step * group, group), :rows, :].reshape(group * rows, x.shape[1])
        for r in range(0, x.shape[0], tile):
            size = min(tile, x.shape[0] - r)
            got = jnp.dot(select[r : r + size, :], part, preferred_element_type=F32)
            got = got + total[r : r + size, :]
            total[r : r + size, :] = got
            x[r : r + size, :] = got.astype(BF16)
        return carry

    lax.fori_loop(0, blocks // group, body, 0)


def route_shapes(dims):
    blocks, rows, top, experts = dims["blocks"], dims["rows"], dims["top"], dims["experts"]
    return (
        jax.ShapeDtypeStruct((blocks, experts, rows), jnp.int32),
        jax.ShapeDtypeStruct((blocks, experts, rows), F32),
        jax.ShapeDtypeStruct((blocks, top, rows), jnp.int32),
    ), jax.ShapeDtypeStruct((2, experts), jnp.int32)


def dispatch(dims, me, gathered):
    shapes, offs = route_shapes(dims)
    width, padded = gathered.shape[2], dims["padded"]
    return pl.pallas_call(
        functools.partial(dispatch_kernel, dims),
        out_shape=shapes + (jax.ShapeDtypeStruct((padded, width), BF16), offs),
        in_specs=[smem(), vmem()],
        out_specs=(vmem(),) * 4 + (smem(),),
        scratch_shapes=[
            pltpu.VMEM((padded, dims["group"] * dims["rows"]), BF16),
            pltpu.VMEM((padded, width), F32),
        ],
        compiler_params=pltpu.CompilerParams(vmem_limit_bytes=VMEM_LIMIT),
        name="dispatch",
    )(me, gathered)


def choose(dims, rowk, block):
    at = lax.broadcasted_iota(jnp.int32, (dims["rows"], dims["total"]), 1)
    rows_of = rowk[block].astype(F32).T.astype(jnp.int32)
    hit = rows_of[:, 0:1] == at
    for k in range(1, dims["top"]):
        hit = hit | (rows_of[:, k : k + 1] == at)
    return hit.astype(F32).astype(BF16)


def weigh_small_kernel(dims, offs, select, probs, scale, chosen, table):
    rows, experts, total, blocks = dims["rows"], dims["experts"], dims["total"], dims["blocks"]
    same = lax.broadcasted_iota(jnp.int32, (rows, rows), 0) == lax.broadcasted_iota(
        jnp.int32, (rows, rows), 1
    )
    eye = same.astype(F32).astype(BF16)
    contract = (((1,), (1,)), ((), ()))
    for b in range(blocks):
        cols = slice(b * rows, (b + 1) * rows)
        picked = lax.dot_general(eye, select[:total, cols], contract, preferred_element_type=F32)
        chosen[b] = picked.astype(BF16)
        exact = probs[b]
        high = exact.astype(BF16)
        rest = exact - high.astype(F32)
        middle = rest.astype(BF16)
        low = (rest - middle.astype(F32)).astype(BF16)
        table[:, cols] = jnp.concatenate([high, middle, low], axis=0)
    wide = lax.dot_general(select[...], table[...], contract, preferred_element_type=F32)
    scale[:, : 3 * experts] = wide
    lane = lax.broadcasted_iota(jnp.int32, (dims["window"], scale.shape[1]), 1)
    for e in range(experts):
        first = aligned(dims, offs[0, e])
        at = pl.ds(first, dims["window"])
        old = scale[at, :]
        mine = (lane == e) | (lane == e + experts) | (lane == e + 2 * experts)
        found = jnp.sum(jnp.where(mine, old, 0.0), axis=1, keepdims=True)
        mask = row_mask(dims, first, offs, e)
        scale[at, :] = jnp.where(mask, jnp.broadcast_to(found, old.shape), old)


def weigh_large_kernel(dims, offs, rowid, probs, scale, chosen):
    chosen[...] = jnp.zeros_like(chosen)
    for e in range(dims["experts"]):
        first = aligned(dims, offs[0, e])
        at = pl.ds(first, dims["window"])

        def share(block, carry):
            hit = window_hits(dims, rowid, block, e, first)
            return carry + jnp.where(hit, probs[block, e : e + 1, :], 0.0)

        shares = loop(dims["blocks"], share, jnp.zeros((dims["window"], dims["rows"]), F32))
        wide = jnp.sum(shares, axis=1, keepdims=True)
        wide = jnp.broadcast_to(wide, (dims["window"], scale.shape[1]))
        scale[at, :] = jnp.where(row_mask(dims, first, offs, e), wide, scale[at, :])


def weigh(dims, offs, rows_of, probs):
    small = dims["small"]
    picked = (dims["blocks"], dims["rows"], dims["total"]) if small else (1, ALIGN, 128)
    outs = (
        jax.ShapeDtypeStruct((dims["padded"], 128), F32),
        jax.ShapeDtypeStruct(picked, BF16),
    )
    table = pltpu.VMEM((3 * dims["experts"], dims["blocks"] * dims["rows"]), BF16)
    return pl.pallas_call(
        functools.partial(weigh_small_kernel if small else weigh_large_kernel, dims),
        out_shape=outs,
        in_specs=[smem(), vmem(), vmem()],
        out_specs=(vmem(), vmem()),
        scratch_shapes=[table] if small else [],
        compiler_params=params(*outs, *held(rows_of, probs)),
        cost_estimate=cost(6e9, 8e6),
        name="weigh",
    )(offs, rows_of, probs)


def row_mask(dims, first, offs, e):
    at = lax.broadcasted_iota(jnp.int32, (dims["window"], 1), 0) + first
    begin = offs[0, e]
    return (at >= begin) & (at < begin + offs[1, e])


def batches(experts):
    return [range(b, min(b + 4, experts)) for b in range(0, experts, 4)]


def gate_up_kernel(dims, c, first_part, me_ref, *refs):
    experts, window, part, quarter = dims["experts"], dims["window"], dims["part"], dims["quarter"]
    if first_part:
        blocks, rows = dims["blocks"], dims["rows"]
        packed, refs = refs[:blocks], refs[blocks:]
        w_gate, w_up, rowid, probs, rowk, x, select, offs_out, peak, refs = *refs[:9], refs[9:]
        gx, uy, g2, u1, g0, u0, gate_w, up_w, gate, up, sems, table, meta = refs
    else:
        offs, x, w_gate, w_up, gx, uy, g2, u1, g0, u0, gate_w, up_w, gate, up, sems = refs
    units = pl.ds(c * part, part)

    def copies(e):
        return (
            pltpu.make_async_copy(w_gate.at[e, units, :], gate_w.at[e], sems.at[0, e]),
            pltpu.make_async_copy(w_up.at[e, units, :], up_w.at[e], sems.at[1, e]),
        )

    for e in range(experts):
        for copy in copies(e):
            copy.start()
    if first_part:
        for j, block in enumerate(packed):
            at = me_ref[1] ^ j
            table[pl.ds(pl.multiple_of(at * rows, rows), rows), :] = block[:rows, :]
            meta[at] = block[rows:, :]
        start, count = route(
            dims, me_ref[1] * experts, lambda block: meta[block], rowid, probs, rowk
        )
        offs = offs_out
        peak[0] = fullest(dims, meta)
        fill_select(dims, rowid, publish(dims, offs, start, count), select, 0)
        for r in range(0, x.shape[0], dims["tile"]):
            size = min(dims["tile"], x.shape[0] - r)
            got = jnp.dot(select[r : r + size, :], table[...], preferred_element_type=F32)
            x[r : r + size, :] = got.astype(BF16)
    contract = (((1,), (1,)), ((), ()))
    for batch in batches(experts):
        for e in batch:
            for copy in copies(e):
                copy.wait()
        for e in batch:
            first = aligned(dims, offs[0, e])
            rows_in = x[pl.ds(first, window), :]
            keep = (lax.broadcasted_iota(jnp.int32, (ALIGN, 1), 0) + first) >= offs[0, e]
            edge, rest = pl.ds(first, ALIGN), pl.ds(first + ALIGN, window - ALIGN)
            for held, into in ((gate_w, gate), (up_w, up)):
                got = lax.dot_general(rows_in, held[e], contract, preferred_element_type=F32)
                into[edge, :] = jnp.where(keep, got[:ALIGN], into[edge, :])
                into[rest, :] = got[ALIGN:]
    me = me_ref[0]

    def piece(total, j):
        return total[pl.ds(pl.multiple_of((me ^ j) * quarter, ALIGN), quarter), :]

    gx[0] = piece(gate, 1).astype(BF16)
    gx[1] = piece(gate, 3).astype(BF16)
    uy[0] = piece(up, 2).astype(BF16)
    uy[1] = piece(up, 3).astype(BF16)
    g2[...] = piece(gate, 2)
    u1[...] = piece(up, 1)
    g0[...] = piece(gate, 0)
    u0[...] = piece(up, 0)


def gate_up(dims, c, me, sources, w_gate, w_up):
    experts, part, quarter, padded = dims["experts"], dims["part"], dims["quarter"], dims["padded"]
    width = w_gate.shape[2]
    half = jax.ShapeDtypeStruct((2, quarter, part), BF16)
    own = jax.ShapeDtypeStruct((quarter, part), F32)
    first_part = len(sources) > 2
    outs = (half, half, own, own, own, own)
    scratch = [
        pltpu.VMEM((experts, part, width), BF16),
        pltpu.VMEM((experts, part, width), BF16),
        pltpu.VMEM((padded, part), F32),
        pltpu.VMEM((padded, part), F32),
        pltpu.SemaphoreType.DMA((2, experts)),
    ]
    into = (vmem(),) * len(outs)
    if first_part:
        blocks, rows = dims["blocks"], dims["rows"]
        shapes, offs = route_shapes(dims)
        x = jax.ShapeDtypeStruct((padded, width), BF16)
        select = jax.ShapeDtypeStruct((padded, blocks * rows), BF16)
        peak = jax.ShapeDtypeStruct((1,), jnp.int32)
        outs = shapes + (x, select, offs, peak) + outs
        into = (vmem(),) * 5 + (smem(),) * 2 + into
        scratch.append(pltpu.VMEM((blocks * rows, width), BF16))
        scratch.append(pltpu.VMEM((blocks, META, width), BF16))
        specs = [vmem()] * blocks
    else:
        specs = [smem(), vmem()]
    return pl.pallas_call(
        functools.partial(gate_up_kernel, dims, c, first_part),
        out_shape=outs,
        in_specs=[smem()] + specs + [hbm(), hbm()],
        out_specs=into,
        scratch_shapes=scratch,
        compiler_params=params(*outs, *held(*sources), *[b for b in scratch if "dma" not in str(b)]),
        cost_estimate=cost(4 * padded * width * part, 4 * experts * part * width + 2 * padded * width),
        name="gate_up",
    )(me, *sources, w_gate, w_up)


def gather_hidden(dims, me, pieces, hidden):
    quarter = dims["quarter"]
    for j, piece in zip((0, 3, 1, 2), pieces):
        hidden[pl.ds(pl.multiple_of((me ^ j) * quarter, ALIGN), quarter), :] = piece[...]


def down_kernel(dims, c, last, me_ref, offs, w_down, *refs):
    experts, window, part = dims["experts"], dims["window"], dims["part"]
    pieces, refs = refs[:4], refs[4:]
    y_in = None
    if c > 0:
        y_in, refs = refs[0], refs[1:]
    if last:
        scale, chosen, rowk, refs = refs[0], refs[1], refs[2], refs[3:]
        if dims["small"]:
            stay, away, held, hidden, sems, y_out = refs
        else:
            out, held, hidden, sems, y_out = refs
        y_out[...] = jnp.zeros_like(y_out)
    else:
        y_out, held, hidden, sems = refs
    units = pl.ds(c * part, part)

    def copy(e):
        return pltpu.make_async_copy(w_down.at[e, units, :], held.at[e], sems.at[e])

    for e in range(experts):
        copy(e).start()
    gather_hidden(dims, me_ref[0], pieces, hidden)
    for batch in batches(experts):
        for e in batch:
            copy(e).wait()
        for e in batch:
            first = aligned(dims, offs[0, e])
            at = pl.ds(first, window)
            got = jnp.dot(hidden[at, :], held[e], preferred_element_type=F32)
            if y_in is not None:
                got = got + y_in[at, :]
            mask = row_mask(dims, first, offs, e)
            if last:
                got = got * scale[at, 0:1]
                y_out[at, :] = jnp.where(mask, got, y_out[at, :].astype(F32)).astype(BF16)
            else:
                y_out[at, :] = jnp.where(mask, got, y_out[at, :])
    if not last:
        return
    rows, total, width = dims["rows"], dims["total"], w_down.shape[2]
    blocks, many = dims["blocks"], min(4, dims["blocks"])
    if dims["small"]:
        for side, into in enumerate((stay, away)):
            for p in range(0, blocks // 2, many):
                at = [me_ref[1] ^ (2 * (p + i) + side) for i in range(many)]
                picked = jnp.concatenate([chosen[i] for i in at], axis=0)
                summed = jnp.dot(picked, y_out[:total, :], preferred_element_type=F32)
                into[p : p + many] = summed.astype(BF16).reshape(many, rows, width)
        return

    def combine(step, carry):
        picked = [choose(dims, rowk, step * many + i) for i in range(many)]
        summed = jnp.dot(
            jnp.concatenate(picked, axis=0), y_out[:total, :], preferred_element_type=F32
        )
        out[pl.ds(step * many, many)] = summed.astype(BF16).reshape(many, rows, width)
        return carry

    lax.fori_loop(0, blocks // many, combine, 0)


def down(dims, c, last, me, offs, w_down, pieces, y, extra):
    experts, padded, part = dims["experts"], dims["padded"], dims["part"]
    width = w_down.shape[2]
    operands = list(pieces) + ([y] if c > 0 else []) + list(extra)
    blocks, rows = dims["blocks"], dims["rows"]
    scratch = [
        pltpu.VMEM((experts, part, width), BF16),
        pltpu.VMEM((padded, part), BF16),
        pltpu.SemaphoreType.DMA((experts,)),
    ]
    if not last:
        outs = (jax.ShapeDtypeStruct((padded, width), F32),)
    else:
        scratch.append(pltpu.VMEM((padded, width), BF16))
        if dims["small"]:
            outs = (jax.ShapeDtypeStruct((blocks // 2, rows, width), BF16),) * 2
        else:
            outs = (jax.ShapeDtypeStruct((blocks, rows, width), BF16),)
    return pl.pallas_call(
        functools.partial(down_kernel, dims, c, last),
        out_shape=outs,
        in_specs=[smem(), smem(), hbm()] + [vmem()] * len(operands),
        out_specs=(vmem(),) * len(outs),
        scratch_shapes=scratch,
        compiler_params=params(*outs, *held(*operands), *[b for b in scratch if "dma" not in str(b)]),
        cost_estimate=cost(4 * padded * width * part, 2 * experts * part * width + 8 * padded * width),
        name="down",
    )(me, offs, w_down, *operands)


def swap(value, axis, bit):
    count = lax.axis_size(axis)
    return lax.ppermute(value, axis, [(i, i ^ bit) for i in range(count)])


def reduce_chunk(came, kept):
    from_x, from_y = came
    g2, u1, g0, u0 = kept
    gate_rest = swap((g2 + from_x[1].astype(F32)).astype(BF16), "rep", 2)
    up_rest = swap((u1 + from_y[1].astype(F32)).astype(BF16), "rep", 1)
    gate = g0 + from_x[0].astype(F32) + gate_rest.astype(F32)
    up = u0 + from_y[0].astype(F32) + up_rest.astype(F32)
    return (jax.nn.silu(gate) * up).astype(BF16)


def spread_chunk(hidden):
    return [hidden] + [swap(hidden, "rep", bit) for bit in (3, 1, 2)]


def gather_tokens(tokens):
    held = {0: tokens}
    bit = lax.axis_size("exp") // 2
    while bit:
        for known in list(held):
            held[known | bit] = swap(held[known], "exp", bit)
        bit //= 2
    return [held[j] for j in range(len(held))]


def sum_over_exp(stay, away):
    total = stay.astype(F32) + swap(away, "exp", 1).astype(F32)
    came = [
        swap(total[i].astype(BF16), "exp", 2 * i) for i in range(total.shape[0] - 1, 0, -1)
    ]
    return (total[0] + sum(part.astype(F32) for part in came)).astype(BF16)


def local(tokens, expert_ids, route_weights, w_gate, w_up, w_down):
    rows, top = expert_ids.shape
    width = tokens.shape[1]
    experts, units, _ = w_gate.shape
    blocks = lax.axis_size("exp")
    replicas = lax.axis_size("rep")
    cap = replicas * max(1, rows * top * 3 // (8 * EXPERTS))
    total = ceil_to(experts * blocks * cap, replicas * 128)
    window = ceil_to(blocks * cap, ALIGN) + ALIGN
    part = units // 2
    small = blocks * rows * total <= 4 * 2**20

    def sizes(total):
        return dict(
            blocks=blocks,
            rows=rows,
            top=top,
            experts=experts,
            window=window,
            total=total,
            quarter=total // replicas,
            padded=total + window,
            part=part,
            group=min(blocks, 8),
            tile=512,
            small=small,
        )

    full = sizes(total)
    me = jnp.stack([lax.axis_index("rep"), lax.axis_index("exp")]).astype(jnp.int32)
    packed = pack(full, tokens, expert_ids, route_weights)
    weights = (w_gate, w_up, w_down)
    if not small:
        gathered = lax.all_gather(packed, "exp", axis=0)
        return one_pass(full, me, gathered, *weights)[0]
    sources = gather_tokens(packed)
    usual = min(total, ceil_to(rows * top * 5 // 4, replicas * 64))
    mixed, peak = one_pass(sizes(usual), me, sources, *weights)
    if usual == total:
        return mixed
    return lax.cond(
        peak[0] > usual, lambda: one_pass(full, me, sources, *weights)[0], lambda: mixed
    )


def one_pass(dims, me, sources, w_gate, w_up, w_down):
    peak = None
    if not dims["small"]:
        rowid, probs, rowk, x, offs = dispatch(dims, me, sources)
        rows_of, sources = rowid, [offs, x]
    parts = []
    for c in range(w_gate.shape[1] // dims["part"]):
        parts.append(gate_up(dims, c, me, sources, w_gate, w_up))
        if len(sources) > 2:
            rowid, probs, rowk, x, rows_of, offs, peak = parts[0][:7]
            sources, parts[0] = [offs, x], parts[0][7:]

    came = []
    for c, (gx, uy, *kept) in enumerate(parts):
        if c > 0:
            came[-1], gx, uy = lax.optimization_barrier((came[-1], gx, uy))
        came.append((swap(gx, "rep", 1), swap(uy, "rep", 2)))
        parts[c] = kept
    rows_of, _ = lax.optimization_barrier((rows_of, parts[-1]))
    scale, chosen = weigh(dims, offs, rows_of, probs)
    pieces = []
    for c, kept in enumerate(parts):
        hidden = reduce_chunk(came[c], kept)
        if c == 0:
            hidden, scale, chosen = lax.optimization_barrier((hidden, scale, chosen))
        pieces.append(spread_chunk(hidden))
    y = None
    last = len(pieces) - 1
    for c in range(last):
        y = down(dims, c, False, me, offs, w_down, pieces[c], y, ())[0]
    mixed = down(dims, last, True, me, offs, w_down, pieces[last], y, (scale, chosen, rowk))
    if dims["small"]:
        return sum_over_exp(*mixed), peak
    return lax.psum_scatter(mixed[0], "exp", scatter_dimension=0, tiled=False), peak


def solution(mesh):
    return jax.shard_map(
        local,
        mesh=mesh,
        in_specs=(
            P("exp", "rep"),
            P("exp", None),
            P("exp", None),
            P("exp", None, "rep"),
            P("exp", None, "rep"),
            P("exp", None, "rep"),
        ),
        out_specs=P("exp", "rep"),
        check_vma=False,
    )
```

```python
import functools
import math

import jax
import jax.numpy as jnp
from jax import lax
from jax.experimental import pallas as pl
from jax.experimental.pallas import tpu as pltpu
from jax.sharding import PartitionSpec as P

EXPERTS = 128
F32 = jnp.float32
BF16 = jnp.bfloat16
VMEM_LIMIT = 56 * 2**20
VMEM_SPARE = 10 * 2**20
ALIGN = 16
META = 16


def ceil_to(value, unit):
    return -(-value // unit) * unit


def vmem():
    return pl.BlockSpec(memory_space=pltpu.VMEM)


def smem():
    return pl.BlockSpec(memory_space=pltpu.SMEM)


def hbm():
    return pl.BlockSpec(memory_space=pltpu.HBM)


def params(*shapes):
    need = sum(math.prod(s.shape) * jnp.dtype(s.dtype).itemsize for s in shapes if hasattr(s, "dtype"))
    return pltpu.CompilerParams(vmem_limit_bytes=min(VMEM_LIMIT, need + need // 4 + VMEM_SPARE))


def held(*arrays):
    return [jax.ShapeDtypeStruct(a.shape, a.dtype) for a in arrays]


def cost(flops, moved):
    return pl.CostEstimate(flops=int(flops), bytes_accessed=int(moved), transcendentals=0)


def pack_kernel(dims, tokens, ids, weights, packed):
    rows, top = dims["rows"], dims["top"]
    chance = weights[...]
    chance = chance / jnp.sum(chance, axis=0, keepdims=True)
    high = chance.astype(BF16)
    rest = chance - high.astype(F32)
    middle = rest.astype(BF16)
    low = (rest - middle.astype(F32)).astype(BF16)
    packed[:rows, :] = tokens[...]
    packed[rows:, :] = jnp.zeros((META, packed.shape[1]), BF16)
    parts = (ids[...].astype(F32), high.astype(F32), middle.astype(F32), low.astype(F32))
    for i, part in enumerate(parts):
        block = jnp.concatenate([part, jnp.zeros((META - top, rows), F32)], axis=0)
        packed[rows:, i * rows : (i + 1) * rows] = block.astype(BF16)


def pack(dims, tokens, ids, weights):
    return pl.pallas_call(
        functools.partial(pack_kernel, dims),
        out_shape=jax.ShapeDtypeStruct((dims["rows"] + META, tokens.shape[1]), BF16),
        in_specs=[vmem()] * 3,
        out_specs=vmem(),
        compiler_params=params(),
        name="pack",
    )(tokens, ids.T, weights.T)


def loop(count, body, carry):
    if count > 8:
        return lax.fori_loop(0, count, body, carry)
    for i in range(count):
        carry = body(i, carry)
    return carry


def route(dims, base, meta_of, rowid, probs, rowk):
    blocks, rows, top, experts = dims["blocks"], dims["rows"], dims["top"], dims["experts"]
    expert_at = lax.broadcasted_iota(jnp.int32, (experts, rows), 0) + base
    upper = (
        lax.broadcasted_iota(jnp.int32, (rows, rows), 0)
        <= lax.broadcasted_iota(jnp.int32, (rows, rows), 1)
    ).astype(BF16)

    def chosen_ids(block):
        return meta_of(block)[:, :rows].astype(F32)[:top].astype(jnp.int32)

    def count(block, seen):
        held = meta_of(block).astype(F32)[:top]
        ids = held[:, :rows].astype(jnp.int32)
        chance = held[:, rows : 2 * rows] + held[:, 2 * rows : 3 * rows]
        chance = chance + held[:, 3 * rows : 4 * rows]
        member = jnp.zeros((experts, rows), F32)
        share = jnp.zeros((experts, rows), F32)
        for k in range(top):
            hit = ids[k : k + 1, :] == expert_at
            member = member + hit.astype(F32)
            share = share + jnp.where(hit, chance[k : k + 1, :], 0.0)
        upto = jnp.dot(member.astype(BF16), upper, preferred_element_type=F32)
        rowid[block] = jnp.where(member > 0, seen + upto - 1.0, -1e6).astype(jnp.int32)
        probs[block] = share
        return seen + upto[:, rows - 1 : rows]

    total = loop(blocks, count, jnp.zeros((experts, rows), F32))
    starts, before = [], jnp.zeros((1, rows), F32)
    for e in range(experts):
        starts.append(before)
        before = before + total[e : e + 1, :]
    start = jnp.concatenate(starts, axis=0) if experts > 1 else starts[0]
    start, total = start.astype(jnp.int32), total.astype(jnp.int32)

    def place(block, carry):
        ids = chosen_ids(block)
        at = rowid[block] + start
        rowid[block] = at
        found = []
        for k in range(top):
            hit = ids[k : k + 1, :] == expert_at
            found.append(jnp.max(jnp.where(hit, at, -1), axis=0, keepdims=True))
        rowk[block] = jnp.concatenate(found, axis=0)
        return carry

    loop(blocks, place, 0)
    return start, total


def window_hits(dims, rowid, block, e, start):
    at = lax.broadcasted_iota(jnp.int32, (dims["window"], dims["rows"]), 0) + start
    return rowid[block, e : e + 1, :] == at


def aligned(dims, value):
    return pl.multiple_of(jnp.minimum(value // ALIGN * ALIGN, dims["total"]), ALIGN)


def fill_select(dims, rowid, starts, select, step):
    rows = dims["rows"]
    select[...] = jnp.zeros_like(select)
    for e in range(dims["experts"]):
        first = aligned(dims, starts[e])
        at = pl.ds(first, dims["window"])
        for inner in range(dims["group"]):
            cols = slice(inner * rows, (inner + 1) * rows)
            hit = window_hits(dims, rowid, step * dims["group"] + inner, e, first)
            select[at, cols] = select[at, cols] + hit.astype(F32).astype(BF16)


def publish(dims, offs, start, total):
    starts = [start[e, 0] for e in range(dims["experts"])]
    for e in range(dims["experts"]):
        offs[0, e] = starts[e]
        offs[1, e] = total[e, 0]
    return starts


def fullest(dims, meta):
    blocks, rows, top, experts = dims["blocks"], dims["rows"], dims["top"], dims["experts"]
    ids = [meta[b][:, :rows].astype(F32)[:top].astype(jnp.int32) for b in range(blocks)]
    counts = []
    for group in range(blocks):
        mine = jnp.zeros((top, rows), F32)
        for block_ids in ids:
            inside = (block_ids >= group * experts) & (block_ids < (group + 1) * experts)
            mine = mine + inside.astype(F32)
        counts.append(jnp.sum(mine, axis=0, keepdims=True))
    return jnp.max(jnp.sum(jnp.concatenate(counts, axis=0), axis=1, keepdims=True)).astype(jnp.int32)


def dispatch_kernel(dims, me_ref, gathered, rowid, probs, rowk, x, offs, select, total):
    blocks, rows, group, tile = dims["blocks"], dims["rows"], dims["group"], dims["tile"]
    start, count = route(
        dims, me_ref[1] * dims["experts"], lambda block: gathered[block, rows:, :], rowid, probs, rowk
    )
    starts = publish(dims, offs, start, count)
    total[...] = jnp.zeros_like(total)

    def body(step, carry):
        fill_select(dims, rowid, starts, select, step)
        part = gathered[pl.ds(step * group, group), :rows, :].reshape(group * rows, x.shape[1])
        for r in range(0, x.shape[0], tile):
            size = min(tile, x.shape[0] - r)
            got = jnp.dot(select[r : r + size, :], part, preferred_element_type=F32)
            got = got + total[r : r + size, :]
            total[r : r + size, :] = got
            x[r : r + size, :] = got.astype(BF16)
        return carry

    lax.fori_loop(0, blocks // group, body, 0)


def route_shapes(dims):
    blocks, rows, top, experts = dims["blocks"], dims["rows"], dims["top"], dims["experts"]
    return (
        jax.ShapeDtypeStruct((blocks, experts, rows), jnp.int32),
        jax.ShapeDtypeStruct((blocks, experts, rows), F32),
        jax.ShapeDtypeStruct((blocks, top, rows), jnp.int32),
    ), jax.ShapeDtypeStruct((2, experts), jnp.int32)


def dispatch(dims, me, gathered):
    shapes, offs = route_shapes(dims)
    width, padded = gathered.shape[2], dims["padded"]
    return pl.pallas_call(
        functools.partial(dispatch_kernel, dims),
        out_shape=shapes + (jax.ShapeDtypeStruct((padded, width), BF16), offs),
        in_specs=[smem(), vmem()],
        out_specs=(vmem(),) * 4 + (smem(),),
        scratch_shapes=[
            pltpu.VMEM((padded, dims["group"] * dims["rows"]), BF16),
            pltpu.VMEM((padded, width), F32),
        ],
        compiler_params=pltpu.CompilerParams(vmem_limit_bytes=VMEM_LIMIT),
        name="dispatch",
    )(me, gathered)


def choose(dims, rowk, block):
    at = lax.broadcasted_iota(jnp.int32, (dims["rows"], dims["total"]), 1)
    rows_of = rowk[block].astype(F32).T.astype(jnp.int32)
    hit = rows_of[:, 0:1] == at
    for k in range(1, dims["top"]):
        hit = hit | (rows_of[:, k : k + 1] == at)
    return hit.astype(F32).astype(BF16)


def weigh_small_kernel(dims, offs, select, probs, meta, scale, chosen, peak, table):
    peak[0] = fullest(dims, meta)
    rows, experts, total, blocks = dims["rows"], dims["experts"], dims["total"], dims["blocks"]
    same = lax.broadcasted_iota(jnp.int32, (rows, rows), 0) == lax.broadcasted_iota(
        jnp.int32, (rows, rows), 1
    )
    eye = same.astype(F32).astype(BF16)
    contract = (((1,), (1,)), ((), ()))
    for b in range(blocks):
        cols = slice(b * rows, (b + 1) * rows)
        picked = lax.dot_general(eye, select[:total, cols], contract, preferred_element_type=F32)
        chosen[b] = picked.astype(BF16)
        exact = probs[b]
        high = exact.astype(BF16)
        rest = exact - high.astype(F32)
        middle = rest.astype(BF16)
        low = (rest - middle.astype(F32)).astype(BF16)
        table[:, cols] = jnp.concatenate([high, middle, low], axis=0)
    wide = lax.dot_general(select[...], table[...], contract, preferred_element_type=F32)
    scale[:, : 3 * experts] = wide
    lane = lax.broadcasted_iota(jnp.int32, (dims["window"], scale.shape[1]), 1)
    for e in range(experts):
        first = aligned(dims, offs[0, e])
        at = pl.ds(first, dims["window"])
        old = scale[at, :]
        mine = (lane == e) | (lane == e + experts) | (lane == e + 2 * experts)
        found = jnp.sum(jnp.where(mine, old, 0.0), axis=1, keepdims=True)
        mask = row_mask(dims, first, offs, e)
        scale[at, :] = jnp.where(mask, jnp.broadcast_to(found, old.shape), old)


def weigh_large_kernel(dims, offs, rowid, probs, scale, chosen):
    chosen[...] = jnp.zeros_like(chosen)
    for e in range(dims["experts"]):
        first = aligned(dims, offs[0, e])
        at = pl.ds(first, dims["window"])

        def share(block, carry):
            hit = window_hits(dims, rowid, block, e, first)
            return carry + jnp.where(hit, probs[block, e : e + 1, :], 0.0)

        shares = loop(dims["blocks"], share, jnp.zeros((dims["window"], dims["rows"]), F32))
        wide = jnp.sum(shares, axis=1, keepdims=True)
        wide = jnp.broadcast_to(wide, (dims["window"], scale.shape[1]))
        scale[at, :] = jnp.where(row_mask(dims, first, offs, e), wide, scale[at, :])


def weigh(dims, offs, rows_of, probs, meta):
    small = dims["small"]
    picked = (dims["blocks"], dims["rows"], dims["total"]) if small else (1, ALIGN, 128)
    outs = (
        jax.ShapeDtypeStruct((dims["padded"], 128), F32),
        jax.ShapeDtypeStruct(picked, BF16),
    )
    table = pltpu.VMEM((3 * dims["experts"], dims["blocks"] * dims["rows"]), BF16)
    operands = (rows_of, probs)
    if small:
        operands += (meta,)
        outs += (jax.ShapeDtypeStruct((1,), jnp.int32),)
    return pl.pallas_call(
        functools.partial(weigh_small_kernel if small else weigh_large_kernel, dims),
        out_shape=outs,
        in_specs=[smem()] + [vmem()] * len(operands),
        out_specs=(vmem(), vmem(), smem())[: len(outs)],
        scratch_shapes=[table] if small else [],
        compiler_params=params(*outs, *held(*operands)),
        cost_estimate=cost(6e9, 8e6),
        name="weigh",
    )(offs, *operands)


def row_mask(dims, first, offs, e):
    at = lax.broadcasted_iota(jnp.int32, (dims["window"], 1), 0) + first
    begin = offs[0, e]
    return (at >= begin) & (at < begin + offs[1, e])


def batches(experts):
    return [range(b, min(b + 4, experts)) for b in range(0, experts, 4)]


def gate_up_kernel(dims, c, first_part, me_ref, *refs):
    experts, window, part, quarter = dims["experts"], dims["window"], dims["part"], dims["quarter"]
    if first_part:
        blocks, rows = dims["blocks"], dims["rows"]
        packed, refs = refs[:blocks], refs[blocks:]
        w_gate, w_up, rowid, probs, rowk, x, select, offs_out, meta, refs = *refs[:9], refs[9:]
        gx, uy, g2, u1, g0, u0, gate_w, up_w, gate, up, sems, table = refs
    else:
        offs, x, w_gate, w_up, gx, uy, g2, u1, g0, u0, gate_w, up_w, gate, up, sems = refs
    units = pl.ds(c * part, part)

    def copies(e):
        return (
            pltpu.make_async_copy(w_gate.at[e, units, :], gate_w.at[e], sems.at[0, e]),
            pltpu.make_async_copy(w_up.at[e, units, :], up_w.at[e], sems.at[1, e]),
        )

    for e in range(experts):
        for copy in copies(e):
            copy.start()
    if first_part:
        for j, block in enumerate(packed):
            at = me_ref[1] ^ j
            table[pl.ds(pl.multiple_of(at * rows, rows), rows), :] = block[:rows, :]
            meta[at] = block[rows:, :]
        start, count = route(
            dims, me_ref[1] * experts, lambda block: meta[block], rowid, probs, rowk
        )
        offs = offs_out
        fill_select(dims, rowid, publish(dims, offs, start, count), select, 0)
        for r in range(0, x.shape[0], dims["tile"]):
            size = min(dims["tile"], x.shape[0] - r)
            got = jnp.dot(select[r : r + size, :], table[...], preferred_element_type=F32)
            x[r : r + size, :] = got.astype(BF16)
    contract = (((1,), (1,)), ((), ()))
    for batch in batches(experts):
        for e in batch:
            for copy in copies(e):
                copy.wait()
        for e in batch:
            first = aligned(dims, offs[0, e])
            rows_in = x[pl.ds(first, window), :]
            keep = (lax.broadcasted_iota(jnp.int32, (ALIGN, 1), 0) + first) >= offs[0, e]
            edge, rest = pl.ds(first, ALIGN), pl.ds(first + ALIGN, window - ALIGN)
            for held, into in ((gate_w, gate), (up_w, up)):
                got = lax.dot_general(rows_in, held[e], contract, preferred_element_type=F32)
                into[edge, :] = jnp.where(keep, got[:ALIGN], into[edge, :])
                into[rest, :] = got[ALIGN:]
    me = me_ref[0]

    def piece(total, j):
        return total[pl.ds(pl.multiple_of((me ^ j) * quarter, ALIGN), quarter), :]

    gx[0] = piece(gate, 1).astype(BF16)
    gx[1] = piece(gate, 3).astype(BF16)
    uy[0] = piece(up, 2).astype(BF16)
    uy[1] = piece(up, 3).astype(BF16)
    g2[...] = piece(gate, 2)
    u1[...] = piece(up, 1)
    g0[...] = piece(gate, 0)
    u0[...] = piece(up, 0)


def gate_up(dims, c, me, sources, w_gate, w_up):
    experts, part, quarter, padded = dims["experts"], dims["part"], dims["quarter"], dims["padded"]
    width = w_gate.shape[2]
    half = jax.ShapeDtypeStruct((2, quarter, part), BF16)
    own = jax.ShapeDtypeStruct((quarter, part), F32)
    first_part = len(sources) > 2
    outs = (half, half, own, own, own, own)
    scratch = [
        pltpu.VMEM((experts, part, width), BF16),
        pltpu.VMEM((experts, part, width), BF16),
        pltpu.VMEM((padded, part), F32),
        pltpu.VMEM((padded, part), F32),
        pltpu.SemaphoreType.DMA((2, experts)),
    ]
    into = (vmem(),) * len(outs)
    if first_part:
        blocks, rows = dims["blocks"], dims["rows"]
        shapes, offs = route_shapes(dims)
        x = jax.ShapeDtypeStruct((padded, width), BF16)
        select = jax.ShapeDtypeStruct((padded, blocks * rows), BF16)
        meta = jax.ShapeDtypeStruct((blocks, META, width), BF16)
        outs = shapes + (x, select, offs, meta) + outs
        into = (vmem(),) * 5 + (smem(), vmem()) + into
        scratch.append(pltpu.VMEM((blocks * rows, width), BF16))
        specs = [vmem()] * blocks
    else:
        specs = [smem(), vmem()]
    return pl.pallas_call(
        functools.partial(gate_up_kernel, dims, c, first_part),
        out_shape=outs,
        in_specs=[smem()] + specs + [hbm(), hbm()],
        out_specs=into,
        scratch_shapes=scratch,
        compiler_params=params(*outs, *held(*sources), *[b for b in scratch if "dma" not in str(b)]),
        cost_estimate=cost(4 * padded * width * part, 4 * experts * part * width + 2 * padded * width),
        name="gate_up",
    )(me, *sources, w_gate, w_up)


def down_kernel(dims, places, me_ref, offs, w_down, scale, chosen, rowk, *refs):
    experts, window, part, quarter = dims["experts"], dims["window"], dims["part"], dims["quarter"]
    pieces, refs = refs[: len(places)], refs[len(places) :]
    if dims["small"]:
        stay, away, hidden, scaled = refs
    else:
        out, hidden, scaled = refs
    scaled[...] = jnp.zeros_like(scaled)
    for (c, j, skip), piece in zip(places, pieces):
        first = pl.multiple_of((me_ref[0] ^ j) * quarter + skip, ALIGN)
        hidden[pl.ds(first, piece.shape[0]), c * part : (c + 1) * part] = piece[...]
    for e in range(experts):
        first = aligned(dims, offs[0, e])
        at = pl.ds(first, window)
        got = jnp.dot(hidden[at, :], w_down[e], preferred_element_type=F32) * scale[at, 0:1]
        mask = row_mask(dims, first, offs, e)
        scaled[at, :] = jnp.where(mask, got, scaled[at, :].astype(F32)).astype(BF16)
    rows, total, width = dims["rows"], dims["total"], w_down.shape[2]
    blocks, many = dims["blocks"], min(4, dims["blocks"])
    if dims["small"]:
        for side, into in enumerate((stay, away)):
            for p in range(0, blocks // 2, many):
                at = [me_ref[1] ^ (2 * (p + i) + side) for i in range(many)]
                picked = jnp.concatenate([chosen[i] for i in at], axis=0)
                summed = jnp.dot(picked, scaled[:total, :], preferred_element_type=F32)
                into[p : p + many] = summed.astype(BF16).reshape(many, rows, width)
        return

    def combine(step, carry):
        picked = [choose(dims, rowk, step * many + i) for i in range(many)]
        summed = jnp.dot(
            jnp.concatenate(picked, axis=0), scaled[:total, :], preferred_element_type=F32
        )
        out[pl.ds(step * many, many)] = summed.astype(BF16).reshape(many, rows, width)
        return carry

    lax.fori_loop(0, blocks // many, combine, 0)


def down(dims, me, offs, w_down, scale, chosen, rowk, chunks):
    padded, width = dims["padded"], w_down.shape[2]
    places = [(c, j, skip) for c, chunk in enumerate(chunks) for j, skip, _ in chunk]
    pieces = [piece for chunk in chunks for _, _, piece in chunk]
    operands = [w_down, scale, chosen, rowk, *pieces]
    blocks, rows = dims["blocks"], dims["rows"]
    scratch = [
        pltpu.VMEM((padded, w_down.shape[1]), BF16),
        pltpu.VMEM((padded, width), BF16),
    ]
    if dims["small"]:
        outs = (jax.ShapeDtypeStruct((blocks // 2, rows, width), BF16),) * 2
    else:
        outs = (jax.ShapeDtypeStruct((blocks, rows, width), BF16),)
    return pl.pallas_call(
        functools.partial(down_kernel, dims, places),
        out_shape=outs,
        in_specs=[smem(), smem()] + [vmem()] * len(operands),
        out_specs=(vmem(),) * len(outs),
        scratch_shapes=scratch,
        compiler_params=params(*outs, *held(*operands), *scratch),
        cost_estimate=cost(2 * padded * width * (w_down.shape[1] + blocks * rows), 2 * w_down.size),
        name="down",
    )(me, offs, *operands)


def swap(value, axis, bit):
    count = lax.axis_size(axis)
    return lax.ppermute(value, axis, [(i, i ^ bit) for i in range(count)])


def reduce_chunk(came, kept):
    from_x, from_y = came
    g2, u1, g0, u0 = kept
    gate_rest = swap((g2 + from_x[1].astype(F32)).astype(BF16), "rep", 2)
    up_rest = swap((u1 + from_y[1].astype(F32)).astype(BF16), "rep", 1)
    gate = g0 + from_x[0].astype(F32) + gate_rest.astype(F32)
    up = u0 + from_y[0].astype(F32) + up_rest.astype(F32)
    return (jax.nn.silu(gate) * up).astype(BF16)


def spread_chunk(hidden, two_steps):
    x, y = swap(hidden, "rep", 1), swap(hidden, "rep", 2)
    if two_steps:
        half = hidden.shape[0] // 2
        corner = [(3, 0, swap(x[:half], "rep", 2)), (3, half, swap(y[half:], "rep", 1))]
    else:
        corner = [(3, 0, swap(hidden, "rep", 3))]
    return [(0, 0, hidden), (1, 0, x), (2, 0, y)] + corner


def gather_tokens(tokens):
    held = {0: tokens}
    bit = lax.axis_size("exp") // 2
    while bit:
        for known in list(held):
            held[known | bit] = swap(held[known], "exp", bit)
        bit //= 2
    return [held[j] for j in range(len(held))]


def sum_over_exp(stay, away):
    total = stay.astype(F32) + swap(away, "exp", 1).astype(F32)
    came = [
        swap(total[i].astype(BF16), "exp", 2 * i) for i in range(total.shape[0] - 1, 0, -1)
    ]
    return (total[0] + sum(part.astype(F32) for part in came)).astype(BF16)


def local(tokens, expert_ids, route_weights, w_gate, w_up, w_down):
    rows, top = expert_ids.shape
    width = tokens.shape[1]
    experts, units, _ = w_gate.shape
    blocks = lax.axis_size("exp")
    replicas = lax.axis_size("rep")
    cap = replicas * max(1, rows * top * 3 // (8 * EXPERTS))
    total = ceil_to(experts * blocks * cap, replicas * 128)
    window = ceil_to(blocks * cap, ALIGN) + ALIGN
    part = units // 2
    small = blocks * rows * total <= 4 * 2**20

    def sizes(total):
        return dict(
            blocks=blocks,
            rows=rows,
            top=top,
            experts=experts,
            window=window,
            total=total,
            quarter=total // replicas,
            padded=total + window,
            part=part,
            group=min(blocks, 8),
            tile=512,
            small=small,
        )

    full = sizes(total)
    me = jnp.stack([lax.axis_index("rep"), lax.axis_index("exp")]).astype(jnp.int32)
    packed = pack(full, tokens, expert_ids, route_weights)
    weights = (w_gate, w_up, w_down)
    if not small:
        gathered = lax.all_gather(packed, "exp", axis=0)
        return one_pass(full, me, gathered, *weights)[0]
    sources = gather_tokens(packed)
    usual = min(total, ceil_to(rows * top * 5 // 4, replicas * 64))
    mixed, peak = one_pass(sizes(usual), me, sources, *weights)
    if usual == total:
        return mixed
    return lax.cond(
        peak[0] > usual, lambda: one_pass(full, me, sources, *weights)[0], lambda: mixed
    )


def one_pass(dims, me, sources, w_gate, w_up, w_down):
    meta = None
    if not dims["small"]:
        rowid, probs, rowk, x, offs = dispatch(dims, me, sources)
        rows_of, sources = rowid, [offs, x]
    parts = []
    for c in range(w_gate.shape[1] // dims["part"]):
        parts.append(gate_up(dims, c, me, sources, w_gate, w_up))
        if len(sources) > 2:
            rowid, probs, rowk, x, rows_of, offs, meta = parts[0][:7]
            sources, parts[0] = [offs, x], parts[0][7:]

    came = []
    for c, (gx, uy, *kept) in enumerate(parts):
        came.append((swap(gx, "rep", 1), swap(uy, "rep", 2)))
        parts[c] = kept
    rows_of, _ = lax.optimization_barrier((rows_of, parts[-1]))
    scale, chosen, *peak = weigh(dims, offs, rows_of, probs, meta)
    chunks = []
    for c, kept in enumerate(parts):
        hidden = reduce_chunk(came[c], kept)
        if c == 0:
            hidden, scale, chosen = lax.optimization_barrier((hidden, scale, chosen))
        chunks.append(spread_chunk(hidden, c + 1 < len(parts)))
    mixed = down(dims, me, offs, w_down, scale, chosen, rowk, chunks)
    if dims["small"]:
        return sum_over_exp(*mixed), peak[0]
    return lax.psum_scatter(mixed[0], "exp", scatter_dimension=0, tiled=False), None


def solution(mesh):
    return jax.shard_map(
        local,
        mesh=mesh,
        in_specs=(
            P("exp", "rep"),
            P("exp", None),
            P("exp", None),
            P("exp", None, "rep"),
            P("exp", None, "rep"),
            P("exp", None, "rep"),
        ),
        out_specs=P("exp", "rep"),
        check_vma=False,
    )
```

```python
import functools
import math

import jax
import jax.numpy as jnp
from jax import lax
from jax.experimental import pallas as pl
from jax.experimental.pallas import tpu as pltpu
from jax.sharding import PartitionSpec as P

EXPERTS = 128
F32 = jnp.float32
BF16 = jnp.bfloat16
VMEM_LIMIT = 56 * 2**20
VMEM_SPARE = 10 * 2**20
ALIGN = 16
META = 16


def ceil_to(value, unit):
    return -(-value // unit) * unit


def vmem():
    return pl.BlockSpec(memory_space=pltpu.VMEM)


def smem():
    return pl.BlockSpec(memory_space=pltpu.SMEM)


def hbm():
    return pl.BlockSpec(memory_space=pltpu.HBM)


def params(*shapes):
    need = sum(math.prod(s.shape) * jnp.dtype(s.dtype).itemsize for s in shapes if hasattr(s, "dtype"))
    return pltpu.CompilerParams(vmem_limit_bytes=min(VMEM_LIMIT, need + need // 4 + VMEM_SPARE))


def held(*arrays):
    return [jax.ShapeDtypeStruct(a.shape, a.dtype) for a in arrays]


def cost(flops, moved):
    return pl.CostEstimate(flops=int(flops), bytes_accessed=int(moved), transcendentals=0)


def pack_kernel(dims, tokens, routing, packed):
    rows, top = dims["rows"], dims["top"]
    chance = routing[top:, :]
    chance = chance / jnp.sum(chance, axis=0, keepdims=True)
    high = chance.astype(BF16)
    rest = chance - high.astype(F32)
    middle = rest.astype(BF16)
    low = (rest - middle.astype(F32)).astype(BF16)
    packed[:rows, :] = tokens[...]
    packed[rows:, :] = jnp.zeros((META, packed.shape[1]), BF16)
    parts = (routing[:top, :], high.astype(F32), middle.astype(F32), low.astype(F32))
    for i, part in enumerate(parts):
        block = jnp.concatenate([part, jnp.zeros((META - top, rows), F32)], axis=0)
        packed[rows:, i * rows : (i + 1) * rows] = block.astype(BF16)


def pack(dims, tokens, ids, weights):
    return pl.pallas_call(
        functools.partial(pack_kernel, dims),
        out_shape=jax.ShapeDtypeStruct((dims["rows"] + META, tokens.shape[1]), BF16),
        in_specs=[vmem()] * 2,
        out_specs=vmem(),
        compiler_params=params(),
        name="pack",
    )(tokens, jnp.concatenate([ids.T.astype(F32), weights.T], axis=0))


def loop(count, body, carry):
    if count > 8:
        return lax.fori_loop(0, count, body, carry)
    for i in range(count):
        carry = body(i, carry)
    return carry


def route(dims, base, meta_of, rowid, probs, rowk):
    blocks, rows, top, experts = dims["blocks"], dims["rows"], dims["top"], dims["experts"]
    expert_at = lax.broadcasted_iota(jnp.int32, (experts, rows), 0) + base
    upper = (
        lax.broadcasted_iota(jnp.int32, (rows, rows), 0)
        <= lax.broadcasted_iota(jnp.int32, (rows, rows), 1)
    ).astype(BF16)

    def chosen_ids(block):
        return meta_of(block)[:, :rows].astype(F32)[:top].astype(jnp.int32)

    def count(block, seen):
        held = meta_of(block).astype(F32)[:top]
        ids = held[:, :rows].astype(jnp.int32)
        chance = held[:, rows : 2 * rows] + held[:, 2 * rows : 3 * rows]
        chance = chance + held[:, 3 * rows : 4 * rows]
        member = jnp.zeros((experts, rows), F32)
        share = jnp.zeros((experts, rows), F32)
        for k in range(top):
            hit = ids[k : k + 1, :] == expert_at
            member = member + hit.astype(F32)
            share = share + jnp.where(hit, chance[k : k + 1, :], 0.0)
        upto = jnp.dot(member.astype(BF16), upper, preferred_element_type=F32)
        rowid[block] = jnp.where(member > 0, seen + upto - 1.0, -1e6).astype(jnp.int32)
        probs[block] = share
        return seen + upto[:, rows - 1 : rows]

    total = loop(blocks, count, jnp.zeros((experts, rows), F32))
    starts, before = [], jnp.zeros((1, rows), F32)
    for e in range(experts):
        starts.append(before)
        before = before + total[e : e + 1, :]
    start = jnp.concatenate(starts, axis=0) if experts > 1 else starts[0]
    start, before = start.astype(jnp.int32), before.astype(jnp.int32)

    def place(block, carry):
        ids = chosen_ids(block)
        at = rowid[block] + start
        rowid[block] = at
        found = []
        for k in range(top):
            hit = ids[k : k + 1, :] == expert_at
            found.append(jnp.max(jnp.where(hit, at, -1), axis=0, keepdims=True))
        rowk[block] = jnp.concatenate(found, axis=0)
        return carry

    loop(blocks, place, 0)
    return start, before


def window_hits(dims, rowid, block, e, start):
    at = lax.broadcasted_iota(jnp.int32, (dims["window"], dims["rows"]), 0) + start
    return rowid[block, e : e + 1, :] == at


def aligned(dims, value):
    return pl.multiple_of(jnp.minimum(value // ALIGN * ALIGN, dims["total"]), ALIGN)


def fill_select(dims, rowid, starts, select, step):
    rows = dims["rows"]
    select[...] = jnp.zeros_like(select)
    for e in range(dims["experts"]):
        first = aligned(dims, starts[e])
        at = pl.ds(first, dims["window"])
        for inner in range(dims["group"]):
            cols = slice(inner * rows, (inner + 1) * rows)
            hit = window_hits(dims, rowid, step * dims["group"] + inner, e, first)
            select[at, cols] = select[at, cols] + hit.astype(F32).astype(BF16)


def publish(dims, offs, start, end):
    starts = [start[e, 0] for e in range(dims["experts"])]
    for e in range(dims["experts"]):
        offs[0, e] = starts[e]
    offs[0, dims["experts"]] = end[0, 0]
    return starts


def fullest(dims, meta):
    blocks, rows, top, experts = dims["blocks"], dims["rows"], dims["top"], dims["experts"]
    ids = [meta[b][:, :rows].astype(F32)[:top].astype(jnp.int32) for b in range(blocks)]
    counts = []
    for group in range(blocks):
        mine = jnp.zeros((top, rows), F32)
        for block_ids in ids:
            inside = (block_ids >= group * experts) & (block_ids < (group + 1) * experts)
            mine = mine + inside.astype(F32)
        counts.append(jnp.sum(mine, axis=0, keepdims=True))
    return jnp.max(jnp.sum(jnp.concatenate(counts, axis=0), axis=1, keepdims=True)).astype(jnp.int32)


def dispatch_kernel(dims, me_ref, gathered, rowid, probs, rowk, x, offs, select, total):
    blocks, rows, group, tile = dims["blocks"], dims["rows"], dims["group"], dims["tile"]
    start, count = route(
        dims, me_ref[1] * dims["experts"], lambda block: gathered[block, rows:, :], rowid, probs, rowk
    )
    starts = publish(dims, offs, start, count)
    total[...] = jnp.zeros_like(total)

    def body(step, carry):
        fill_select(dims, rowid, starts, select, step)
        part = gathered[pl.ds(step * group, group), :rows, :].reshape(group * rows, x.shape[1])
        for r in range(0, x.shape[0], tile):
            size = min(tile, x.shape[0] - r)
            got = jnp.dot(select[r : r + size, :], part, preferred_element_type=F32)
            got = got + total[r : r + size, :]
            total[r : r + size, :] = got
            x[r : r + size, :] = got.astype(BF16)
        return carry

    lax.fori_loop(0, blocks // group, body, 0)


def route_shapes(dims):
    blocks, rows, top, experts = dims["blocks"], dims["rows"], dims["top"], dims["experts"]
    return (
        jax.ShapeDtypeStruct((blocks, experts, rows), jnp.int32),
        jax.ShapeDtypeStruct((blocks, experts, rows), F32),
        jax.ShapeDtypeStruct((blocks, top, rows), jnp.int32),
    ), jax.ShapeDtypeStruct((1, experts + 1), jnp.int32)


def dispatch(dims, me, gathered):
    shapes, offs = route_shapes(dims)
    width, padded = gathered.shape[2], dims["padded"]
    return pl.pallas_call(
        functools.partial(dispatch_kernel, dims),
        out_shape=shapes + (jax.ShapeDtypeStruct((padded, width), BF16), offs),
        in_specs=[smem(), vmem()],
        out_specs=(vmem(),) * 4 + (smem(),),
        scratch_shapes=[
            pltpu.VMEM((padded, dims["group"] * dims["rows"]), BF16),
            pltpu.VMEM((padded, width), F32),
        ],
        compiler_params=pltpu.CompilerParams(vmem_limit_bytes=VMEM_LIMIT),
        name="dispatch",
    )(me, gathered)


def choose(dims, rowk, block):
    at = lax.broadcasted_iota(jnp.int32, (dims["rows"], dims["total"]), 1)
    rows_of = rowk[block].astype(F32).T.astype(jnp.int32)
    hit = rows_of[:, 0:1] == at
    for k in range(1, dims["top"]):
        hit = hit | (rows_of[:, k : k + 1] == at)
    return hit.astype(F32).astype(BF16)


def weigh_small_kernel(dims, offs, select, probs, meta, scale, chosen, peak, table):
    peak[0] = fullest(dims, meta)
    rows, experts, total, blocks = dims["rows"], dims["experts"], dims["total"], dims["blocks"]
    same = lax.broadcasted_iota(jnp.int32, (rows, rows), 0) == lax.broadcasted_iota(
        jnp.int32, (rows, rows), 1
    )
    eye = same.astype(F32).astype(BF16)
    contract = (((1,), (1,)), ((), ()))
    for b in range(blocks):
        cols = slice(b * rows, (b + 1) * rows)
        picked = lax.dot_general(eye, select[:total, cols], contract, preferred_element_type=F32)
        chosen[b] = picked.astype(BF16)
        exact = probs[b]
        high = exact.astype(BF16)
        rest = exact - high.astype(F32)
        middle = rest.astype(BF16)
        low = (rest - middle.astype(F32)).astype(BF16)
        table[:, cols] = jnp.concatenate([high, middle, low], axis=0)
    wide = lax.dot_general(select[...], table[...], contract, preferred_element_type=F32)
    scale[:, : 3 * experts] = wide
    lane = lax.broadcasted_iota(jnp.int32, (dims["window"], scale.shape[1]), 1)
    for e in range(experts):
        first = aligned(dims, offs[0, e])
        at = pl.ds(first, dims["window"])
        old = scale[at, :]
        mine = (lane == e) | (lane == e + experts) | (lane == e + 2 * experts)
        found = jnp.sum(jnp.where(mine, old, 0.0), axis=1, keepdims=True)
        mask = row_mask(dims, first, offs, e)
        scale[at, :] = jnp.where(mask, jnp.broadcast_to(found, old.shape), old)


def weigh_large_kernel(dims, offs, rowid, probs, scale, chosen):
    chosen[...] = jnp.zeros_like(chosen)
    for e in range(dims["experts"]):
        first = aligned(dims, offs[0, e])
        at = pl.ds(first, dims["window"])

        def share(block, carry):
            hit = window_hits(dims, rowid, block, e, first)
            return carry + jnp.where(hit, probs[block, e : e + 1, :], 0.0)

        shares = loop(dims["blocks"], share, jnp.zeros((dims["window"], dims["rows"]), F32))
        wide = jnp.sum(shares, axis=1, keepdims=True)
        wide = jnp.broadcast_to(wide, (dims["window"], scale.shape[1]))
        scale[at, :] = jnp.where(row_mask(dims, first, offs, e), wide, scale[at, :])


def weigh(dims, offs, rows_of, probs, meta):
    small = dims["small"]
    picked = (dims["blocks"], dims["rows"], dims["total"]) if small else (1, ALIGN, 128)
    outs = (
        jax.ShapeDtypeStruct((dims["padded"], 128), F32),
        jax.ShapeDtypeStruct(picked, BF16),
    )
    table = pltpu.VMEM((3 * dims["experts"], dims["blocks"] * dims["rows"]), BF16)
    operands = (rows_of, probs)
    if small:
        operands += (meta,)
        outs += (jax.ShapeDtypeStruct((1,), jnp.int32),)
    return pl.pallas_call(
        functools.partial(weigh_small_kernel if small else weigh_large_kernel, dims),
        out_shape=outs,
        in_specs=[smem()] + [vmem()] * len(operands),
        out_specs=(vmem(), vmem(), smem())[: len(outs)],
        scratch_shapes=[table] if small else [],
        compiler_params=params(*outs, *held(*operands)),
        cost_estimate=cost(6e9, 8e6),
        name="weigh",
    )(offs, *operands)


def row_mask(dims, first, offs, e):
    at = lax.broadcasted_iota(jnp.int32, (dims["window"], 1), 0) + first
    return (at >= offs[0, e]) & (at < offs[0, e + 1])


def batches(experts):
    return [range(b, min(b + 4, experts)) for b in range(0, experts, 4)]


def gate_up_kernel(dims, c, first_part, me_ref, *refs):
    experts, window, part, quarter = dims["experts"], dims["window"], dims["part"], dims["quarter"]
    if first_part:
        blocks, rows = dims["blocks"], dims["rows"]
        packed, refs = refs[:blocks], refs[blocks:]
        w_gate, w_up, rowid, probs, rowk, x, select, offs_out, meta, refs = *refs[:9], refs[9:]
        gx, uy, g2, u1, g0, u0, weights, sums, sems, table = refs
    else:
        offs, x, w_gate, w_up, gx, uy, g2, u1, g0, u0, weights, sums, sems = refs
    units = pl.ds(c * part, part)

    def copies(e):
        return (
            pltpu.make_async_copy(w_gate.at[e, units, :], weights.at[e, pl.ds(0, part), :], sems.at[0, e]),
            pltpu.make_async_copy(w_up.at[e, units, :], weights.at[e, pl.ds(part, part), :], sems.at[1, e]),
        )

    for e in range(experts):
        for copy in copies(e):
            copy.start()
    if first_part:
        for j, block in enumerate(packed):
            at = me_ref[1] ^ j
            table[pl.ds(pl.multiple_of(at * rows, rows), rows), :] = block[:rows, :]
            meta[at] = block[rows:, :]
        start, count = route(
            dims, me_ref[1] * experts, lambda block: meta[block], rowid, probs, rowk
        )
        offs = offs_out
        fill_select(dims, rowid, publish(dims, offs, start, count), select, 0)
        for r in range(0, x.shape[0], dims["tile"]):
            size = min(dims["tile"], x.shape[0] - r)
            got = jnp.dot(select[r : r + size, :], table[...], preferred_element_type=F32)
            x[r : r + size, :] = got.astype(BF16)
    contract = (((1,), (1,)), ((), ()))
    for batch in batches(experts):
        for e in batch:
            for copy in copies(e):
                copy.wait()
        for e in batch:
            first = aligned(dims, offs[0, e])
            rows_in = x[pl.ds(first, window), :]
            keep = (lax.broadcasted_iota(jnp.int32, (ALIGN, 1), 0) + first) >= offs[0, e]
            edge, rest = pl.ds(first, ALIGN), pl.ds(first + ALIGN, window - ALIGN)
            got = lax.dot_general(rows_in, weights[e], contract, preferred_element_type=F32)
            sums[edge, :] = jnp.where(keep, got[:ALIGN], sums[edge, :])
            sums[rest, :] = got[ALIGN:]
    me = me_ref[0]

    gate, up = slice(0, part), slice(part, 2 * part)

    def piece(cols, j):
        return sums[pl.ds(pl.multiple_of((me ^ j) * quarter, ALIGN), quarter), cols]

    gx[0] = piece(gate, 1).astype(BF16)
    gx[1] = piece(gate, 3).astype(BF16)
    uy[0] = piece(up, 2).astype(BF16)
    uy[1] = piece(up, 3).astype(BF16)
    g2[...] = piece(gate, 2)
    u1[...] = piece(up, 1)
    g0[...] = piece(gate, 0)
    u0[...] = piece(up, 0)


def gate_up(dims, c, me, sources, w_gate, w_up):
    experts, part, quarter, padded = dims["experts"], dims["part"], dims["quarter"], dims["padded"]
    width = w_gate.shape[2]
    half = jax.ShapeDtypeStruct((2, quarter, part), BF16)
    own = jax.ShapeDtypeStruct((quarter, part), F32)
    first_part = len(sources) > 2
    outs = (half, half, own, own, own, own)
    scratch = [
        pltpu.VMEM((experts, 2 * part, width), BF16),
        pltpu.VMEM((padded, 2 * part), F32),
        pltpu.SemaphoreType.DMA((2, experts)),
    ]
    into = (vmem(),) * len(outs)
    if first_part:
        blocks, rows = dims["blocks"], dims["rows"]
        shapes, offs = route_shapes(dims)
        x = jax.ShapeDtypeStruct((padded, width), BF16)
        select = jax.ShapeDtypeStruct((padded, blocks * rows), BF16)
        meta = jax.ShapeDtypeStruct((blocks, META, width), BF16)
        outs = shapes + (x, select, offs, meta) + outs
        into = (vmem(),) * 5 + (smem(), vmem()) + into
        scratch.append(pltpu.VMEM((blocks * rows, width), BF16))
        specs = [vmem()] * blocks
    else:
        specs = [smem(), vmem()]
    return pl.pallas_call(
        functools.partial(gate_up_kernel, dims, c, first_part),
        out_shape=outs,
        in_specs=[smem()] + specs + [hbm(), hbm()],
        out_specs=into,
        scratch_shapes=scratch,
        compiler_params=params(*outs, *held(*sources), *[b for b in scratch if "dma" not in str(b)]),
        cost_estimate=cost(4 * padded * width * part, 4 * experts * part * width + 2 * padded * width),
        name="gate_up",
    )(me, *sources, w_gate, w_up)


def down_kernel(dims, places, me_ref, offs, w_down, scale, chosen, rowk, *refs):
    experts, window, part, quarter = dims["experts"], dims["window"], dims["part"], dims["quarter"]
    pieces, refs = refs[: len(places)], refs[len(places) :]
    if dims["small"]:
        stay, away, hidden, scaled = refs
    else:
        out, hidden, scaled = refs
    scaled[...] = jnp.zeros_like(scaled)
    for (c, j, skip), piece in zip(places, pieces):
        first = pl.multiple_of((me_ref[0] ^ j) * quarter + skip, ALIGN)
        hidden[pl.ds(first, piece.shape[0]), c * part : (c + 1) * part] = piece[...]
    for e in range(experts):
        first = aligned(dims, offs[0, e])
        at = pl.ds(first, window)
        got = jnp.dot(hidden[at, :], w_down[e], preferred_element_type=F32) * scale[at, 0:1]
        mask = row_mask(dims, first, offs, e)
        scaled[at, :] = jnp.where(mask, got, scaled[at, :].astype(F32)).astype(BF16)
    rows, total, width = dims["rows"], dims["total"], w_down.shape[2]
    blocks, many = dims["blocks"], min(4, dims["blocks"])
    if dims["small"]:
        for side, into in enumerate((stay, away)):
            for p in range(0, blocks // 2, many):
                at = [me_ref[1] ^ (2 * (p + i) + side) for i in range(many)]
                picked = jnp.concatenate([chosen[i] for i in at], axis=0)
                summed = jnp.dot(picked, scaled[:total, :], preferred_element_type=F32)
                into[p : p + many] = summed.astype(BF16).reshape(many, rows, width)
        return

    def combine(step, carry):
        picked = [choose(dims, rowk, step * many + i) for i in range(many)]
        summed = jnp.dot(
            jnp.concatenate(picked, axis=0), scaled[:total, :], preferred_element_type=F32
        )
        out[pl.ds(step * many, many)] = summed.astype(BF16).reshape(many, rows, width)
        return carry

    lax.fori_loop(0, blocks // many, combine, 0)


def down(dims, me, offs, w_down, scale, chosen, rowk, chunks):
    padded, width = dims["padded"], w_down.shape[2]
    places = [(c, j, skip) for c, chunk in enumerate(chunks) for j, skip, _ in chunk]
    pieces = [piece for chunk in chunks for _, _, piece in chunk]
    operands = [w_down, scale, chosen, rowk, *pieces]
    blocks, rows = dims["blocks"], dims["rows"]
    scratch = [
        pltpu.VMEM((padded, w_down.shape[1]), BF16),
        pltpu.VMEM((padded, width), BF16),
    ]
    if dims["small"]:
        outs = (jax.ShapeDtypeStruct((blocks // 2, rows, width), BF16),) * 2
    else:
        outs = (jax.ShapeDtypeStruct((blocks, rows, width), BF16),)
    return pl.pallas_call(
        functools.partial(down_kernel, dims, places),
        out_shape=outs,
        in_specs=[smem(), smem()] + [vmem()] * len(operands),
        out_specs=(vmem(),) * len(outs),
        scratch_shapes=scratch,
        compiler_params=params(*outs, *held(*operands), *scratch),
        cost_estimate=cost(2 * padded * width * (w_down.shape[1] + blocks * rows), 2 * w_down.size),
        name="down",
    )(me, offs, *operands)


def swap(value, axis, bit):
    count = lax.axis_size(axis)
    return lax.ppermute(value, axis, [(i, i ^ bit) for i in range(count)])


def reduce_chunk(came, kept):
    from_x, from_y = came
    g2, u1, g0, u0 = kept
    gate_rest = swap((g2 + from_x[1].astype(F32)).astype(BF16), "rep", 2)
    up_rest = swap((u1 + from_y[1].astype(F32)).astype(BF16), "rep", 1)
    gate = g0 + from_x[0].astype(F32) + gate_rest.astype(F32)
    up = u0 + from_y[0].astype(F32) + up_rest.astype(F32)
    return (jax.nn.silu(gate) * up).astype(BF16)


def spread_chunk(hidden, two_steps):
    x, y = swap(hidden, "rep", 1), swap(hidden, "rep", 2)
    if two_steps:
        half = hidden.shape[0] // 2
        corner = [(3, 0, swap(x[:half], "rep", 2)), (3, half, swap(y[half:], "rep", 1))]
    else:
        corner = [(3, 0, swap(hidden, "rep", 3))]
    return [(0, 0, hidden), (1, 0, x), (2, 0, y)] + corner


def gather_tokens(tokens):
    held = {0: tokens}
    bit = lax.axis_size("exp") // 2
    while bit:
        for known in list(held):
            held[known | bit] = swap(held[known], "exp", bit)
        bit //= 2
    return [held[j] for j in range(len(held))]


def sum_over_exp(stay, away):
    total = stay.astype(F32) + swap(away, "exp", 1).astype(F32)
    came = [
        swap(total[i].astype(BF16), "exp", 2 * i) for i in range(total.shape[0] - 1, 0, -1)
    ]
    return (total[0] + sum(part.astype(F32) for part in came)).astype(BF16)


def local(tokens, expert_ids, route_weights, w_gate, w_up, w_down):
    rows, top = expert_ids.shape
    width = tokens.shape[1]
    experts, units, _ = w_gate.shape
    blocks = lax.axis_size("exp")
    replicas = lax.axis_size("rep")
    cap = replicas * max(1, rows * top * 3 // (8 * EXPERTS))
    total = ceil_to(experts * blocks * cap, replicas * 128)
    window = ceil_to(blocks * cap, ALIGN) + ALIGN
    part = units // 2
    small = blocks * rows * total <= 4 * 2**20

    def sizes(total):
        return dict(
            blocks=blocks,
            rows=rows,
            top=top,
            experts=experts,
            window=window,
            total=total,
            quarter=total // replicas,
            padded=total + window,
            part=part,
            group=min(blocks, 8),
            tile=512,
            small=small,
        )

    full = sizes(total)
    me = jnp.stack([lax.axis_index("rep"), lax.axis_index("exp")]).astype(jnp.int32)
    packed = pack(full, tokens, expert_ids, route_weights)
    weights = (w_gate, w_up, w_down)
    if not small:
        gathered = lax.all_gather(packed, "exp", axis=0)
        return one_pass(full, me, gathered, *weights)[0]
    sources = gather_tokens(packed)
    usual = min(total, ceil_to(rows * top * 5 // 4, replicas * 64))
    mixed, peak = one_pass(sizes(usual), me, sources, *weights)
    if usual == total:
        return mixed
    return lax.cond(
        peak[0] > usual, lambda: one_pass(full, me, sources, *weights)[0], lambda: mixed
    )


def one_pass(dims, me, sources, w_gate, w_up, w_down):
    meta = None
    if not dims["small"]:
        rowid, probs, rowk, x, offs = dispatch(dims, me, sources)
        rows_of, sources = rowid, [offs, x]
    parts = []
    for c in range(w_gate.shape[1] // dims["part"]):
        parts.append(gate_up(dims, c, me, sources, w_gate, w_up))
        if len(sources) > 2:
            rowid, probs, rowk, x, rows_of, offs, meta = parts[0][:7]
            sources, parts[0] = [offs, x], parts[0][7:]

    came = []
    for c, (gx, uy, *kept) in enumerate(parts):
        came.append((swap(gx, "rep", 1), swap(uy, "rep", 2)))
        parts[c] = kept
    rows_of, _ = lax.optimization_barrier((rows_of, parts[-1]))
    scale, chosen, *peak = weigh(dims, offs, rows_of, probs, meta)
    chunks = []
    for c, kept in enumerate(parts):
        hidden = reduce_chunk(came[c], kept)
        if c == 0:
            hidden, scale, chosen = lax.optimization_barrier((hidden, scale, chosen))
        chunks.append(spread_chunk(hidden, c + 1 < len(parts)))
    mixed = down(dims, me, offs, w_down, scale, chosen, rowk, chunks)
    if dims["small"]:
        return sum_over_exp(*mixed), peak[0]
    return lax.psum_scatter(mixed[0], "exp", scatter_dimension=0, tiled=False), None


def solution(mesh):
    return jax.shard_map(
        local,
        mesh=mesh,
        in_specs=(
            P("exp", "rep"),
            P("exp", None),
            P("exp", None),
            P("exp", None, "rep"),
            P("exp", None, "rep"),
            P("exp", None, "rep"),
        ),
        out_specs=P("exp", "rep"),
        check_vma=False,
    )
```

```python
import functools
import math

import jax
import jax.numpy as jnp
from jax import lax
from jax.experimental import pallas as pl
from jax.experimental.pallas import tpu as pltpu
from jax.sharding import PartitionSpec as P

EXPERTS = 128
F32 = jnp.float32
BF16 = jnp.bfloat16
VMEM_LIMIT = 56 * 2**20
VMEM_SPARE = 10 * 2**20
PACK_VMEM = 64 * 2**20
ALIGN = 16
META = 16


def ceil_to(value, unit):
    return -(-value // unit) * unit


def vmem():
    return pl.BlockSpec(memory_space=pltpu.VMEM)


def smem():
    return pl.BlockSpec(memory_space=pltpu.SMEM)


def hbm():
    return pl.BlockSpec(memory_space=pltpu.HBM)


def params(*shapes):
    need = sum(math.prod(s.shape) * jnp.dtype(s.dtype).itemsize for s in shapes if hasattr(s, "dtype"))
    return pltpu.CompilerParams(vmem_limit_bytes=min(VMEM_LIMIT, need + need // 4 + VMEM_SPARE))


def held(*arrays):
    return [jax.ShapeDtypeStruct(a.shape, a.dtype) for a in arrays]


def cost(flops, moved):
    return pl.CostEstimate(flops=int(flops), bytes_accessed=int(moved), transcendentals=0)


def pack_kernel(dims, tokens, ids_in, weights_in, packed, ids, weights, sems):
    rows, top = dims["rows"], dims["top"]
    copies = [
        pltpu.make_async_copy(ids_in, ids, sems.at[0]),
        pltpu.make_async_copy(weights_in, weights, sems.at[1]),
        pltpu.make_async_copy(tokens, packed.at[pl.ds(0, rows), :], sems.at[2]),
    ]
    for copy in copies:
        copy.start()
    for copy in copies[:2]:
        copy.wait()
    chance = weights[...]
    chance = chance / jnp.sum(chance, axis=0, keepdims=True)
    high = chance.astype(BF16)
    rest = chance - high.astype(F32)
    middle = rest.astype(BF16)
    low = (rest - middle.astype(F32)).astype(BF16)
    packed[rows:, :] = jnp.zeros((META, packed.shape[1]), BF16)
    parts = (ids[...].astype(F32), high.astype(F32), middle.astype(F32), low.astype(F32))
    for i, part in enumerate(parts):
        block = jnp.concatenate([part, jnp.zeros((META - top, rows), F32)], axis=0)
        packed[rows:, i * rows : (i + 1) * rows] = block.astype(BF16)
    copies[2].wait()


def pack(dims, tokens, ids, weights):
    return pl.pallas_call(
        functools.partial(pack_kernel, dims),
        out_shape=jax.ShapeDtypeStruct((dims["rows"] + META, tokens.shape[1]), BF16),
        in_specs=[hbm()] * 3,
        out_specs=vmem(),
        scratch_shapes=[
            pltpu.VMEM(ids.T.shape, jnp.int32),
            pltpu.VMEM(weights.T.shape, F32),
            pltpu.SemaphoreType.DMA((3,)),
        ],
        compiler_params=pltpu.CompilerParams(vmem_limit_bytes=PACK_VMEM),
        name="pack",
    )(tokens, ids.T, weights.T)


def loop(count, body, carry):
    if count > 8:
        return lax.fori_loop(0, count, body, carry)
    for i in range(count):
        carry = body(i, carry)
    return carry


def route(dims, base, meta_of, rowid, probs, rowk):
    blocks, rows, top, experts = dims["blocks"], dims["rows"], dims["top"], dims["experts"]
    expert_at = lax.broadcasted_iota(jnp.int32, (experts, rows), 0) + base
    upper = (
        lax.broadcasted_iota(jnp.int32, (rows, rows), 0)
        <= lax.broadcasted_iota(jnp.int32, (rows, rows), 1)
    ).astype(BF16)

    def chosen_ids(block):
        return meta_of(block)[:, :rows].astype(F32)[:top].astype(jnp.int32)

    def count(block, seen):
        held = meta_of(block).astype(F32)[:top]
        ids = held[:, :rows].astype(jnp.int32)
        chance = held[:, rows : 2 * rows] + held[:, 2 * rows : 3 * rows]
        chance = chance + held[:, 3 * rows : 4 * rows]
        member = jnp.zeros((experts, rows), F32)
        share = jnp.zeros((experts, rows), F32)
        for k in range(top):
            hit = ids[k : k + 1, :] == expert_at
            member = member + hit.astype(F32)
            share = share + jnp.where(hit, chance[k : k + 1, :], 0.0)
        upto = jnp.dot(member.astype(BF16), upper, preferred_element_type=F32)
        rowid[block] = jnp.where(member > 0, seen + upto - 1.0, -1e6).astype(jnp.int32)
        probs[block] = share
        return seen + upto[:, rows - 1 : rows]

    total = loop(blocks, count, jnp.zeros((experts, rows), F32))
    starts, before = [], jnp.zeros((1, rows), F32)
    for e in range(experts):
        starts.append(before)
        before = before + total[e : e + 1, :]
    start = jnp.concatenate(starts, axis=0) if experts > 1 else starts[0]
    start, total = start.astype(jnp.int32), total.astype(jnp.int32)

    def place(block, carry):
        ids = chosen_ids(block)
        at = rowid[block] + start
        rowid[block] = at
        found = []
        for k in range(top):
            hit = ids[k : k + 1, :] == expert_at
            found.append(jnp.max(jnp.where(hit, at, -1), axis=0, keepdims=True))
        rowk[block] = jnp.concatenate(found, axis=0)
        return carry

    loop(blocks, place, 0)
    return start, total


def window_hits(dims, rowid, block, e, start):
    at = lax.broadcasted_iota(jnp.int32, (dims["window"], dims["rows"]), 0) + start
    return rowid[block, e : e + 1, :] == at


def aligned(dims, value):
    return pl.multiple_of(jnp.minimum(value // ALIGN * ALIGN, dims["total"]), ALIGN)


def fill_select(dims, rowid, starts, select, step):
    rows = dims["rows"]
    select[...] = jnp.zeros_like(select)
    for e in range(dims["experts"]):
        first = aligned(dims, starts[e])
        at = pl.ds(first, dims["window"])
        for inner in range(dims["group"]):
            cols = slice(inner * rows, (inner + 1) * rows)
            hit = window_hits(dims, rowid, step * dims["group"] + inner, e, first)
            select[at, cols] = select[at, cols] + hit.astype(F32).astype(BF16)


def publish(dims, offs, start, total):
    starts = [start[e, 0] for e in range(dims["experts"])]
    for e in range(dims["experts"]):
        offs[0, e] = starts[e]
        offs[1, e] = total[e, 0]
    return starts


def fullest(dims, meta):
    blocks, rows, top, experts = dims["blocks"], dims["rows"], dims["top"], dims["experts"]
    ids = [meta[b][:, :rows].astype(F32)[:top].astype(jnp.int32) for b in range(blocks)]
    counts = []
    for group in range(blocks):
        mine = jnp.zeros((top, rows), F32)
        for block_ids in ids:
            inside = (block_ids >= group * experts) & (block_ids < (group + 1) * experts)
            mine = mine + inside.astype(F32)
        counts.append(jnp.sum(mine, axis=0, keepdims=True))
    return jnp.max(jnp.sum(jnp.concatenate(counts, axis=0), axis=1, keepdims=True)).astype(jnp.int32)


def dispatch_kernel(dims, me_ref, gathered, rowid, probs, rowk, x, offs, select, total):
    blocks, rows, group, tile = dims["blocks"], dims["rows"], dims["group"], dims["tile"]
    start, count = route(
        dims, me_ref[1] * dims["experts"], lambda block: gathered[block, rows:, :], rowid, probs, rowk
    )
    starts = publish(dims, offs, start, count)
    total[...] = jnp.zeros_like(total)

    def body(step, carry):
        fill_select(dims, rowid, starts, select, step)
        part = gathered[pl.ds(step * group, group), :rows, :].reshape(group * rows, x.shape[1])
        for r in range(0, x.shape[0], tile):
            size = min(tile, x.shape[0] - r)
            got = jnp.dot(select[r : r + size, :], part, preferred_element_type=F32)
            got = got + total[r : r + size, :]
            total[r : r + size, :] = got
            x[r : r + size, :] = got.astype(BF16)
        return carry

    lax.fori_loop(0, blocks // group, body, 0)


def route_shapes(dims):
    blocks, rows, top, experts = dims["blocks"], dims["rows"], dims["top"], dims["experts"]
    return (
        jax.ShapeDtypeStruct((blocks, experts, rows), jnp.int32),
        jax.ShapeDtypeStruct((blocks, experts, rows), F32),
        jax.ShapeDtypeStruct((blocks, top, rows), jnp.int32),
    ), jax.ShapeDtypeStruct((2, experts), jnp.int32)


def dispatch(dims, me, gathered):
    shapes, offs = route_shapes(dims)
    width, padded = gathered.shape[2], dims["padded"]
    return pl.pallas_call(
        functools.partial(dispatch_kernel, dims),
        out_shape=shapes + (jax.ShapeDtypeStruct((padded, width), BF16), offs),
        in_specs=[smem(), vmem()],
        out_specs=(vmem(),) * 4 + (smem(),),
        scratch_shapes=[
            pltpu.VMEM((padded, dims["group"] * dims["rows"]), BF16),
            pltpu.VMEM((padded, width), F32),
        ],
        compiler_params=pltpu.CompilerParams(vmem_limit_bytes=VMEM_LIMIT),
        name="dispatch",
    )(me, gathered)


def choose(dims, rowk, block):
    at = lax.broadcasted_iota(jnp.int32, (dims["rows"], dims["total"]), 1)
    rows_of = rowk[block].astype(F32).T.astype(jnp.int32)
    hit = rows_of[:, 0:1] == at
    for k in range(1, dims["top"]):
        hit = hit | (rows_of[:, k : k + 1] == at)
    return hit.astype(F32).astype(BF16)


def weigh_small_kernel(dims, offs, select, probs, meta, scale, chosen, peak, table):
    peak[0] = fullest(dims, meta)
    rows, experts, total, blocks = dims["rows"], dims["experts"], dims["total"], dims["blocks"]
    same = lax.broadcasted_iota(jnp.int32, (rows, rows), 0) == lax.broadcasted_iota(
        jnp.int32, (rows, rows), 1
    )
    eye = same.astype(F32).astype(BF16)
    contract = (((1,), (1,)), ((), ()))
    for b in range(blocks):
        cols = slice(b * rows, (b + 1) * rows)
        picked = lax.dot_general(eye, select[:total, cols], contract, preferred_element_type=F32)
        chosen[b] = picked.astype(BF16)
        exact = probs[b]
        high = exact.astype(BF16)
        rest = exact - high.astype(F32)
        middle = rest.astype(BF16)
        low = (rest - middle.astype(F32)).astype(BF16)
        table[:, cols] = jnp.concatenate([high, middle, low], axis=0)
    wide = lax.dot_general(select[...], table[...], contract, preferred_element_type=F32)
    scale[:, : 3 * experts] = wide
    lane = lax.broadcasted_iota(jnp.int32, (dims["window"], scale.shape[1]), 1)
    for e in range(experts):
        first = aligned(dims, offs[0, e])
        at = pl.ds(first, dims["window"])
        old = scale[at, :]
        mine = (lane == e) | (lane == e + experts) | (lane == e + 2 * experts)
        found = jnp.sum(jnp.where(mine, old, 0.0), axis=1, keepdims=True)
        mask = row_mask(dims, first, offs, e)
        scale[at, :] = jnp.where(mask, jnp.broadcast_to(found, old.shape), old)


def weigh_large_kernel(dims, offs, rowid, probs, scale, chosen):
    chosen[...] = jnp.zeros_like(chosen)
    for e in range(dims["experts"]):
        first = aligned(dims, offs[0, e])
        at = pl.ds(first, dims["window"])

        def share(block, carry):
            hit = window_hits(dims, rowid, block, e, first)
            return carry + jnp.where(hit, probs[block, e : e + 1, :], 0.0)

        shares = loop(dims["blocks"], share, jnp.zeros((dims["window"], dims["rows"]), F32))
        wide = jnp.sum(shares, axis=1, keepdims=True)
        wide = jnp.broadcast_to(wide, (dims["window"], scale.shape[1]))
        scale[at, :] = jnp.where(row_mask(dims, first, offs, e), wide, scale[at, :])


def weigh(dims, offs, rows_of, probs, meta):
    small = dims["small"]
    picked = (dims["blocks"], dims["rows"], dims["total"]) if small else (1, ALIGN, 128)
    outs = (
        jax.ShapeDtypeStruct((dims["padded"], 128), F32),
        jax.ShapeDtypeStruct(picked, BF16),
    )
    table = pltpu.VMEM((3 * dims["experts"], dims["blocks"] * dims["rows"]), BF16)
    operands = (rows_of, probs)
    if small:
        operands += (meta,)
        outs += (jax.ShapeDtypeStruct((1,), jnp.int32),)
    return pl.pallas_call(
        functools.partial(weigh_small_kernel if small else weigh_large_kernel, dims),
        out_shape=outs,
        in_specs=[smem()] + [vmem()] * len(operands),
        out_specs=(vmem(), vmem(), smem())[: len(outs)],
        scratch_shapes=[table] if small else [],
        compiler_params=params(*outs, *held(*operands)),
        cost_estimate=cost(6e9, 8e6),
        name="weigh",
    )(offs, *operands)


def row_mask(dims, first, offs, e):
    at = lax.broadcasted_iota(jnp.int32, (dims["window"], 1), 0) + first
    begin = offs[0, e]
    return (at >= begin) & (at < begin + offs[1, e])


def batches(experts):
    return [range(b, min(b + 4, experts)) for b in range(0, experts, 4)]


def gate_up_kernel(dims, c, first_part, me_ref, *refs):
    experts, window, part, quarter = dims["experts"], dims["window"], dims["part"], dims["quarter"]
    if first_part:
        blocks, rows = dims["blocks"], dims["rows"]
        packed, refs = refs[:blocks], refs[blocks:]
        w_gate, w_up, rowid, probs, rowk, x, select, offs_out, meta, refs = *refs[:9], refs[9:]
        gx, uy, g2, u1, g0, u0, gate_w, up_w, gate, up, sems, table = refs
    else:
        offs, x, w_gate, w_up, gx, uy, g2, u1, g0, u0, gate_w, up_w, gate, up, sems = refs
    units = pl.ds(c * part, part)

    def copies(e):
        return (
            pltpu.make_async_copy(w_gate.at[e, units, :], gate_w.at[e], sems.at[0, e]),
            pltpu.make_async_copy(w_up.at[e, units, :], up_w.at[e], sems.at[1, e]),
        )

    for e in range(experts):
        for copy in copies(e):
            copy.start()
    if first_part:
        for j, block in enumerate(packed):
            at = me_ref[1] ^ j
            table[pl.ds(pl.multiple_of(at * rows, rows), rows), :] = block[:rows, :]
            meta[at] = block[rows:, :]
        start, count = route(
            dims, me_ref[1] * experts, lambda block: meta[block], rowid, probs, rowk
        )
        offs = offs_out
        fill_select(dims, rowid, publish(dims, offs, start, count), select, 0)
        for r in range(0, x.shape[0], dims["tile"]):
            size = min(dims["tile"], x.shape[0] - r)
            got = jnp.dot(select[r : r + size, :], table[...], preferred_element_type=F32)
            x[r : r + size, :] = got.astype(BF16)
    contract = (((1,), (1,)), ((), ()))
    for batch in batches(experts):
        for e in batch:
            for copy in copies(e):
                copy.wait()
        for e in batch:
            first = aligned(dims, offs[0, e])
            rows_in = x[pl.ds(first, window), :]
            keep = (lax.broadcasted_iota(jnp.int32, (ALIGN, 1), 0) + first) >= offs[0, e]
            edge, rest = pl.ds(first, ALIGN), pl.ds(first + ALIGN, window - ALIGN)
            for held, into in ((gate_w, gate), (up_w, up)):
                got = lax.dot_general(rows_in, held[e], contract, preferred_element_type=F32)
                into[edge, :] = jnp.where(keep, got[:ALIGN], into[edge, :])
                into[rest, :] = got[ALIGN:]
    me = me_ref[0]

    def piece(total, j):
        return total[pl.ds(pl.multiple_of((me ^ j) * quarter, ALIGN), quarter), :]

    gx[0] = piece(gate, 1).astype(BF16)
    gx[1] = piece(gate, 3).astype(BF16)
    uy[0] = piece(up, 2).astype(BF16)
    uy[1] = piece(up, 3).astype(BF16)
    g2[...] = piece(gate, 2)
    u1[...] = piece(up, 1)
    g0[...] = piece(gate, 0)
    u0[...] = piece(up, 0)


def gate_up(dims, c, me, sources, w_gate, w_up):
    experts, part, quarter, padded = dims["experts"], dims["part"], dims["quarter"], dims["padded"]
    width = w_gate.shape[2]
    half = jax.ShapeDtypeStruct((2, quarter, part), BF16)
    own = jax.ShapeDtypeStruct((quarter, part), F32)
    first_part = len(sources) > 2
    outs = (half, half, own, own, own, own)
    scratch = [
        pltpu.VMEM((experts, part, width), BF16),
        pltpu.VMEM((experts, part, width), BF16),
        pltpu.VMEM((padded, part), F32),
        pltpu.VMEM((padded, part), F32),
        pltpu.SemaphoreType.DMA((2, experts)),
    ]
    into = (vmem(),) * len(outs)
    if first_part:
        blocks, rows = dims["blocks"], dims["rows"]
        shapes, offs = route_shapes(dims)
        x = jax.ShapeDtypeStruct((padded, width), BF16)
        select = jax.ShapeDtypeStruct((padded, blocks * rows), BF16)
        meta = jax.ShapeDtypeStruct((blocks, META, width), BF16)
        outs = shapes + (x, select, offs, meta) + outs
        into = (vmem(),) * 5 + (smem(), vmem()) + into
        scratch.append(pltpu.VMEM((blocks * rows, width), BF16))
        specs = [vmem()] * blocks
    else:
        specs = [smem(), vmem()]
    return pl.pallas_call(
        functools.partial(gate_up_kernel, dims, c, first_part),
        out_shape=outs,
        in_specs=[smem()] + specs + [hbm(), hbm()],
        out_specs=into,
        scratch_shapes=scratch,
        compiler_params=params(*outs, *held(*sources), *[b for b in scratch if "dma" not in str(b)]),
        cost_estimate=cost(4 * padded * width * part, 4 * experts * part * width + 2 * padded * width),
        name="gate_up",
    )(me, *sources, w_gate, w_up)


def down_kernel(dims, places, me_ref, offs, w_down, scale, chosen, rowk, *refs):
    experts, window, part, quarter = dims["experts"], dims["window"], dims["part"], dims["quarter"]
    pieces, refs = refs[: len(places)], refs[len(places) :]
    if dims["small"]:
        stay, away, hidden, scaled = refs
    else:
        out, hidden, scaled = refs
    scaled[...] = jnp.zeros_like(scaled)
    for (c, j, skip), piece in zip(places, pieces):
        first = pl.multiple_of((me_ref[0] ^ j) * quarter + skip, ALIGN)
        hidden[pl.ds(first, piece.shape[0]), c * part : (c + 1) * part] = piece[...]
    for e in range(experts):
        first = aligned(dims, offs[0, e])
        at = pl.ds(first, window)
        got = jnp.dot(hidden[at, :], w_down[e], preferred_element_type=F32) * scale[at, 0:1]
        mask = row_mask(dims, first, offs, e)
        scaled[at, :] = jnp.where(mask, got, scaled[at, :].astype(F32)).astype(BF16)
    rows, total, width = dims["rows"], dims["total"], w_down.shape[2]
    blocks, many = dims["blocks"], min(4, dims["blocks"])
    if dims["small"]:
        for side, into in enumerate((stay, away)):
            for p in range(0, blocks // 2, many):
                at = [me_ref[1] ^ (2 * (p + i) + side) for i in range(many)]
                picked = jnp.concatenate([chosen[i] for i in at], axis=0)
                summed = jnp.dot(picked, scaled[:total, :], preferred_element_type=F32)
                into[p : p + many] = summed.astype(BF16).reshape(many, rows, width)
        return

    def combine(step, carry):
        picked = [choose(dims, rowk, step * many + i) for i in range(many)]
        summed = jnp.dot(
            jnp.concatenate(picked, axis=0), scaled[:total, :], preferred_element_type=F32
        )
        out[pl.ds(step * many, many)] = summed.astype(BF16).reshape(many, rows, width)
        return carry

    lax.fori_loop(0, blocks // many, combine, 0)


def down(dims, me, offs, w_down, scale, chosen, rowk, chunks):
    padded, width = dims["padded"], w_down.shape[2]
    places = [(c, j, skip) for c, chunk in enumerate(chunks) for j, skip, _ in chunk]
    pieces = [piece for chunk in chunks for _, _, piece in chunk]
    operands = [w_down, scale, chosen, rowk, *pieces]
    blocks, rows = dims["blocks"], dims["rows"]
    scratch = [
        pltpu.VMEM((padded, w_down.shape[1]), BF16),
        pltpu.VMEM((padded, width), BF16),
    ]
    if dims["small"]:
        outs = (jax.ShapeDtypeStruct((blocks // 2, rows, width), BF16),) * 2
    else:
        outs = (jax.ShapeDtypeStruct((blocks, rows, width), BF16),)
    return pl.pallas_call(
        functools.partial(down_kernel, dims, places),
        out_shape=outs,
        in_specs=[smem(), smem()] + [vmem()] * len(operands),
        out_specs=(vmem(),) * len(outs),
        scratch_shapes=scratch,
        compiler_params=params(*outs, *held(*operands), *scratch),
        cost_estimate=cost(2 * padded * width * (w_down.shape[1] + blocks * rows), 2 * w_down.size),
        name="down",
    )(me, offs, *operands)


def swap(value, axis, bit):
    count = lax.axis_size(axis)
    return lax.ppermute(value, axis, [(i, i ^ bit) for i in range(count)])


def reduce_chunk(came, kept):
    from_x, from_y = came
    g2, u1, g0, u0 = kept
    gate_rest = swap((g2 + from_x[1].astype(F32)).astype(BF16), "rep", 2)
    up_rest = swap((u1 + from_y[1].astype(F32)).astype(BF16), "rep", 1)
    gate = g0 + from_x[0].astype(F32) + gate_rest.astype(F32)
    up = u0 + from_y[0].astype(F32) + up_rest.astype(F32)
    return (jax.nn.silu(gate) * up).astype(BF16)


def spread_chunk(hidden):
    x, y = swap(hidden, "rep", 1), swap(hidden, "rep", 2)
    half = hidden.shape[0] // 2
    corner = [(3, 0, swap(x[:half], "rep", 2)), (3, half, swap(y[half:], "rep", 1))]
    return [(0, 0, hidden), (1, 0, x), (2, 0, y)] + corner


def gather_tokens(tokens):
    held = {0: tokens}
    bit = lax.axis_size("exp") // 2
    while bit:
        for known in list(held):
            held[known | bit] = swap(held[known], "exp", bit)
        bit //= 2
    return [held[j] for j in range(len(held))]


def sum_over_exp(stay, away):
    total = stay.astype(F32) + swap(away, "exp", 1).astype(F32)
    came = [
        swap(total[i].astype(BF16), "exp", 2 * i) for i in range(total.shape[0] - 1, 0, -1)
    ]
    return (total[0] + sum(part.astype(F32) for part in came)).astype(BF16)


def local(tokens, expert_ids, route_weights, w_gate, w_up, w_down):
    rows, top = expert_ids.shape
    width = tokens.shape[1]
    experts, units, _ = w_gate.shape
    blocks = lax.axis_size("exp")
    replicas = lax.axis_size("rep")
    cap = replicas * max(1, rows * top * 3 // (8 * EXPERTS))
    total = ceil_to(experts * blocks * cap, replicas * 128)
    window = ceil_to(blocks * cap, ALIGN) + ALIGN
    part = units // 2
    small = blocks * rows * total <= 4 * 2**20

    def sizes(total):
        return dict(
            blocks=blocks,
            rows=rows,
            top=top,
            experts=experts,
            window=window,
            total=total,
            quarter=total // replicas,
            padded=total + window,
            part=part,
            group=min(blocks, 8),
            tile=512,
            small=small,
        )

    full = sizes(total)
    me = jnp.stack([lax.axis_index("rep"), lax.axis_index("exp")]).astype(jnp.int32)
    packed = pack(full, tokens, expert_ids, route_weights)
    weights = (w_gate, w_up, w_down)
    if not small:
        gathered = lax.all_gather(packed, "exp", axis=0)
        return one_pass(full, me, gathered, *weights)[0]
    sources = gather_tokens(packed)
    usual = min(total, ceil_to(rows * top * 5 // 4, replicas * 64))
    mixed, peak = one_pass(sizes(usual), me, sources, *weights)
    if usual == total:
        return mixed
    return lax.cond(
        peak[0] > usual, lambda: one_pass(full, me, sources, *weights)[0], lambda: mixed
    )


def one_pass(dims, me, sources, w_gate, w_up, w_down):
    meta = None
    if not dims["small"]:
        rowid, probs, rowk, x, offs = dispatch(dims, me, sources)
        rows_of, sources = rowid, [offs, x]
    parts = []
    for c in range(w_gate.shape[1] // dims["part"]):
        parts.append(gate_up(dims, c, me, sources, w_gate, w_up))
        if len(sources) > 2:
            rowid, probs, rowk, x, rows_of, offs, meta = parts[0][:7]
            sources, parts[0] = [offs, x], parts[0][7:]

    came = []
    for c, (gx, uy, *kept) in enumerate(parts):
        came.append((swap(gx, "rep", 1), swap(uy, "rep", 2)))
        parts[c] = kept
    rows_of, _ = lax.optimization_barrier((rows_of, parts[-1]))
    scale, chosen, *peak = weigh(dims, offs, rows_of, probs, meta)
    chunks = []
    for c, kept in enumerate(parts):
        hidden = reduce_chunk(came[c], kept)
        if c == 0:
            hidden, scale, chosen = lax.optimization_barrier((hidden, scale, chosen))
        chunks.append(spread_chunk(hidden))
    mixed = down(dims, me, offs, w_down, scale, chosen, rowk, chunks)
    if dims["small"]:
        return sum_over_exp(*mixed), peak[0]
    return lax.psum_scatter(mixed[0], "exp", scatter_dimension=0, tiled=False), None


def solution(mesh):
    return jax.shard_map(
        local,
        mesh=mesh,
        in_specs=(
            P("exp", "rep"),
            P("exp", None),
            P("exp", None),
            P("exp", None, "rep"),
            P("exp", None, "rep"),
            P("exp", None, "rep"),
        ),
        out_specs=P("exp", "rep"),
        check_vma=False,
    )
```

```python
import functools
import math

import jax
import jax.numpy as jnp
from jax import lax
from jax.experimental import pallas as pl
from jax.experimental.pallas import tpu as pltpu
from jax.sharding import PartitionSpec as P

EXPERTS = 128
F32 = jnp.float32
BF16 = jnp.bfloat16
VMEM_LIMIT = 56 * 2**20
VMEM_SPARE = 10 * 2**20
ALIGN = 16
META = 16


def ceil_to(value, unit):
    return -(-value // unit) * unit


def vmem():
    return pl.BlockSpec(memory_space=pltpu.VMEM)


def smem():
    return pl.BlockSpec(memory_space=pltpu.SMEM)


def hbm():
    return pl.BlockSpec(memory_space=pltpu.HBM)


def params(*shapes):
    need = sum(math.prod(s.shape) * jnp.dtype(s.dtype).itemsize for s in shapes if hasattr(s, "dtype"))
    return pltpu.CompilerParams(vmem_limit_bytes=min(VMEM_LIMIT, need + need // 4 + VMEM_SPARE))


def held(*arrays):
    return [jax.ShapeDtypeStruct(a.shape, a.dtype) for a in arrays]


def cost(flops, moved):
    return pl.CostEstimate(flops=int(flops), bytes_accessed=int(moved), transcendentals=0)


def pack_kernel(dims, tokens, ids, weights, packed):
    rows, top = dims["rows"], dims["top"]
    chance = weights[...]
    chance = chance / jnp.sum(chance, axis=0, keepdims=True)
    high = chance.astype(BF16)
    rest = chance - high.astype(F32)
    middle = rest.astype(BF16)
    low = (rest - middle.astype(F32)).astype(BF16)
    packed[:rows, :] = tokens[...]
    packed[rows:, :] = jnp.zeros((META, packed.shape[1]), BF16)
    parts = (ids[...].astype(F32), high.astype(F32), middle.astype(F32), low.astype(F32))
    for i, part in enumerate(parts):
        block = jnp.concatenate([part, jnp.zeros((META - top, rows), F32)], axis=0)
        packed[rows:, i * rows : (i + 1) * rows] = block.astype(BF16)


def pack(dims, tokens, ids, weights):
    return pl.pallas_call(
        functools.partial(pack_kernel, dims),
        out_shape=jax.ShapeDtypeStruct((dims["rows"] + META, tokens.shape[1]), BF16),
        in_specs=[vmem()] * 3,
        out_specs=vmem(),
        compiler_params=params(),
        name="pack",
    )(tokens, ids.T, weights.T)


def loop(count, body, carry):
    if count > 8:
        return lax.fori_loop(0, count, body, carry)
    for i in range(count):
        carry = body(i, carry)
    return carry


def route(dims, base, meta_of, rowid, probs, rowk):
    blocks, rows, top, experts = dims["blocks"], dims["rows"], dims["top"], dims["experts"]
    expert_at = lax.broadcasted_iota(jnp.int32, (experts, rows), 0) + base
    upper = (
        lax.broadcasted_iota(jnp.int32, (rows, rows), 0)
        <= lax.broadcasted_iota(jnp.int32, (rows, rows), 1)
    ).astype(BF16)

    def chosen_ids(block):
        return meta_of(block)[:, :rows].astype(F32)[:top].astype(jnp.int32)

    def count(block, seen):
        held = meta_of(block).astype(F32)[:top]
        ids = held[:, :rows].astype(jnp.int32)
        chance = held[:, rows : 2 * rows] + held[:, 2 * rows : 3 * rows]
        chance = chance + held[:, 3 * rows : 4 * rows]
        member = jnp.zeros((experts, rows), F32)
        share = jnp.zeros((experts, rows), F32)
        for k in range(top):
            hit = ids[k : k + 1, :] == expert_at
            member = member + hit.astype(F32)
            share = share + jnp.where(hit, chance[k : k + 1, :], 0.0)
        upto = jnp.dot(member.astype(BF16), upper, preferred_element_type=F32)
        rowid[block] = jnp.where(member > 0, seen + upto - 1.0, -1e6).astype(jnp.int32)
        probs[block] = share
        return seen + upto[:, rows - 1 : rows]

    total = loop(blocks, count, jnp.zeros((experts, rows), F32))
    starts, before = [], jnp.zeros((1, rows), F32)
    for e in range(experts):
        starts.append(before)
        before = before + total[e : e + 1, :]
    start = jnp.concatenate(starts, axis=0) if experts > 1 else starts[0]
    start, total = start.astype(jnp.int32), total.astype(jnp.int32)

    def place(block, carry):
        ids = chosen_ids(block)
        at = rowid[block] + start
        rowid[block] = at
        found = []
        for k in range(top):
            hit = ids[k : k + 1, :] == expert_at
            found.append(jnp.max(jnp.where(hit, at, -1), axis=0, keepdims=True))
        rowk[block] = jnp.concatenate(found, axis=0)
        return carry

    loop(blocks, place, 0)
    return start, total


def window_hits(dims, rowid, block, e, start):
    at = lax.broadcasted_iota(jnp.int32, (dims["window"], dims["rows"]), 0) + start
    return rowid[block, e : e + 1, :] == at


def aligned(dims, value):
    return pl.multiple_of(jnp.minimum(value // ALIGN * ALIGN, dims["total"]), ALIGN)


def fill_select(dims, rowid, starts, select, step):
    rows = dims["rows"]
    select[...] = jnp.zeros_like(select)
    for e in range(dims["experts"]):
        first = aligned(dims, starts[e])
        at = pl.ds(first, dims["window"])
        for inner in range(dims["group"]):
            cols = slice(inner * rows, (inner + 1) * rows)
            hit = window_hits(dims, rowid, step * dims["group"] + inner, e, first)
            select[at, cols] = select[at, cols] + hit.astype(F32).astype(BF16)


def publish(dims, offs, start, total):
    starts = [start[e, 0] for e in range(dims["experts"])]
    for e in range(dims["experts"]):
        offs[0, e] = starts[e]
        offs[1, e] = total[e, 0]
    return starts


def fullest(dims, meta):
    blocks, rows, top, experts = dims["blocks"], dims["rows"], dims["top"], dims["experts"]
    ids = [meta[b][:, :rows].astype(F32)[:top].astype(jnp.int32) for b in range(blocks)]
    counts = []
    for group in range(blocks):
        mine = jnp.zeros((top, rows), F32)
        for block_ids in ids:
            inside = (block_ids >= group * experts) & (block_ids < (group + 1) * experts)
            mine = mine + inside.astype(F32)
        counts.append(jnp.sum(mine, axis=0, keepdims=True))
    return jnp.max(jnp.sum(jnp.concatenate(counts, axis=0), axis=1, keepdims=True)).astype(jnp.int32)


def dispatch_kernel(dims, me_ref, gathered, rowid, probs, rowk, x, offs, select, total):
    blocks, rows, group, tile = dims["blocks"], dims["rows"], dims["group"], dims["tile"]
    start, count = route(
        dims, me_ref[1] * dims["experts"], lambda block: gathered[block, rows:, :], rowid, probs, rowk
    )
    starts = publish(dims, offs, start, count)
    total[...] = jnp.zeros_like(total)

    def body(step, carry):
        fill_select(dims, rowid, starts, select, step)
        part = gathered[pl.ds(step * group, group), :rows, :].reshape(group * rows, x.shape[1])
        for r in range(0, x.shape[0], tile):
            size = min(tile, x.shape[0] - r)
            got = jnp.dot(select[r : r + size, :], part, preferred_element_type=F32)
            got = got + total[r : r + size, :]
            total[r : r + size, :] = got
            x[r : r + size, :] = got.astype(BF16)
        return carry

    lax.fori_loop(0, blocks // group, body, 0)


def route_shapes(dims):
    blocks, rows, top, experts = dims["blocks"], dims["rows"], dims["top"], dims["experts"]
    return (
        jax.ShapeDtypeStruct((blocks, experts, rows), jnp.int32),
        jax.ShapeDtypeStruct((blocks, experts, rows), F32),
        jax.ShapeDtypeStruct((blocks, top, rows), jnp.int32),
    ), jax.ShapeDtypeStruct((2, experts), jnp.int32)


def dispatch(dims, me, gathered):
    shapes, offs = route_shapes(dims)
    width, padded = gathered.shape[2], dims["padded"]
    return pl.pallas_call(
        functools.partial(dispatch_kernel, dims),
        out_shape=shapes + (jax.ShapeDtypeStruct((padded, width), BF16), offs),
        in_specs=[smem(), vmem()],
        out_specs=(vmem(),) * 4 + (smem(),),
        scratch_shapes=[
            pltpu.VMEM((padded, dims["group"] * dims["rows"]), BF16),
            pltpu.VMEM((padded, width), F32),
        ],
        compiler_params=pltpu.CompilerParams(vmem_limit_bytes=VMEM_LIMIT),
        name="dispatch",
    )(me, gathered)


def choose(dims, rowk, block):
    at = lax.broadcasted_iota(jnp.int32, (dims["rows"], dims["total"]), 1)
    rows_of = rowk[block].astype(F32).T.astype(jnp.int32)
    hit = rows_of[:, 0:1] == at
    for k in range(1, dims["top"]):
        hit = hit | (rows_of[:, k : k + 1] == at)
    return hit.astype(F32).astype(BF16)


def weigh_small_kernel(dims, offs, select, probs, meta, scale, chosen, peak, table):
    peak[0] = fullest(dims, meta)
    rows, experts, total, blocks = dims["rows"], dims["experts"], dims["total"], dims["blocks"]
    same = lax.broadcasted_iota(jnp.int32, (rows, rows), 0) == lax.broadcasted_iota(
        jnp.int32, (rows, rows), 1
    )
    eye = same.astype(F32).astype(BF16)
    contract = (((1,), (1,)), ((), ()))
    for b in range(blocks):
        cols = slice(b * rows, (b + 1) * rows)
        picked = lax.dot_general(eye, select[:total, cols], contract, preferred_element_type=F32)
        chosen[b] = picked.astype(BF16)
        exact = probs[b]
        high = exact.astype(BF16)
        rest = exact - high.astype(F32)
        middle = rest.astype(BF16)
        low = (rest - middle.astype(F32)).astype(BF16)
        table[:, cols] = jnp.concatenate([high, middle, low], axis=0)
    wide = lax.dot_general(select[...], table[...], contract, preferred_element_type=F32)
    scale[:, : 3 * experts] = wide
    lane = lax.broadcasted_iota(jnp.int32, (dims["window"], scale.shape[1]), 1)
    for e in range(experts):
        first = aligned(dims, offs[0, e])
        at = pl.ds(first, dims["window"])
        old = scale[at, :]
        mine = (lane == e) | (lane == e + experts) | (lane == e + 2 * experts)
        found = jnp.sum(jnp.where(mine, old, 0.0), axis=1, keepdims=True)
        mask = row_mask(dims, first, offs, e)
        scale[at, :] = jnp.where(mask, jnp.broadcast_to(found, old.shape), old)


def weigh_large_kernel(dims, offs, rowid, probs, scale, chosen):
    chosen[...] = jnp.zeros_like(chosen)
    scale[...] = jnp.zeros_like(scale)
    for e in range(dims["experts"]):
        first = aligned(dims, offs[0, e])
        at = pl.ds(first, dims["window"])

        def share(block, carry):
            hit = window_hits(dims, rowid, block, e, first)
            return carry + jnp.where(hit, probs[block, e : e + 1, :], 0.0)

        shares = loop(dims["blocks"], share, jnp.zeros((dims["window"], dims["rows"]), F32))
        wide = jnp.sum(shares, axis=1, keepdims=True)
        wide = jnp.broadcast_to(wide, (dims["window"], scale.shape[1]))
        scale[at, :] = jnp.where(row_mask(dims, first, offs, e), wide, scale[at, :])


def weigh(dims, offs, rows_of, probs, meta):
    small = dims["small"]
    picked = (dims["blocks"], dims["rows"], dims["total"]) if small else (1, ALIGN, 128)
    outs = (
        jax.ShapeDtypeStruct((dims["padded"], 128), F32),
        jax.ShapeDtypeStruct(picked, BF16),
    )
    table = pltpu.VMEM((3 * dims["experts"], dims["blocks"] * dims["rows"]), BF16)
    operands = (rows_of, probs)
    if small:
        operands += (meta,)
        outs += (jax.ShapeDtypeStruct((1,), jnp.int32),)
    return pl.pallas_call(
        functools.partial(weigh_small_kernel if small else weigh_large_kernel, dims),
        out_shape=outs,
        in_specs=[smem()] + [vmem()] * len(operands),
        out_specs=(vmem(), vmem(), smem())[: len(outs)],
        scratch_shapes=[table] if small else [],
        compiler_params=params(*outs, *held(*operands)),
        cost_estimate=cost(6e9, 8e6),
        name="weigh",
    )(offs, *operands)


def row_mask(dims, first, offs, e):
    at = lax.broadcasted_iota(jnp.int32, (dims["window"], 1), 0) + first
    begin = offs[0, e]
    return (at >= begin) & (at < begin + offs[1, e])


def batches(experts):
    return [range(b, min(b + 4, experts)) for b in range(0, experts, 4)]


def gate_up_kernel(dims, c, first_part, me_ref, *refs):
    experts, window, part, quarter = dims["experts"], dims["window"], dims["part"], dims["quarter"]
    if first_part:
        blocks, rows = dims["blocks"], dims["rows"]
        packed, refs = refs[:blocks], refs[blocks:]
        w_gate, w_up, rowid, probs, rowk, x, select, offs_out, meta, refs = *refs[:9], refs[9:]
        gx, uy, g2, u1, g0, u0, gate_w, up_w, gate, up, sems, table = refs
    else:
        offs, x, w_gate, w_up, gx, uy, g2, u1, g0, u0, gate_w, up_w, gate, up, sems = refs
    units = pl.ds(c * part, part)

    def copies(e):
        return (
            pltpu.make_async_copy(w_gate.at[e, units, :], gate_w.at[e], sems.at[0, e]),
            pltpu.make_async_copy(w_up.at[e, units, :], up_w.at[e], sems.at[1, e]),
        )

    for e in range(experts):
        for copy in copies(e):
            copy.start()
    if first_part:
        for j, block in enumerate(packed):
            at = me_ref[1] ^ j
            table[pl.ds(pl.multiple_of(at * rows, rows), rows), :] = block[:rows, :]
            meta[at] = block[rows:, :]
        start, count = route(
            dims, me_ref[1] * experts, lambda block: meta[block], rowid, probs, rowk
        )
        offs = offs_out
        fill_select(dims, rowid, publish(dims, offs, start, count), select, 0)
        for r in range(0, x.shape[0], dims["tile"]):
            size = min(dims["tile"], x.shape[0] - r)
            got = jnp.dot(select[r : r + size, :], table[...], preferred_element_type=F32)
            x[r : r + size, :] = got.astype(BF16)
    contract = (((1,), (1,)), ((), ()))
    for batch in batches(experts):
        for e in batch:
            for copy in copies(e):
                copy.wait()
        for e in batch:
            first = aligned(dims, offs[0, e])
            rows_in = x[pl.ds(first, window), :]
            keep = (lax.broadcasted_iota(jnp.int32, (ALIGN, 1), 0) + first) >= offs[0, e]
            edge, rest = pl.ds(first, ALIGN), pl.ds(first + ALIGN, window - ALIGN)
            for held, into in ((gate_w, gate), (up_w, up)):
                got = lax.dot_general(rows_in, held[e], contract, preferred_element_type=F32)
                into[edge, :] = jnp.where(keep, got[:ALIGN], into[edge, :])
                into[rest, :] = got[ALIGN:]
    me = me_ref[0]

    def piece(total, j):
        return total[pl.ds(pl.multiple_of((me ^ j) * quarter, ALIGN), quarter), :]

    gx[0] = piece(gate, 1).astype(BF16)
    gx[1] = piece(gate, 3).astype(BF16)
    uy[0] = piece(up, 2).astype(BF16)
    uy[1] = piece(up, 3).astype(BF16)
    g2[...] = piece(gate, 2)
    u1[...] = piece(up, 1)
    g0[...] = piece(gate, 0)
    u0[...] = piece(up, 0)


def gate_up(dims, c, me, sources, w_gate, w_up):
    experts, part, quarter, padded = dims["experts"], dims["part"], dims["quarter"], dims["padded"]
    width = w_gate.shape[2]
    half = jax.ShapeDtypeStruct((2, quarter, part), BF16)
    own = jax.ShapeDtypeStruct((quarter, part), F32)
    first_part = len(sources) > 2
    outs = (half, half, own, own, own, own)
    scratch = [
        pltpu.VMEM((experts, part, width), BF16),
        pltpu.VMEM((experts, part, width), BF16),
        pltpu.VMEM((padded, part), F32),
        pltpu.VMEM((padded, part), F32),
        pltpu.SemaphoreType.DMA((2, experts)),
    ]
    into = (vmem(),) * len(outs)
    if first_part:
        blocks, rows = dims["blocks"], dims["rows"]
        shapes, offs = route_shapes(dims)
        x = jax.ShapeDtypeStruct((padded, width), BF16)
        select = jax.ShapeDtypeStruct((padded, blocks * rows), BF16)
        meta = jax.ShapeDtypeStruct((blocks, META, width), BF16)
        outs = shapes + (x, select, offs, meta) + outs
        into = (vmem(),) * 5 + (smem(), vmem()) + into
        scratch.append(pltpu.VMEM((blocks * rows, width), BF16))
        specs = [vmem()] * blocks
    else:
        specs = [smem(), vmem()]
    return pl.pallas_call(
        functools.partial(gate_up_kernel, dims, c, first_part),
        out_shape=outs,
        in_specs=[smem()] + specs + [hbm(), hbm()],
        out_specs=into,
        scratch_shapes=scratch,
        compiler_params=params(*outs, *held(*sources), *[b for b in scratch if "dma" not in str(b)]),
        cost_estimate=cost(4 * padded * width * part, 4 * experts * part * width + 2 * padded * width),
        name="gate_up",
    )(me, *sources, w_gate, w_up)


def down_kernel(dims, places, me_ref, offs, w_down, scale, chosen, rowk, *refs):
    experts, window, part, quarter = dims["experts"], dims["window"], dims["part"], dims["quarter"]
    pieces, refs = refs[: len(places)], refs[len(places) :]
    if dims["small"]:
        stay, away, hidden, scaled = refs
    else:
        out, hidden, scaled = refs
    scaled[...] = jnp.zeros_like(scaled)
    for (c, j, skip), piece in zip(places, pieces):
        first = pl.multiple_of((me_ref[0] ^ j) * quarter + skip, ALIGN)
        hidden[pl.ds(first, piece.shape[0]), c * part : (c + 1) * part] = piece[...]
    for e in range(experts):
        first = aligned(dims, offs[0, e])
        at = pl.ds(first, window)
        got = jnp.dot(hidden[at, :], w_down[e], preferred_element_type=F32) * scale[at, 0:1]
        keep = (lax.broadcasted_iota(jnp.int32, (ALIGN, 1), 0) + first) >= offs[0, e]
        edge = pl.ds(first, ALIGN)
        old = scaled[edge, :].astype(F32)
        scaled[edge, :] = jnp.where(keep, got[:ALIGN], old).astype(BF16)
        scaled[pl.ds(first + ALIGN, window - ALIGN), :] = got[ALIGN:].astype(BF16)
    rows, total, width = dims["rows"], dims["total"], w_down.shape[2]
    blocks, many = dims["blocks"], min(4, dims["blocks"])
    if dims["small"]:
        for side, into in enumerate((stay, away)):
            for p in range(0, blocks // 2, many):
                at = [me_ref[1] ^ (2 * (p + i) + side) for i in range(many)]
                picked = jnp.concatenate([chosen[i] for i in at], axis=0)
                summed = jnp.dot(picked, scaled[:total, :], preferred_element_type=F32)
                into[p : p + many] = summed.astype(BF16).reshape(many, rows, width)
        return

    def combine(step, carry):
        picked = [choose(dims, rowk, step * many + i) for i in range(many)]
        summed = jnp.dot(
            jnp.concatenate(picked, axis=0), scaled[:total, :], preferred_element_type=F32
        )
        out[pl.ds(step * many, many)] = summed.astype(BF16).reshape(many, rows, width)
        return carry

    lax.fori_loop(0, blocks // many, combine, 0)


def down(dims, me, offs, w_down, scale, chosen, rowk, chunks):
    padded, width = dims["padded"], w_down.shape[2]
    places = [(c, j, skip) for c, chunk in enumerate(chunks) for j, skip, _ in chunk]
    pieces = [piece for chunk in chunks for _, _, piece in chunk]
    operands = [w_down, scale, chosen, rowk, *pieces]
    blocks, rows = dims["blocks"], dims["rows"]
    scratch = [
        pltpu.VMEM((padded, w_down.shape[1]), BF16),
        pltpu.VMEM((padded, width), BF16),
    ]
    if dims["small"]:
        outs = (jax.ShapeDtypeStruct((blocks // 2, rows, width), BF16),) * 2
    else:
        outs = (jax.ShapeDtypeStruct((blocks, rows, width), BF16),)
    return pl.pallas_call(
        functools.partial(down_kernel, dims, places),
        out_shape=outs,
        in_specs=[smem(), smem()] + [vmem()] * len(operands),
        out_specs=(vmem(),) * len(outs),
        scratch_shapes=scratch,
        compiler_params=params(*outs, *held(*operands), *scratch),
        cost_estimate=cost(2 * padded * width * (w_down.shape[1] + blocks * rows), 2 * w_down.size),
        name="down",
    )(me, offs, *operands)


def swap(value, axis, bit):
    count = lax.axis_size(axis)
    return lax.ppermute(value, axis, [(i, i ^ bit) for i in range(count)])


def reduce_chunk(came, kept):
    from_x, from_y = came
    g2, u1, g0, u0 = kept
    gate_rest = swap((g2 + from_x[1].astype(F32)).astype(BF16), "rep", 2)
    up_rest = swap((u1 + from_y[1].astype(F32)).astype(BF16), "rep", 1)
    gate = g0 + from_x[0].astype(F32) + gate_rest.astype(F32)
    up = u0 + from_y[0].astype(F32) + up_rest.astype(F32)
    return (jax.nn.silu(gate) * up).astype(BF16)


def spread_chunk(hidden):
    x, y = swap(hidden, "rep", 1), swap(hidden, "rep", 2)
    half = hidden.shape[0] // 2
    corner = [(3, 0, swap(x[:half], "rep", 2)), (3, half, swap(y[half:], "rep", 1))]
    return [(0, 0, hidden), (1, 0, x), (2, 0, y)] + corner


def gather_tokens(tokens):
    held = {0: tokens}
    bit = lax.axis_size("exp") // 2
    while bit:
        for known in list(held):
            held[known | bit] = swap(held[known], "exp", bit)
        bit //= 2
    return [held[j] for j in range(len(held))]


def sum_over_exp(stay, away):
    total = stay.astype(F32) + swap(away, "exp", 1).astype(F32)
    came = [
        swap(total[i].astype(BF16), "exp", 2 * i) for i in range(total.shape[0] - 1, 0, -1)
    ]
    return (total[0] + sum(part.astype(F32) for part in came)).astype(BF16)


def local(tokens, expert_ids, route_weights, w_gate, w_up, w_down):
    rows, top = expert_ids.shape
    width = tokens.shape[1]
    experts, units, _ = w_gate.shape
    blocks = lax.axis_size("exp")
    replicas = lax.axis_size("rep")
    cap = replicas * max(1, rows * top * 3 // (8 * EXPERTS))
    total = ceil_to(experts * blocks * cap, replicas * 128)
    window = ceil_to(blocks * cap, ALIGN) + ALIGN
    part = units // 2
    small = blocks * rows * total <= 4 * 2**20

    def sizes(total):
        return dict(
            blocks=blocks,
            rows=rows,
            top=top,
            experts=experts,
            window=window,
            total=total,
            quarter=total // replicas,
            padded=total + window,
            part=part,
            group=min(blocks, 8),
            tile=512,
            small=small,
        )

    full = sizes(total)
    me = jnp.stack([lax.axis_index("rep"), lax.axis_index("exp")]).astype(jnp.int32)
    packed = pack(full, tokens, expert_ids, route_weights)
    weights = (w_gate, w_up, w_down)
    if not small:
        gathered = lax.all_gather(packed, "exp", axis=0)
        return one_pass(full, me, gathered, *weights)[0]
    sources = gather_tokens(packed)
    usual = min(total, ceil_to(rows * top * 5 // 4, replicas * 64))
    mixed, peak = one_pass(sizes(usual), me, sources, *weights)
    if usual == total:
        return mixed
    return lax.cond(
        peak[0] > usual, lambda: one_pass(full, me, sources, *weights)[0], lambda: mixed
    )


def one_pass(dims, me, sources, w_gate, w_up, w_down):
    meta = None
    if not dims["small"]:
        rowid, probs, rowk, x, offs = dispatch(dims, me, sources)
        rows_of, sources = rowid, [offs, x]
    parts = []
    for c in range(w_gate.shape[1] // dims["part"]):
        parts.append(gate_up(dims, c, me, sources, w_gate, w_up))
        if len(sources) > 2:
            rowid, probs, rowk, x, rows_of, offs, meta = parts[0][:7]
            sources, parts[0] = [offs, x], parts[0][7:]

    came = []
    for c, (gx, uy, *kept) in enumerate(parts):
        came.append((swap(gx, "rep", 1), swap(uy, "rep", 2)))
        parts[c] = kept
    rows_of, came[0] = lax.optimization_barrier((rows_of, came[0]))
    scale, chosen, *peak = weigh(dims, offs, rows_of, probs, meta)
    chunks = []
    for c, kept in enumerate(parts):
        hidden = reduce_chunk(came[c], kept)
        if c == 0:
            hidden, scale, chosen = lax.optimization_barrier((hidden, scale, chosen))
        chunks.append(spread_chunk(hidden))
    mixed = down(dims, me, offs, w_down, scale, chosen, rowk, chunks)
    if dims["small"]:
        return sum_over_exp(*mixed), peak[0]
    return lax.psum_scatter(mixed[0], "exp", scatter_dimension=0, tiled=False), None


def solution(mesh):
    return jax.shard_map(
        local,
        mesh=mesh,
        in_specs=(
            P("exp", "rep"),
            P("exp", None),
            P("exp", None),
            P("exp", None, "rep"),
            P("exp", None, "rep"),
            P("exp", None, "rep"),
        ),
        out_specs=P("exp", "rep"),
        check_vma=False,
    )
```

```python
import functools
import math

import jax
import jax.numpy as jnp
from jax import lax
from jax.experimental import pallas as pl
from jax.experimental.pallas import tpu as pltpu
from jax.sharding import PartitionSpec as P

EXPERTS = 128
F32 = jnp.float32
BF16 = jnp.bfloat16
VMEM_LIMIT = 56 * 2**20
VMEM_SPARE = 10 * 2**20
ALIGN = 16
META = 16


def ceil_to(value, unit):
    return -(-value // unit) * unit


def vmem():
    return pl.BlockSpec(memory_space=pltpu.VMEM)


def smem():
    return pl.BlockSpec(memory_space=pltpu.SMEM)


def hbm():
    return pl.BlockSpec(memory_space=pltpu.HBM)


def params(*shapes):
    need = sum(math.prod(s.shape) * jnp.dtype(s.dtype).itemsize for s in shapes if hasattr(s, "dtype"))
    return pltpu.CompilerParams(vmem_limit_bytes=min(VMEM_LIMIT, need + need // 4 + VMEM_SPARE))


def held(*arrays):
    return [jax.ShapeDtypeStruct(a.shape, a.dtype) for a in arrays]


def cost(flops, moved):
    return pl.CostEstimate(flops=int(flops), bytes_accessed=int(moved), transcendentals=0)


def pack_kernel(dims, tokens, ids, weights, packed):
    rows, top = dims["rows"], dims["top"]
    chance = weights[...]
    chance = chance / jnp.sum(chance, axis=0, keepdims=True)
    high = chance.astype(BF16)
    rest = chance - high.astype(F32)
    middle = rest.astype(BF16)
    low = (rest - middle.astype(F32)).astype(BF16)
    packed[:rows, :] = tokens[...]
    packed[rows:, :] = jnp.zeros((META, packed.shape[1]), BF16)
    parts = (ids[...].astype(F32), high.astype(F32), middle.astype(F32), low.astype(F32))
    for i, part in enumerate(parts):
        block = jnp.concatenate([part, jnp.zeros((META - top, rows), F32)], axis=0)
        packed[rows:, i * rows : (i + 1) * rows] = block.astype(BF16)


def pack(dims, tokens, ids, weights):
    return pl.pallas_call(
        functools.partial(pack_kernel, dims),
        out_shape=jax.ShapeDtypeStruct((dims["rows"] + META, tokens.shape[1]), BF16),
        in_specs=[vmem()] * 3,
        out_specs=vmem(),
        compiler_params=params(),
        name="pack",
    )(tokens, ids.T, weights.T)


def loop(count, body, carry):
    if count > 8:
        return lax.fori_loop(0, count, body, carry)
    for i in range(count):
        carry = body(i, carry)
    return carry


def route(dims, base, meta_of, rowid, probs, rowk):
    blocks, rows, top, experts = dims["blocks"], dims["rows"], dims["top"], dims["experts"]
    expert_at = lax.broadcasted_iota(jnp.int32, (experts, rows), 0) + base
    upper = (
        lax.broadcasted_iota(jnp.int32, (rows, rows), 0)
        <= lax.broadcasted_iota(jnp.int32, (rows, rows), 1)
    ).astype(BF16)

    def chosen_ids(block):
        return meta_of(block)[:, :rows].astype(F32)[:top].astype(jnp.int32)

    def count(block, seen):
        held = meta_of(block).astype(F32)[:top]
        ids = held[:, :rows].astype(jnp.int32)
        chance = held[:, rows : 2 * rows] + held[:, 2 * rows : 3 * rows]
        chance = chance + held[:, 3 * rows : 4 * rows]
        member = jnp.zeros((experts, rows), F32)
        share = jnp.zeros((experts, rows), F32)
        for k in range(top):
            hit = ids[k : k + 1, :] == expert_at
            member = member + hit.astype(F32)
            share = share + jnp.where(hit, chance[k : k + 1, :], 0.0)
        upto = jnp.dot(member.astype(BF16), upper, preferred_element_type=F32)
        rowid[block] = jnp.where(member > 0, seen + upto - 1.0, -1e6).astype(jnp.int32)
        probs[block] = share
        return seen + upto[:, rows - 1 : rows]

    total = loop(blocks, count, jnp.zeros((experts, rows), F32))
    starts, before = [], jnp.zeros((1, rows), F32)
    for e in range(experts):
        starts.append(before)
        before = before + total[e : e + 1, :]
    start = jnp.concatenate(starts, axis=0) if experts > 1 else starts[0]
    start, total = start.astype(jnp.int32), total.astype(jnp.int32)

    def place(block, carry):
        ids = chosen_ids(block)
        at = rowid[block] + start
        rowid[block] = at
        found = []
        for k in range(top):
            hit = ids[k : k + 1, :] == expert_at
            found.append(jnp.max(jnp.where(hit, at, -1), axis=0, keepdims=True))
        rowk[block] = jnp.concatenate(found, axis=0)
        return carry

    loop(blocks, place, 0)
    return start, total


def window_hits(dims, rowid, block, e, start):
    at = lax.broadcasted_iota(jnp.int32, (dims["window"], dims["rows"]), 0) + start
    return rowid[block, e : e + 1, :] == at


def aligned(dims, value):
    return pl.multiple_of(jnp.minimum(value // ALIGN * ALIGN, dims["total"]), ALIGN)


def fill_select(dims, rowid, starts, select, step):
    rows = dims["rows"]
    select[...] = jnp.zeros_like(select)
    for e in range(dims["experts"]):
        first = aligned(dims, starts[e])
        at = pl.ds(first, dims["window"])
        for inner in range(dims["group"]):
            cols = slice(inner * rows, (inner + 1) * rows)
            hit = window_hits(dims, rowid, step * dims["group"] + inner, e, first)
            select[at, cols] = select[at, cols] + hit.astype(F32).astype(BF16)


def publish(dims, offs, start, total):
    starts = [start[e, 0] for e in range(dims["experts"])]
    for e in range(dims["experts"]):
        offs[0, e] = starts[e]
        offs[1, e] = total[e, 0]
    return starts


def fullest(dims, meta):
    blocks, rows, top, experts = dims["blocks"], dims["rows"], dims["top"], dims["experts"]
    ids = [meta[b][:, :rows].astype(F32)[:top].astype(jnp.int32) for b in range(blocks)]
    counts = []
    for group in range(blocks):
        mine = jnp.zeros((top, rows), F32)
        for block_ids in ids:
            inside = (block_ids >= group * experts) & (block_ids < (group + 1) * experts)
            mine = mine + inside.astype(F32)
        counts.append(jnp.sum(mine, axis=0, keepdims=True))
    return jnp.max(jnp.sum(jnp.concatenate(counts, axis=0), axis=1, keepdims=True)).astype(jnp.int32)


def dispatch_kernel(dims, me_ref, gathered, rowid, probs, rowk, x, offs, select, total):
    blocks, rows, group, tile = dims["blocks"], dims["rows"], dims["group"], dims["tile"]
    start, count = route(
        dims, me_ref[1] * dims["experts"], lambda block: gathered[block, rows:, :], rowid, probs, rowk
    )
    starts = publish(dims, offs, start, count)
    total[...] = jnp.zeros_like(total)

    def body(step, carry):
        fill_select(dims, rowid, starts, select, step)
        part = gathered[pl.ds(step * group, group), :rows, :].reshape(group * rows, x.shape[1])
        for r in range(0, x.shape[0], tile):
            size = min(tile, x.shape[0] - r)
            got = jnp.dot(select[r : r + size, :], part, preferred_element_type=F32)
            got = got + total[r : r + size, :]
            total[r : r + size, :] = got
            x[r : r + size, :] = got.astype(BF16)
        return carry

    lax.fori_loop(0, blocks // group, body, 0)


def route_shapes(dims):
    blocks, rows, top, experts = dims["blocks"], dims["rows"], dims["top"], dims["experts"]
    return (
        jax.ShapeDtypeStruct((blocks, experts, rows), jnp.int32),
        jax.ShapeDtypeStruct((blocks, experts, rows), F32),
        jax.ShapeDtypeStruct((blocks, top, rows), jnp.int32),
    ), jax.ShapeDtypeStruct((2, experts), jnp.int32)


def dispatch(dims, me, gathered):
    shapes, offs = route_shapes(dims)
    width, padded = gathered.shape[2], dims["padded"]
    return pl.pallas_call(
        functools.partial(dispatch_kernel, dims),
        out_shape=shapes + (jax.ShapeDtypeStruct((padded, width), BF16), offs),
        in_specs=[smem(), vmem()],
        out_specs=(vmem(),) * 4 + (smem(),),
        scratch_shapes=[
            pltpu.VMEM((padded, dims["group"] * dims["rows"]), BF16),
            pltpu.VMEM((padded, width), F32),
        ],
        compiler_params=pltpu.CompilerParams(vmem_limit_bytes=VMEM_LIMIT),
        name="dispatch",
    )(me, gathered)


def choose(dims, rowk, block):
    at = lax.broadcasted_iota(jnp.int32, (dims["rows"], dims["total"]), 1)
    rows_of = rowk[block].astype(F32).T.astype(jnp.int32)
    hit = rows_of[:, 0:1] == at
    for k in range(1, dims["top"]):
        hit = hit | (rows_of[:, k : k + 1] == at)
    return hit.astype(F32).astype(BF16)


def weigh_small_kernel(dims, offs, select, probs, meta, scale, chosen, peak, table):
    peak[0] = fullest(dims, meta)
    rows, experts, total, blocks = dims["rows"], dims["experts"], dims["total"], dims["blocks"]
    same = lax.broadcasted_iota(jnp.int32, (rows, rows), 0) == lax.broadcasted_iota(
        jnp.int32, (rows, rows), 1
    )
    eye = same.astype(F32).astype(BF16)
    contract = (((1,), (1,)), ((), ()))
    for b in range(blocks):
        cols = slice(b * rows, (b + 1) * rows)
        picked = lax.dot_general(eye, select[:total, cols], contract, preferred_element_type=F32)
        chosen[b] = picked.astype(BF16)
        exact = probs[b]
        high = exact.astype(BF16)
        rest = exact - high.astype(F32)
        middle = rest.astype(BF16)
        low = (rest - middle.astype(F32)).astype(BF16)
        table[:, cols] = jnp.concatenate([high, middle, low], axis=0)
    wide = lax.dot_general(select[...], table[...], contract, preferred_element_type=F32)
    scale[:, : 3 * experts] = wide
    lane = lax.broadcasted_iota(jnp.int32, (dims["window"], scale.shape[1]), 1)
    for e in range(experts):
        first = aligned(dims, offs[0, e])
        at = pl.ds(first, dims["window"])
        old = scale[at, :]
        mine = (lane == e) | (lane == e + experts) | (lane == e + 2 * experts)
        found = jnp.sum(jnp.where(mine, old, 0.0), axis=1, keepdims=True)
        mask = row_mask(dims, first, offs, e)
        scale[at, :] = jnp.where(mask, jnp.broadcast_to(found, old.shape), old)


def weigh_large_kernel(dims, offs, rowid, probs, scale, chosen):
    chosen[...] = jnp.zeros_like(chosen)
    scale[...] = jnp.zeros_like(scale)
    for e in range(dims["experts"]):
        first = aligned(dims, offs[0, e])
        at = pl.ds(first, dims["window"])

        def share(block, carry):
            hit = window_hits(dims, rowid, block, e, first)
            return carry + jnp.where(hit, probs[block, e : e + 1, :], 0.0)

        shares = loop(dims["blocks"], share, jnp.zeros((dims["window"], dims["rows"]), F32))
        wide = jnp.sum(shares, axis=1, keepdims=True)
        wide = jnp.broadcast_to(wide, (dims["window"], scale.shape[1]))
        scale[at, :] = jnp.where(row_mask(dims, first, offs, e), wide, scale[at, :])


def weigh(dims, offs, rows_of, probs, meta):
    small = dims["small"]
    picked = (dims["blocks"], dims["rows"], dims["total"]) if small else (1, ALIGN, 128)
    outs = (
        jax.ShapeDtypeStruct((dims["padded"], 128), F32),
        jax.ShapeDtypeStruct(picked, BF16),
    )
    table = pltpu.VMEM((3 * dims["experts"], dims["blocks"] * dims["rows"]), BF16)
    operands = (rows_of, probs)
    if small:
        operands += (meta,)
        outs += (jax.ShapeDtypeStruct((1,), jnp.int32),)
    return pl.pallas_call(
        functools.partial(weigh_small_kernel if small else weigh_large_kernel, dims),
        out_shape=outs,
        in_specs=[smem()] + [vmem()] * len(operands),
        out_specs=(vmem(), vmem(), smem())[: len(outs)],
        scratch_shapes=[table] if small else [],
        compiler_params=params(*outs, *held(*operands)),
        cost_estimate=cost(6e9, 8e6),
        name="weigh",
    )(offs, *operands)


def row_mask(dims, first, offs, e):
    at = lax.broadcasted_iota(jnp.int32, (dims["window"], 1), 0) + first
    begin = offs[0, e]
    return (at >= begin) & (at < begin + offs[1, e])


def batches(experts):
    return [range(b, min(b + 4, experts)) for b in range(0, experts, 4)]


def gate_up_kernel(dims, c, first_part, me_ref, *refs):
    experts, window, part, quarter = dims["experts"], dims["window"], dims["part"], dims["quarter"]
    if first_part:
        blocks, rows = dims["blocks"], dims["rows"]
        packed, refs = refs[:blocks], refs[blocks:]
        w_gate, w_up, rowid, probs, rowk, x, select, offs_out, meta, refs = *refs[:9], refs[9:]
        gx, uy, g2, u1, g0, u0, gate_w, up_w, gate, up, sems, table = refs
    else:
        offs, x, w_gate, w_up, gx, uy, g2, u1, g0, u0, gate_w, up_w, gate, up, sems = refs
    units = pl.ds(c * part, part)

    def copies(e):
        return (
            pltpu.make_async_copy(w_gate.at[e, units, :], gate_w.at[e], sems.at[0, e]),
            pltpu.make_async_copy(w_up.at[e, units, :], up_w.at[e], sems.at[1, e]),
        )

    for e in range(experts):
        for copy in copies(e):
            copy.start()
    if first_part:
        for j, block in enumerate(packed):
            at = me_ref[1] ^ j
            table[pl.ds(pl.multiple_of(at * rows, rows), rows), :] = block[:rows, :]
            meta[at] = block[rows:, :]
        start, count = route(
            dims, me_ref[1] * experts, lambda block: meta[block], rowid, probs, rowk
        )
        offs = offs_out
        fill_select(dims, rowid, publish(dims, offs, start, count), select, 0)
        for r in range(0, x.shape[0], dims["tile"]):
            size = min(dims["tile"], x.shape[0] - r)
            got = jnp.dot(select[r : r + size, :], table[...], preferred_element_type=F32)
            x[r : r + size, :] = got.astype(BF16)
    contract = (((1,), (1,)), ((), ()))
    for batch in batches(experts):
        for e in batch:
            for copy in copies(e):
                copy.wait()
        for e in batch:
            first = aligned(dims, offs[0, e])
            rows_in = x[pl.ds(first, window), :]
            keep = (lax.broadcasted_iota(jnp.int32, (ALIGN, 1), 0) + first) >= offs[0, e]
            edge, rest = pl.ds(first, ALIGN), pl.ds(first + ALIGN, window - ALIGN)
            for held, into in ((gate_w, gate), (up_w, up)):
                got = lax.dot_general(rows_in, held[e], contract, preferred_element_type=F32)
                into[edge, :] = jnp.where(keep, got[:ALIGN], into[edge, :])
                into[rest, :] = got[ALIGN:]
    me = me_ref[0]

    def piece(total, j):
        return total[pl.ds(pl.multiple_of((me ^ j) * quarter, ALIGN), quarter), :]

    gx[0] = piece(gate, 1).astype(BF16)
    gx[1] = piece(gate, 3).astype(BF16)
    uy[0] = piece(up, 2).astype(BF16)
    uy[1] = piece(up, 3).astype(BF16)
    g2[...] = piece(gate, 2)
    u1[...] = piece(up, 1)
    g0[...] = piece(gate, 0)
    u0[...] = piece(up, 0)


def gate_up(dims, c, me, sources, w_gate, w_up):
    experts, part, quarter, padded = dims["experts"], dims["part"], dims["quarter"], dims["padded"]
    width = w_gate.shape[2]
    half = jax.ShapeDtypeStruct((2, quarter, part), BF16)
    own = jax.ShapeDtypeStruct((quarter, part), F32)
    first_part = len(sources) > 2
    outs = (half, half, own, own, own, own)
    scratch = [
        pltpu.VMEM((experts, part, width), BF16),
        pltpu.VMEM((experts, part, width), BF16),
        pltpu.VMEM((padded, part), F32),
        pltpu.VMEM((padded, part), F32),
        pltpu.SemaphoreType.DMA((2, experts)),
    ]
    into = (vmem(),) * len(outs)
    if first_part:
        blocks, rows = dims["blocks"], dims["rows"]
        shapes, offs = route_shapes(dims)
        x = jax.ShapeDtypeStruct((padded, width), BF16)
        select = jax.ShapeDtypeStruct((padded, blocks * rows), BF16)
        meta = jax.ShapeDtypeStruct((blocks, META, width), BF16)
        outs = shapes + (x, select, offs, meta) + outs
        into = (vmem(),) * 5 + (smem(), vmem()) + into
        scratch.append(pltpu.VMEM((blocks * rows, width), BF16))
        specs = [vmem()] * blocks
    else:
        specs = [smem(), vmem()]
    return pl.pallas_call(
        functools.partial(gate_up_kernel, dims, c, first_part),
        out_shape=outs,
        in_specs=[smem()] + specs + [hbm(), hbm()],
        out_specs=into,
        scratch_shapes=scratch,
        compiler_params=params(*outs, *held(*sources), *[b for b in scratch if "dma" not in str(b)]),
        cost_estimate=cost(4 * padded * width * part, 4 * experts * part * width + 2 * padded * width),
        name="gate_up",
    )(me, *sources, w_gate, w_up)


def down_kernel(dims, places, me_ref, offs, w_down, scale, chosen, rowk, *refs):
    experts, window, part, quarter = dims["experts"], dims["window"], dims["part"], dims["quarter"]
    pieces, refs = refs[: len(places)], refs[len(places) :]
    if dims["small"]:
        stay, away, hidden, scaled = refs
    else:
        out, hidden, scaled = refs
    scaled[...] = jnp.zeros_like(scaled)
    for (c, j, skip), piece in zip(places, pieces):
        first = pl.multiple_of((me_ref[0] ^ j) * quarter + skip, ALIGN)
        hidden[pl.ds(first, piece.shape[0]), c * part : (c + 1) * part] = piece[...]
    for e in range(experts):
        first = aligned(dims, offs[0, e])
        at = pl.ds(first, window)
        got = jnp.dot(hidden[at, :], w_down[e], preferred_element_type=F32) * scale[at, 0:1]
        keep = (lax.broadcasted_iota(jnp.int32, (ALIGN, 1), 0) + first) >= offs[0, e]
        edge = pl.ds(first, ALIGN)
        old = scaled[edge, :].astype(F32)
        scaled[edge, :] = jnp.where(keep, got[:ALIGN], old).astype(BF16)
        scaled[pl.ds(first + ALIGN, window - ALIGN), :] = got[ALIGN:].astype(BF16)
    rows, total, width = dims["rows"], dims["total"], w_down.shape[2]
    blocks, many = dims["blocks"], min(4, dims["blocks"])
    if dims["small"]:
        for side, into in enumerate((stay, away)):
            for p in range(0, blocks // 2, many):
                at = [me_ref[1] ^ (2 * (p + i) + side) for i in range(many)]
                picked = jnp.concatenate([chosen[i] for i in at], axis=0)
                summed = jnp.dot(picked, scaled[:total, :], preferred_element_type=F32)
                into[p : p + many] = summed.astype(BF16).reshape(many, rows, width)
        return

    def combine(step, carry):
        picked = [choose(dims, rowk, step * many + i) for i in range(many)]
        summed = jnp.dot(
            jnp.concatenate(picked, axis=0), scaled[:total, :], preferred_element_type=F32
        )
        out[pl.ds(step * many, many)] = summed.astype(BF16).reshape(many, rows, width)
        return carry

    lax.fori_loop(0, blocks // many, combine, 0)


def down(dims, me, offs, w_down, scale, chosen, rowk, chunks):
    padded, width = dims["padded"], w_down.shape[2]
    places = [(c, j, skip) for c, chunk in enumerate(chunks) for j, skip, _ in chunk]
    pieces = [piece for chunk in chunks for _, _, piece in chunk]
    operands = [w_down, scale, chosen, rowk, *pieces]
    blocks, rows = dims["blocks"], dims["rows"]
    scratch = [
        pltpu.VMEM((padded, w_down.shape[1]), BF16),
        pltpu.VMEM((padded, width), BF16),
    ]
    if dims["small"]:
        outs = (jax.ShapeDtypeStruct((blocks // 2, rows, width), BF16),) * 2
    else:
        outs = (jax.ShapeDtypeStruct((blocks, rows, width), BF16),)
    return pl.pallas_call(
        functools.partial(down_kernel, dims, places),
        out_shape=outs,
        in_specs=[smem(), smem()] + [vmem()] * len(operands),
        out_specs=(vmem(),) * len(outs),
        scratch_shapes=scratch,
        compiler_params=params(*outs, *held(*operands), *scratch),
        cost_estimate=cost(2 * padded * width * (w_down.shape[1] + blocks * rows), 2 * w_down.size),
        name="down",
    )(me, offs, *operands)


def swap(value, axis, bit):
    count = lax.axis_size(axis)
    return lax.ppermute(value, axis, [(i, i ^ bit) for i in range(count)])


def reduce_chunk(came, kept):
    from_x, from_y = came
    g2, u1, g0, u0 = kept
    gate_rest = swap((g2 + from_x[1].astype(F32)).astype(BF16), "rep", 2)
    up_rest = swap((u1 + from_y[1].astype(F32)).astype(BF16), "rep", 1)
    gate = g0 + from_x[0].astype(F32) + gate_rest.astype(F32)
    up = u0 + from_y[0].astype(F32) + up_rest.astype(F32)
    return (jax.nn.silu(gate) * up).astype(BF16)


def spread_chunk(hidden):
    x, y = swap(hidden, "rep", 1), swap(hidden, "rep", 2)
    half = hidden.shape[0] // 2
    corner = [(3, 0, swap(x[:half], "rep", 2)), (3, half, swap(y[half:], "rep", 1))]
    return [(0, 0, hidden), (1, 0, x), (2, 0, y)] + corner


def gather_tokens(tokens):
    count = lax.axis_size("exp")
    blocks = {0: tokens}
    for j in range(count - 2, 0, -2):
        blocks[j] = swap(tokens, "exp", j)
    for j in range(0, count, 2):
        blocks[j + 1] = swap(blocks[j], "exp", 1)
    return [blocks[j] for j in range(count)]


def sum_over_exp(stay, away):
    total = stay.astype(F32) + swap(away, "exp", 1).astype(F32)
    came = [
        swap(total[i].astype(BF16), "exp", 2 * i) for i in range(total.shape[0] - 1, 0, -1)
    ]
    return (total[0] + sum(part.astype(F32) for part in came)).astype(BF16)


def local(tokens, expert_ids, route_weights, w_gate, w_up, w_down):
    rows, top = expert_ids.shape
    width = tokens.shape[1]
    experts, units, _ = w_gate.shape
    blocks = lax.axis_size("exp")
    replicas = lax.axis_size("rep")
    cap = replicas * max(1, rows * top * 3 // (8 * EXPERTS))
    total = ceil_to(experts * blocks * cap, replicas * 128)
    window = ceil_to(blocks * cap, ALIGN) + ALIGN
    part = units // 2
    small = blocks * rows * total <= 4 * 2**20

    def sizes(total):
        return dict(
            blocks=blocks,
            rows=rows,
            top=top,
            experts=experts,
            window=window,
            total=total,
            quarter=total // replicas,
            padded=total + window,
            part=part,
            group=min(blocks, 8),
            tile=512,
            small=small,
        )

    full = sizes(total)
    me = jnp.stack([lax.axis_index("rep"), lax.axis_index("exp")]).astype(jnp.int32)
    packed = pack(full, tokens, expert_ids, route_weights)
    weights = (w_gate, w_up, w_down)
    if not small:
        gathered = lax.all_gather(packed, "exp", axis=0)
        return one_pass(full, me, gathered, *weights)[0]
    sources = gather_tokens(packed)
    usual = min(total, ceil_to(rows * top * 5 // 4, replicas * 64))
    mixed, peak = one_pass(sizes(usual), me, sources, *weights)
    if usual == total:
        return mixed
    return lax.cond(
        peak[0] > usual, lambda: one_pass(full, me, sources, *weights)[0], lambda: mixed
    )


def one_pass(dims, me, sources, w_gate, w_up, w_down):
    meta = None
    if not dims["small"]:
        rowid, probs, rowk, x, offs = dispatch(dims, me, sources)
        rows_of, sources = rowid, [offs, x]
    parts = []
    for c in range(w_gate.shape[1] // dims["part"]):
        parts.append(gate_up(dims, c, me, sources, w_gate, w_up))
        if len(sources) > 2:
            rowid, probs, rowk, x, rows_of, offs, meta = parts[0][:7]
            sources, parts[0] = [offs, x], parts[0][7:]

    came = []
    for c, (gx, uy, *kept) in enumerate(parts):
        came.append((swap(gx, "rep", 1), swap(uy, "rep", 2)))
        parts[c] = kept
    rows_of, came[0] = lax.optimization_barrier((rows_of, came[0]))
    scale, chosen, *peak = weigh(dims, offs, rows_of, probs, meta)
    chunks = []
    for c, kept in enumerate(parts):
        hidden = reduce_chunk(came[c], kept)
        if c == 0:
            hidden, scale, chosen = lax.optimization_barrier((hidden, scale, chosen))
        chunks.append(spread_chunk(hidden))
    mixed = down(dims, me, offs, w_down, scale, chosen, rowk, chunks)
    if dims["small"]:
        return sum_over_exp(*mixed), peak[0]
    return lax.psum_scatter(mixed[0], "exp", scatter_dimension=0, tiled=False), None


def solution(mesh):
    return jax.shard_map(
        local,
        mesh=mesh,
        in_specs=(
            P("exp", "rep"),
            P("exp", None),
            P("exp", None),
            P("exp", None, "rep"),
            P("exp", None, "rep"),
            P("exp", None, "rep"),
        ),
        out_specs=P("exp", "rep"),
        check_vma=False,
    )
```
